32 devices in a mesh: dp: 8 (over y, x, core), tensor: 4 (over z).
Axes of the slice: x: 2, y: 2, z: 4, core: 2. Of those that a mesh axis runs over, the one named last changes fastest.
Arguments:
- tokens: bfloat16 [8192, 768], P('dp'), may hold values from -6 to 6
- type_table: float32 [2, 768], replicated, may hold values from -3 to 3
- norm_gain: float32 [2, 2, 768], replicated, may hold values from 0.5 to 1.5
- norm_bias: float32 [2, 2, 768], replicated, may hold values from -1.8 to 1.8
- w_qkv: bfloat16 [2, 768, 3, 768], P(None, None, None, 'tensor'), may hold values from -0.21875 to 0.21875
- w_out: bfloat16 [2, 768, 768], P(None, 'tensor'), may hold values from -0.625 to 0.625
- w_up: bfloat16 [2, 768, 3072], P(None, None, 'tensor'), may hold values from -0.21875 to 0.21875
- w_down: bfloat16 [2, 3072, 768], P(None, 'tensor'), may hold values from -0.109375 to 0.109375
- cotangent: bfloat16 [32, 12, 768], P('dp'), may hold values from -6 to 6
- positions: int32 [32, 12], P('dp'), may hold values from -1 to 39, as said below
Outputs:
- hidden_out: float32 [8192, 768], P('dp')
- grad_tokens: float32 [8192, 768], P('dp')
- grad_type: float32 [2, 768], P(None, 'dp')
- grad_gain: float32 [2, 2, 768], P(None, None, 'dp')
- grad_bias: float32 [2, 2, 768], P(None, None, 'dp')
- grad_qkv: float32 [2, 768, 3, 768], P(None, 'dp', None, 'tensor')
- grad_out: float32 [2, 768, 768], P(None, 'tensor', 'dp')
- grad_up: float32 [2, 768, 3072], P(None, 'dp', 'tensor')
- grad_down: float32 [2, 3072, 768], P(None, 'tensor', 'dp')
The draws below stay inside these ranges and needn't reach their ends.
Inputs may be any that keep to these rules, and one draw needn't show every extreme that they name: `positions`: each pair has between 1 and 12 masked words in its first slots, at distinct rows below 40; the slots after them hold -1; in every draw some pair has all 12 slots used.
All inputs are finite; a program needn't handle non-finite values.
Results may differ from the reference program's by a relative error of at most 0.03.
Values may be sent and summed in bfloat16 or wider, within the bound.
No kernel may reach another device: no remote copies, remote signals or barrier semaphores. Data moves between devices by JAX's collectives and lax.ppermute only.
A program may use at most 128 MiB of HBM per device.

```python
import math
import jax
import jax.numpy as jnp
from jax import lax

D = 768
HEADS = 12
HD = 64
FF = 3072
WORDS = 40
MASK_MAX = 12
LAYERS = 2
SEQ = 256
PAIRS = 32
TOKENS = 8192
N_TENSOR = 4


def draw_positions(key, part):
    key = jax.random.fold_in(key, 11)
    subkeys = jax.random.split(key, 5)
    orders = jax.vmap(lambda single: jax.random.permutation(single, WORDS))(jax.random.split(subkeys[0], PAIRS))
    first = jax.random.randint(subkeys[1], (PAIRS,), 0, MASK_MAX)
    second = jax.random.randint(subkeys[2], (PAIRS,), 0, MASK_MAX)
    third = jax.random.randint(subkeys[3], (PAIRS,), 0, MASK_MAX)
    counts = 1 + jnp.maximum(first, second * third // max(MASK_MAX - 1, 1))
    chosen = jax.random.randint(subkeys[4], (), 0, PAIRS)
    counts = jnp.where(jnp.arange(PAIRS) == chosen, MASK_MAX, counts)
    slots = jnp.arange(MASK_MAX)[None, :]
    return jnp.where(slots < counts[:, None], orders[:, :MASK_MAX], -1).astype(jnp.int32)


def strengthened(drawn, own_key, source, target, shards_of, factor):
    def block_of(dim):
        return (jnp.arange(drawn.shape[dim]) // (drawn.shape[dim] // shards_of)).reshape((-1,) + (1,) * (drawn.ndim - 1 - dim))

    one_side = jax.random.permutation(own_key, shards_of)[block_of(target)]
    other_side = (block_of(target) + shards_of // 2) % shards_of
    return jnp.where((block_of(source) == one_side) | (block_of(source) == other_side), factor * drawn, drawn)


def steps_of(own_key, dims, cuts, smallest, top_value):
    loudness = 1.0
    for dim, blocks in cuts:
        steps = jax.random.uniform(jax.random.fold_in(jax.random.fold_in(own_key, 6), dim), (blocks,), jnp.float32, smallest / len(cuts), top_value / len(cuts))
        loudness = loudness * jnp.repeat(jnp.exp(steps), dims[dim] // blocks).reshape((-1,) + (1,) * (len(dims) - 1 - dim))
    return loudness


def bell_draw(key, extent, width, limit, cuts=(), dtype=jnp.bfloat16):
    entries = width * jax.random.normal(key, extent, jnp.float32)
    if cuts:
        entries = entries * steps_of(key, extent, cuts, -0.22, 0.18)
    return jnp.clip(entries, -limit, limit).astype(dtype)


def bell_draw_with(key, dims, deviation, reach, shards, heavy, held_as=jnp.bfloat16):
    result = deviation * jax.random.normal(key, dims, jnp.float32)
    if shards:
        result = result * steps_of(key, dims, shards, -0.22, 0.18)
    return jnp.clip(strengthened(result, jax.random.fold_in(key, 3), *heavy), -reach, reach).astype(held_as)


def setup_inputs(seed: int = 0) -> dict:
    splits = jax.random.split(jax.random.key(seed), 11)
    return {
        "tokens": bell_draw_with(splits[0], (TOKENS, D), 1.0, 6.0, ((0, 8),), (0, 1, 8, 2.0)),
        "type_table": bell_draw(splits[1], (2, D), 0.5, 3.0, (), jnp.float32),
        "norm_gain": jnp.clip(1.0 + 0.1 * jax.random.normal(splits[2], (LAYERS, 2, D), jnp.float32), 0.5, 1.5),
        "norm_bias": bell_draw(splits[3], (LAYERS, 2, D), 0.3, 1.8, (), jnp.float32),
        "w_qkv": bell_draw(splits[4], (LAYERS, D, 3, D), D ** -0.5, 0.21875, ((3, 4),)),
        "w_out": bell_draw(splits[5], (LAYERS, D, D), (D // 8) ** -0.5, 0.625, ((1, 4),)),
        "w_up": bell_draw(splits[6], (LAYERS, D, FF), D ** -0.5, 0.21875, ((2, 4),)),
        "w_down": bell_draw(splits[7], (LAYERS, FF, D), FF ** -0.5, 0.109375, ((1, 4),)),
        "cotangent": bell_draw_with(splits[8], (PAIRS, MASK_MAX, D), 1.0, 6.0, ((0, 8),), (0, 2, 8, 2.0)),
        "positions": draw_positions(jax.random.fold_in(splits[10], 71), 0),
    }


@jax.custom_vjp
def low(v):
    return lax.optimization_barrier(v.astype(jnp.bfloat16)).astype(jnp.float32)

@jax.custom_vjp
def low_back(v):
    return v

def low_keep(v):
    return (low(v), None)

def low_pass(kept, grad):
    return (grad,)

def back_keep(v):
    return (v, None)

def back_low(kept, grad):
    return (low(grad),)
low.defvjp(low_keep, low_pass)
low_back.defvjp(back_keep, back_low)
EPSILON = 1e-06
EXACT = lax.Precision.HIGHEST
ROOT_HALF = 0.7071067811865476

def layer_norm(values, scale_row, shift_row):
    average = lax.optimization_barrier(jnp.mean(values, axis=-1, keepdims=True))
    centred = values - average
    spread = lax.optimization_barrier(jnp.mean(centred * centred, axis=-1, keepdims=True))
    return centred * lax.rsqrt(spread + EPSILON) * scale_row + shift_row

def gelu_exact(values):
    return 0.5 * values * (1.0 + lax.erf(values * ROOT_HALF))

def grouped(left, right):
    pair_count, length, inner_width = left.shape
    share = inner_width // N_TENSOR
    pieces = jnp.einsum('pstf,tfd->tpsd', left.reshape(pair_count, length, N_TENSOR, share), right.reshape(N_TENSOR, share, right.shape[1]), precision=EXACT)
    return low_back(lax.optimization_barrier(jnp.sum(low(pieces), axis=0)))

def encoder_layer(stream, scale_rows, shift_rows, qkv_weight, out_weight, up_weight, down_weight):
    pair_count, length, feature_width = stream.shape
    normed = low(layer_norm(stream, scale_rows[0], shift_rows[0]))
    projected = low(low_back(jnp.einsum('psd,dcf->cpsf', normed, qkv_weight, precision=EXACT)))
    heads_split = projected.reshape(3, pair_count, length, HEADS, HD)
    scores = low_back(jnp.einsum('pqhe,pkhe->phqk', heads_split[0], heads_split[1], precision=EXACT) * float(HD) ** (-0.5))
    row_max = lax.optimization_barrier(jnp.max(scores, axis=-1, keepdims=True))
    logsum = row_max + jnp.log(lax.optimization_barrier(jnp.sum(jnp.exp(scores - row_max), axis=-1, keepdims=True)))
    weights = low(jnp.exp(scores - logsum))
    mixed_heads = low(low_back(jnp.einsum('phqk,pkhe->pqhe', weights, heads_split[2], precision=EXACT)))
    middle = stream + grouped(mixed_heads.reshape(pair_count, length, feature_width), out_weight)
    normed_mlp = low(layer_norm(middle, scale_rows[1], shift_rows[1]))
    upward = low_back(jnp.einsum('psd,df->psf', normed_mlp, up_weight, precision=EXACT))
    active = low(gelu_exact(upward))
    return middle + grouped(active, down_weight)

def forward(tokens, type_table, norm_gain, norm_bias, w_qkv, w_out, w_up, w_down):
    length = tokens.shape[1]
    position_rows = lax.broadcasted_iota(jnp.int32, (length, 1), 0)
    stream = tokens + jnp.where(position_rows < WORDS, type_table[0], type_table[1])
    for layer_index in range(LAYERS):
        stream = encoder_layer(stream, norm_gain[layer_index], norm_bias[layer_index], w_qkv[layer_index], w_out[layer_index], w_up[layer_index], w_down[layer_index])
    return stream

def place_rows(cot_block, position_block):
    pair_count = cot_block.shape[0]
    pair_index = lax.broadcasted_iota(jnp.int32, position_block.shape, 0)
    target = jnp.where(position_block >= 0, position_block, SEQ).astype(jnp.int32)
    empty = jnp.zeros((pair_count, SEQ, D), jnp.float32)
    return empty.at[pair_index, target].add(cot_block, mode='drop')

def reference(tokens, type_table, norm_gain, norm_bias, w_qkv, w_out, w_up, w_down, cotangent, positions):
    parameters = (type_table.astype(jnp.float32), norm_gain.astype(jnp.float32), norm_bias.astype(jnp.float32), w_qkv.astype(jnp.float32), w_out.astype(jnp.float32), w_up.astype(jnp.float32), w_down.astype(jnp.float32))
    group_pairs = math.gcd(PAIRS, 16)
    groups = PAIRS // group_pairs
    token_groups = tokens.astype(jnp.float32).reshape(groups, group_pairs, SEQ, D)
    cot_groups = cotangent.astype(jnp.float32).reshape(groups, group_pairs, MASK_MAX, D)
    position_groups = positions.reshape(groups, group_pairs, MASK_MAX)

    def group_step(totals, group_items):
        token_block, cot_block, position_block = group_items
        incoming = place_rows(cot_block, position_block)
        output, pullback = jax.vjp(forward, token_block, *parameters)
        gradients = pullback(incoming)
        totals = tuple((running + update for running, update in zip(totals, gradients[1:])))
        return (totals, (output, gradients[0]))
    initial = tuple((jnp.zeros_like(parameter) for parameter in parameters))
    totals, (outputs, token_grads) = lax.scan(group_step, initial, (token_groups, cot_groups, position_groups))
    return (outputs.reshape(TOKENS, D), token_grads.reshape(TOKENS, D), totals[0], totals[1], totals[2], totals[3], totals[4], totals[5], totals[6])
```

```python
import jax
import jax.numpy as jnp
from jax import lax
from jax.sharding import PartitionSpec as P

HD = 64
WORDS = 40
EPSILON = 1e-06
ROOT_HALF = 0.7071067811865476
ROOT_TWO_PI = 2.5066282746310002
GROUP = 8
F32 = jnp.float32
BF16 = jnp.bfloat16


def dot(left, right, dims):
    return lax.dot_general(left, right, (dims, ((), ())), preferred_element_type=F32)


def nn(left, right):
    return dot(left, right, ((1,), (0,)))


def nt(left, right):
    return dot(left, right, ((1,), (1,)))


def tn(left, right):
    return dot(left, right, ((0,), (0,)))


def norm_parts(values):
    average = jnp.mean(values, axis=-1, keepdims=True)
    centred = values - average
    spread = jnp.mean(centred * centred, axis=-1, keepdims=True)
    rate = lax.rsqrt(spread + EPSILON)
    return centred * rate, rate


def norm_back(values, gain, incoming):
    unit, rate = norm_parts(values)
    scaled = incoming * gain
    inner = jnp.mean(scaled * unit, axis=-1, keepdims=True)
    grad = rate * (scaled - jnp.mean(scaled, axis=-1, keepdims=True) - unit * inner)
    return grad, jnp.sum(incoming * unit, axis=0), jnp.sum(incoming, axis=0)


def swap(values, bit, size):
    return lax.ppermute(values, "dp", [(i, i ^ bit) for i in range(size)])


def shift(values, size):
    return lax.ppermute(values, "tensor", [(i, (i + 1) % size) for i in range(size)])


def gather_blocks(part, place, n_dp, n_t):
    rows = part.shape[0]
    half = rows // 2
    quarters = []
    held = part
    for _ in range(n_t - 1):
        held = shift(held, n_t)
        along_x = swap(held, 2, n_dp)
        along_y = swap(held, 4, n_dp)
        corner_a = swap(along_x[:half], 4, n_dp)
        corner_b = swap(along_y[half:], 2, n_dp)
        plane = jnp.concatenate([held, along_x, along_y, corner_a, corner_b], 0)
        other = swap(plane, 1, n_dp)
        quarters.append(place(plane, other))
    return quarters


def reduce_blocks(keep, send, n_dp, n_t):
    half = keep.shape[2] // 2
    got = swap(send, 1, n_dp)

    def both(i, rows=slice(None)):
        return keep[i, :, rows].astype(F32) + got[i, :, rows].astype(F32)

    low, high = slice(0, half), slice(half, None)
    corner_a = swap(both(3, low).astype(BF16), 2, n_dp)
    corner_b = swap(both(3, high).astype(BF16), 4, n_dp)
    x_piece = jnp.concatenate([both(1, low), both(1, high) + corner_b.astype(F32)], 1)
    y_piece = jnp.concatenate([both(2, low) + corner_a.astype(F32), both(2, high)], 1)
    from_x = swap(x_piece.astype(BF16), 2, n_dp)
    from_y = swap(y_piece.astype(BF16), 4, n_dp)
    mine = both(0) + from_x.astype(F32) + from_y.astype(F32)
    total = mine[1]
    for k in range(2, n_t):
        total = shift(total.astype(BF16), n_t).astype(F32) + mine[k]
    total = shift(total.astype(BF16), n_t).astype(F32) + mine[0]
    rows = total.shape[0]
    bit = n_dp // 2
    while bit >= GROUP:
        rows //= 2
        total = total[:rows] + swap(total[rows:], bit, n_dp)
        bit //= 2
    return total


def sum_all(values, n_dp, n_t):
    bit = 1
    while bit < n_dp:
        values = values + swap(values, bit, n_dp)
        bit *= 2
    bit = 1
    while bit < n_t:
        values = values + lax.ppermute(
            values, "tensor", [(i, i ^ bit) for i in range(n_t)]
        )
        bit *= 2
    return values


def attention_forward(stream, gain, bias, blocks):
    heads = blocks[0].shape[1] // 4 // HD
    normed = (norm_parts(stream)[0] * gain + bias).astype(BF16)
    kept, logsums, mixes = [], [], []
    middle = stream
    for block in blocks:
        proj = nn(normed, block[:, : 3 * heads * HD]).astype(BF16)
        parts = proj.reshape(-1, 3, heads, HD)
        scores = jnp.einsum("qhe,khe->hqk", parts[:, 0], parts[:, 1], preferred_element_type=F32) * HD**-0.5
        top = jnp.max(scores, axis=-1, keepdims=True)
        logsum = top + jnp.log(jnp.sum(jnp.exp(scores - top), axis=-1, keepdims=True))
        weights = jnp.exp(scores - logsum).astype(BF16)
        mixed = jnp.einsum("hqk,khe->qhe", weights, parts[:, 2], preferred_element_type=F32)
        mixed = mixed.astype(BF16).reshape(-1, heads * HD)
        middle = middle + nt(mixed, block[:, 3 * heads * HD :]).astype(BF16).astype(F32)
        kept.append(proj)
        logsums.append(logsum)
        mixes.append(mixed)
    return middle, normed, kept, logsums, mixes


def gelu(values):
    return 0.5 * values * (1.0 + lax.erf(values * ROOT_HALF))


def gelu_slope(values):
    return 0.5 * (1.0 + lax.erf(values * ROOT_HALF)) + values * jnp.exp(-0.5 * values * values) / ROOT_TWO_PI


def mlp_forward(middle, gain, bias, ups, downs):
    normed = (norm_parts(middle)[0] * gain + bias).astype(BF16)
    upwards = []
    out = middle
    for up, down in zip(ups, downs):
        upward = nn(normed, up)
        out = out + nn(gelu(upward).astype(BF16), down).astype(BF16).astype(F32)
        upwards.append(upward)
    return out, normed, upwards


def mlp_backward(incoming, middle, gain, normed, upwards, ups, downs, cut):
    low = incoming.astype(BF16)
    grad_normed = 0.0
    down_blocks, up_blocks = [], []
    for up, down, upward in zip(ups, downs, upwards):
        active = gelu(upward).astype(BF16)
        grad_upward = (nt(low, down) * gelu_slope(upward)).astype(BF16)
        grad_normed = grad_normed + nt(grad_upward, up)
        down_blocks.append((low, active))
        up_blocks.append((normed, grad_upward))
    grad, gain_grad, bias_grad = norm_back(middle, gain, grad_normed)
    return incoming + grad, gain_grad, bias_grad, down_blocks, up_blocks


def attention_backward(grad_middle, stream, gain, normed, projs, logsums, mixes, blocks):
    heads = blocks[0].shape[1] // 4 // HD
    low = grad_middle.astype(BF16)
    grad_normed = 0.0
    pieces = []
    for block, proj, logsum, mixed in zip(blocks, projs, logsums, mixes):
        parts = proj.reshape(-1, 3, heads, HD)
        queries, keys, values = parts[:, 0], parts[:, 1], parts[:, 2]
        grad_mixed = nn(low, block[:, 3 * heads * HD :]).astype(BF16).reshape(-1, heads, HD)
        scores = jnp.einsum("qhe,khe->hqk", queries, keys, preferred_element_type=F32) * HD**-0.5
        weights = jnp.exp(scores - logsum)
        grad_values = jnp.einsum("hqk,qhe->khe", weights.astype(BF16), grad_mixed, preferred_element_type=F32)
        grad_weights = jnp.einsum("qhe,khe->hqk", grad_mixed, values, preferred_element_type=F32)
        inner = jnp.sum(weights * grad_weights, axis=-1, keepdims=True)
        grad_scores = (weights * (grad_weights - inner)).astype(BF16)
        grad_queries = jnp.einsum("hqk,khe->qhe", grad_scores, keys, preferred_element_type=F32) * HD**-0.5
        grad_keys = jnp.einsum("hqk,qhe->khe", grad_scores, queries, preferred_element_type=F32) * HD**-0.5
        grad_proj = jnp.stack([grad_queries, grad_keys, grad_values], 1).astype(BF16).reshape(proj.shape)
        grad_normed = grad_normed + nt(grad_proj, block[:, : 3 * heads * HD])
        pieces.append((normed, grad_proj, low, mixed))
    grad, gain_grad, bias_grad = norm_back(stream, gain, grad_normed)
    return grad_middle + grad, gain_grad, bias_grad, pieces


def shards(tokens, type_table, norm_gain, norm_bias, w_qkv, w_out, w_up, w_down, cotangent, positions, n_dp, n_t):
    total_rows, width = tokens.shape
    pair_count, slots = positions.shape
    assert pair_count == n_t
    length = total_rows // pair_count
    layers = w_qkv.shape[0]
    inner = w_qkv.shape[3]
    me, quarter = lax.axis_index("dp"), lax.axis_index("tensor")
    rows = width // GROUP
    spot = me % GROUP
    units = n_dp // GROUP
    unit = width // n_dp

    own = [
        jnp.concatenate([w_qkv[l].reshape(width, 3 * inner), w_out[l].T], 1)
        for l in range(layers)
    ]

    def part_of(block):
        return lax.dynamic_slice_in_dim(block, spot * rows, rows, 0)

    def in_place(pieces):
        block = jnp.zeros((GROUP, rows, width), BF16)
        for s, piece in enumerate(pieces):
            block = lax.dynamic_update_slice(block, piece[None], (spot ^ s, 0, 0))
        return block.reshape(width, width)

    def place_one(plane, other):
        a, b = plane.reshape(4, rows, width), other.reshape(4, rows, width)
        return in_place([v[i] for i in range(4) for v in (a, b)])

    def place_two(plane, other):
        up, down = [], []
        for v in (plane, other):
            four = v.reshape(4, 2, rows, width)
            up.append(four[:, 0])
            down.append(four[:, 1])
        return (
            in_place([v[i] for i in range(4) for v in up]),
            in_place([v[i] for i in range(4) for v in down]),
        )

    attn_blocks, ups, downs = [], [], []
    for l in range(layers):
        attn_blocks.append([own[l]] + gather_blocks(part_of(own[l]), place_one, n_dp, n_t))
        both = gather_blocks(
            jnp.concatenate([part_of(w_up[l]), part_of(w_down[l])], 0), place_two, n_dp, n_t
        )
        ups.append([w_up[l]] + [pair[0] for pair in both])
        downs.append([w_down[l]] + [pair[1] for pair in both])

    mine = lax.dynamic_slice_in_dim(tokens, quarter * length, length, 0).astype(F32)
    row_ids = lax.broadcasted_iota(jnp.int32, (length, 1), 0)
    stream = mine + jnp.where(row_ids < WORDS, type_table[0], type_table[1])
    saved = []
    for l in range(layers):
        middle, normed, projs, logsums, mixes = attention_forward(
            stream, norm_gain[l, 0], norm_bias[l, 0], attn_blocks[l]
        )
        following, normed_mlp, upwards = mlp_forward(
            middle, norm_gain[l, 1], norm_bias[l, 1], ups[l], downs[l]
        )
        saved.append((stream, normed, projs, logsums, mixes, middle, normed_mlp, upwards))
        stream = following

    def whole_pairs(values):
        held = values.astype(BF16)
        out = jnp.zeros((total_rows, width), F32)
        for k in range(n_t):
            out = lax.dynamic_update_slice(out, held.astype(F32), (((quarter - k) % n_t) * length, 0))
            if k < n_t - 1:
                held = shift(held, n_t)
        return out

    hidden_out = whole_pairs(stream)

    place = lax.dynamic_slice_in_dim(positions, quarter, 1, 0)[0]
    cot = lax.dynamic_slice_in_dim(cotangent, quarter, 1, 0)[0]
    onehot = (row_ids == place[None, :]).astype(BF16)
    incoming = nn(onehot, cot)

    def cut(left, right):
        flipped = left.T.reshape(n_dp, unit, left.shape[0])
        order = [
            lax.dynamic_slice_in_dim(flipped, me ^ (s + GROUP * h), 1, 0)
            for c in (0, 1)
            for s in range(c, GROUP, 2)
            for h in range(units)
        ]
        flipped = jnp.concatenate(order, 0).reshape(width, left.shape[0])
        return nn(flipped, right).astype(BF16).reshape(2, 4, rows, -1)

    def reduced(cuts):
        keep = jnp.stack([c[0] for c in cuts], 1)
        send = jnp.stack([c[1] for c in cuts], 1)
        return reduce_blocks(keep, send, n_dp, n_t)

    sums = {}
    gains = [[None, None] for _ in range(layers)]
    biases = [[None, None] for _ in range(layers)]
    for l in range(layers - 1, -1, -1):
        stream_l, normed, projs, logsums, mixes, middle, normed_mlp, upwards = saved[l]
        incoming, gains[l][1], biases[l][1], down_pairs, up_pairs = mlp_backward(
            incoming, middle, norm_gain[l, 1], normed_mlp, upwards, ups[l], downs[l], cut
        )
        sums["down", l] = reduced([cut(*p) for p in down_pairs])
        sums["up", l] = reduced([cut(*p) for p in up_pairs])
        incoming, gains[l][0], biases[l][0], pieces = attention_backward(
            incoming, stream_l, norm_gain[l, 0], normed, projs, logsums, mixes, attn_blocks[l]
        )
        sums["attn", l] = reduced(
            [jnp.concatenate([cut(n, g), cut(m, x)], -1) for n, g, m, x in pieces]
        )

    grad_tokens = whole_pairs(incoming)
    type_grad = jnp.stack([jnp.sum(incoming[:WORDS], 0), jnp.sum(incoming[WORDS:], 0)])
    rows_all = jnp.concatenate(
        [type_grad] + [jnp.stack(g) for g in gains] + [jnp.stack(b) for b in biases], 0
    )
    rows_all = sum_all(rows_all, n_dp, n_t)
    rows_mine = lax.dynamic_slice_in_dim(rows_all, me * unit, unit, 1)
    grad_gain = rows_mine[2 : 2 + 2 * layers].reshape(layers, 2, unit)
    grad_bias = rows_mine[2 + 2 * layers :].reshape(layers, 2, unit)
    grad_qkv = jnp.stack(
        [sums["attn", l][:, : 3 * inner].reshape(unit, 3, inner) for l in range(layers)]
    )
    grad_out = jnp.stack([sums["attn", l][:, 3 * inner :].T for l in range(layers)])
    grad_up = jnp.stack([sums["up", l] for l in range(layers)])
    grad_down = jnp.stack([sums["down", l].T for l in range(layers)])
    return hidden_out, grad_tokens, rows_mine[:2], grad_gain, grad_bias, grad_qkv, grad_out, grad_up, grad_down


def solution(mesh):
    n_dp, n_t = mesh.shape["dp"], mesh.shape["tensor"]
    placed = (
        P("dp", None),
        P(),
        P(),
        P(),
        P(None, None, None, "tensor"),
        P(None, "tensor", None),
        P(None, None, "tensor"),
        P(None, "tensor", None),
        P("dp", None, None),
        P("dp", None),
    )

    def run(*args):
        return shards(*args, n_dp, n_t)

    return jax.shard_map(
        run,
        mesh=mesh,
        in_specs=placed,
        out_specs=(
            P("dp", None),
            P("dp", None),
            P(None, "dp"),
            P(None, None, "dp"),
            P(None, None, "dp"),
            P(None, "dp", None, "tensor"),
            P(None, "tensor", "dp"),
            P(None, "dp", "tensor"),
            P(None, "tensor", "dp"),
        ),
        check_vma=False,
    )
```

```python
import functools

import jax
import jax.numpy as jnp
from jax import lax
from jax.experimental import pallas as pl
from jax.experimental.pallas import tpu as pltpu
from jax.sharding import PartitionSpec as P

HD = 64
WORDS = 40
TOP_ROWS = 48
SLOT_ROWS = 16
EPSILON = 1e-06
ROOT_HALF = 0.7071067811865476
ROOT_TWO_PI = 2.5066282746310002
GROUP = 8
STEP = 32
F32 = jnp.float32
BF16 = jnp.bfloat16
VMEM_BYTES = 48 * 1024 * 1024


def dot(left, right, dims):
    return lax.dot_general(left, right, (dims, ((), ())), preferred_element_type=F32)


def nn(left, right):
    return dot(left, right, ((1,), (0,)))


def nt(left, right):
    return dot(left, right, ((1,), (1,)))


def tn(left, right):
    return dot(left, right, ((0,), (0,)))


def gelu(values):
    return 0.5 * values * (1.0 + lax.erf(values * ROOT_HALF))


def gelu_slope(values):
    return 0.5 * (1.0 + lax.erf(values * ROOT_HALF)) + values * jnp.exp(-0.5 * values * values) / ROOT_TWO_PI


def norm_parts(values):
    average = jnp.mean(values, axis=-1, keepdims=True)
    centred = values - average
    spread = jnp.mean(centred * centred, axis=-1, keepdims=True)
    rate = lax.rsqrt(spread + EPSILON)
    return centred * rate, rate


def norm_rows(source, gain, bias, target):
    for r in range(0, source.shape[0], STEP):
        rows = slice(r, r + STEP)
        target[rows, :] = (norm_parts(source[rows, :])[0] * gain[...] + bias[...]).astype(BF16)


def norm_back_rows(rows, values, gain, incoming, gain_grad, bias_grad):
    unit, rate = norm_parts(values[rows, :])
    e = incoming[rows, :]
    scaled = e * gain[...]
    inner = jnp.mean(scaled * unit, axis=-1, keepdims=True)
    gain_grad[...] += jnp.sum(e * unit, axis=0, keepdims=True)
    bias_grad[...] += jnp.sum(e, axis=0, keepdims=True)
    return rate * (scaled - jnp.mean(scaled, axis=-1, keepdims=True) - unit * inner)


def fetch(spot, own, pieces, scratches, sems):
    count = len(scratches)
    rows = scratches[0].shape[1] // GROUP
    for source, scratch in zip(own, scratches):
        pltpu.make_async_copy(source, scratch.at[0], sems.at[0]).start()
    for k, pair in enumerate(pieces, 1):
        for c, source in enumerate(pair):
            for i in range(GROUP // 2):
                at = pl.multiple_of((spot ^ (2 * i + c)) * rows, rows)
                for m, scratch in enumerate(scratches):
                    pltpu.make_async_copy(
                        source.at[pl.ds((i * count + m) * rows, rows)],
                        scratch.at[k, pl.ds(at, rows)],
                        sems.at[k],
                    ).start()


def arrived(k, scratches, sems):
    for scratch in scratches:
        pltpu.make_async_copy(scratch.at[k], scratch.at[k], sems.at[k]).wait()


def flip(spot, source, target):
    width = source.shape[1]
    rows = width // GROUP
    turned = source.astype(F32).T.astype(BF16)
    for j in range(GROUP):
        s = spot ^ j
        at = pl.multiple_of(((s & 1) * (GROUP // 2) + (s >> 1)) * rows, rows)
        target[pl.ds(at, rows), :] = turned[j * rows : (j + 1) * rows, :]


def put_block(block, keep, send, columns=slice(None)):
    half = block.shape[0] // 2
    rows = half // (GROUP // 2)
    for i in range(GROUP // 2):
        keep[i, 0, :, columns] = block[i * rows : (i + 1) * rows].astype(BF16)
        send[i, 0, :, columns] = block[half + i * rows : half + (i + 1) * rows].astype(BF16)


def any_spec():
    return pl.BlockSpec(memory_space=pl.ANY)


def smem_spec():
    return pl.BlockSpec(memory_space=pltpu.SMEM)


def whole(shape):
    return pl.BlockSpec(shape, lambda k: (0,) * len(shape))


def per_quarter(shape):
    return pl.BlockSpec((1,) + shape, lambda k: (k,) + (0,) * len(shape))


def block_specs(rows, width):
    return [pl.BlockSpec((GROUP // 2, 1, rows, width), lambda k: (0, k, 0, 0))] * 2


def params():
    return pltpu.CompilerParams(vmem_limit_bytes=VMEM_BYTES, dimension_semantics=("arbitrary",))


def cost(flops, moved):
    return pl.CostEstimate(flops=flops, bytes_accessed=moved, transcendentals=0)


def attention_forward_kernel(spot_ref, x, gain, bias, own, *rest):
    n = len(rest) - 5 - 2
    pieces = [(rest[2 * i], rest[2 * i + 1]) for i in range(n // 2)]
    middle, normed, proj, logsum, mixed, block, sems = rest[n:]
    k = pl.program_id(0)
    inner = mixed.shape[-1]
    heads = inner // HD

    @pl.when(k == 0)
    def _():
        fetch(spot_ref[0], [own], pieces, [block], sems)
        norm_rows(x, gain, bias, normed)
        middle[...] = x[...]
        logsum[...] = jnp.zeros_like(logsum)

    arrived(k, [block], sems)
    proj[0] = nn(normed[...], block[k, :, : 3 * inner]).astype(BF16)
    lane = lax.broadcasted_iota(jnp.int32, logsum.shape, 1)
    for h in range(heads):
        own_lanes = slice(h * HD, (h + 1) * HD)
        queries = proj[0, :, own_lanes] * jnp.asarray(HD**-0.5, BF16)
        keys = proj[0, :, inner + h * HD : inner + (h + 1) * HD]
        values = proj[0, :, 2 * inner + h * HD : 2 * inner + (h + 1) * HD]
        scores = nt(queries, keys)
        top = jnp.max(scores, axis=-1, keepdims=True)
        powers = jnp.exp(scores - top)
        total = jnp.sum(powers, axis=-1, keepdims=True)
        logsum[...] = jnp.where(lane == k * heads + h, top + jnp.log(total), logsum[...])
        weights = (powers * (1.0 / total)).astype(BF16)
        mixed[0, :, own_lanes] = nn(weights, values).astype(BF16)
    middle[...] += nt(mixed[0], block[k, :, 3 * inner :]).astype(BF16).astype(F32)


def attention_forward(spot, x, gain, bias, own, pieces):
    length, width = x.shape
    n_t = len(pieces) + 1
    inner = own.shape[1] // 4
    flat = [v for pair in pieces for v in pair]
    out = [
        jax.ShapeDtypeStruct((length, width), F32),
        jax.ShapeDtypeStruct((length, width), BF16),
        jax.ShapeDtypeStruct((n_t, length, 3 * inner), BF16),
        jax.ShapeDtypeStruct((length, 128), F32),
        jax.ShapeDtypeStruct((n_t, length, inner), BF16),
    ]
    return pl.pallas_call(
        attention_forward_kernel,
        grid=(n_t,),
        out_shape=out,
        in_specs=[smem_spec(), whole((length, width)), whole((1, width)), whole((1, width))] + [any_spec()] * (1 + len(flat)),
        out_specs=[
            whole((length, width)),
            whole((length, width)),
            per_quarter((length, 3 * inner)),
            whole((length, 128)),
            per_quarter((length, inner)),
        ],
        scratch_shapes=[pltpu.VMEM((n_t,) + own.shape, BF16), pltpu.SemaphoreType.DMA((n_t,))],
        compiler_params=params(),
        cost_estimate=cost(4_000_000_000, 10_000_000),
        name="attention_forward",
    )(spot, x, gain, bias, own, *flat)


def mlp_forward_kernel(kept_rows, top, spot_ref, x, gain, bias, own_up, own_down, *rest):
    n = len(rest) - 3 - 4
    pieces = [(rest[2 * i], rest[2 * i + 1]) for i in range(n // 2)]
    out, normed, upward, ups, downs, total, sems = rest[n:]
    k = pl.program_id(0)

    @pl.when(k == 0)
    def _():
        fetch(spot_ref[0], [own_up, own_down], pieces, [ups, downs], sems)
        norm_rows(x, gain, bias, normed)
        total[...] = x[...]

    arrived(k, [ups, downs], sems)
    up = nn(normed[...], ups[k])
    upward[0] = up[:kept_rows]
    active = gelu(up).astype(BF16)
    total[...] += nn(active, downs[k]).astype(BF16).astype(F32)

    @pl.when(k == pl.num_programs(0) - 1)
    def _():
        out[...] = total[...].astype(out.dtype)


def mlp_forward(spot, x, gain, bias, own_up, own_down, pieces, kept_rows, top):
    length, width = x.shape
    n_t = len(pieces) + 1
    hidden = own_up.shape[1]
    flat = [v for pair in pieces for v in pair]
    out_type = BF16 if top else F32
    out = [
        jax.ShapeDtypeStruct((length, width), out_type),
        jax.ShapeDtypeStruct((length, width), BF16),
        jax.ShapeDtypeStruct((n_t, kept_rows, hidden), F32),
    ]
    return pl.pallas_call(
        functools.partial(mlp_forward_kernel, kept_rows, top),
        grid=(n_t,),
        out_shape=out,
        in_specs=[smem_spec(), whole((length, width)), whole((1, width)), whole((1, width))] + [any_spec()] * (2 + len(flat)),
        out_specs=[whole((length, width)), whole((length, width)), per_quarter((kept_rows, hidden))],
        scratch_shapes=[
            pltpu.VMEM((n_t,) + own_up.shape, BF16),
            pltpu.VMEM((n_t,) + own_down.shape, BF16),
            pltpu.VMEM((length, width), F32),
            pltpu.SemaphoreType.DMA((n_t,)),
        ],
        compiler_params=params(),
        cost_estimate=cost(4_000_000_000, 10_000_000),
        name="mlp_forward",
    )(spot, x, gain, bias, own_up, own_down, *flat)


def mlp_backward_kernel(blocks, spot_ref, incoming, x, gain, normed, upward, own_up, own_down, *rest):
    outs = 3 + (4 if blocks else 0)
    scr = 6 if blocks else 4
    n = len(rest) - outs - scr
    pieces = [(rest[2 * i], rest[2 * i + 1]) for i in range(n // 2)]
    grad, gain_grad, bias_grad = rest[n : n + 3]
    ups, downs, total, sems = rest[n + outs : n + outs + 4]
    k = pl.program_id(0)

    @pl.when(k == 0)
    def _():
        fetch(spot_ref[0], [own_up, own_down], pieces, [ups, downs], sems)
        total[...] = jnp.zeros_like(total)
        if blocks:
            low_t, normed_t = rest[-2:]
            flip(spot_ref[0], incoming[...], low_t)
            flip(spot_ref[0], normed[...], normed_t)

    arrived(k, [ups, downs], sems)
    up = upward[0]
    grad_active = nt(incoming[...].astype(BF16), downs[k])
    bell = 0.5 * (1.0 + lax.erf(up * ROOT_HALF))
    grad_up = (grad_active * (bell + up * jnp.exp(-0.5 * up * up) * (1.0 / ROOT_TWO_PI))).astype(BF16)
    total[...] += nt(grad_up, ups[k])
    if blocks:
        down_keep, down_send, up_keep, up_send = rest[n + 3 : n + 7]
        put_block(nn(low_t_of(rest)[...], (up * bell).astype(BF16)), down_keep, down_send)
        put_block(nn(rest[-1][...], grad_up), up_keep, up_send)

    @pl.when(k == pl.num_programs(0) - 1)
    def _():
        gain_grad[...] = jnp.zeros_like(gain_grad)
        bias_grad[...] = jnp.zeros_like(bias_grad)
        size = min(STEP, 16) if x.shape[0] % STEP else STEP
        for r in range(0, x.shape[0], size):
            rows = slice(r, r + size)
            grad[rows, :] = incoming[rows, :] + norm_back_rows(rows, x, gain, total, gain_grad, bias_grad)


def low_t_of(rest):
    return rest[-2]


def mlp_backward(spot, incoming, x, gain, normed, upward, own_up, own_down, pieces, blocks):
    length, width = incoming.shape
    n_t = len(pieces) + 1
    hidden = own_up.shape[1]
    flat = [v for pair in pieces for v in pair]
    out = [
        jax.ShapeDtypeStruct((length, width), F32),
        jax.ShapeDtypeStruct((1, width), F32),
        jax.ShapeDtypeStruct((1, width), F32),
    ]
    out_specs = [whole((length, width)), whole((1, width)), whole((1, width))]
    scratch = [
        pltpu.VMEM((n_t,) + own_up.shape, BF16),
        pltpu.VMEM((n_t,) + own_down.shape, BF16),
        pltpu.VMEM((length, width), F32),
        pltpu.SemaphoreType.DMA((n_t,)),
    ]
    if blocks:
        out += [jax.ShapeDtypeStruct((GROUP // 2, n_t, width // GROUP, hidden), BF16)] * 4
        out_specs += block_specs(width // GROUP, hidden) * 2
        scratch += [pltpu.VMEM((width, length), BF16)] * 2
    return pl.pallas_call(
        functools.partial(mlp_backward_kernel, blocks),
        grid=(n_t,),
        out_shape=out,
        in_specs=[
            smem_spec(),
            whole((length, width)),
            whole((length, width)),
            whole((1, width)),
            whole((length, width)),
            per_quarter((length, hidden)),
        ]
        + [any_spec()] * (2 + len(flat)),
        out_specs=out_specs,
        scratch_shapes=scratch,
        compiler_params=params(),
        cost_estimate=cost(6_000_000_000, 20_000_000),
        name="mlp_backward",
    )(spot, incoming, x, gain, normed, upward, own_up, own_down, *flat)


def attention_backward_kernel(spot_ref, incoming, x, gain, normed, proj, logsum, mixed, own, *rest):
    n = len(rest) - 5 - 6
    pieces = [(rest[2 * i], rest[2 * i + 1]) for i in range(n // 2)]
    grad, gain_grad, bias_grad, keep, send, block, total, grad_proj, sems, low_t, normed_t = rest[n:]
    k = pl.program_id(0)
    top = incoming.shape[0]
    inner = mixed.shape[-1]
    heads = inner // HD

    @pl.when(k == 0)
    def _():
        fetch(spot_ref[0], [own], pieces, [block], sems)
        total[...] = jnp.zeros_like(total)
        grad_proj[...] = jnp.zeros_like(grad_proj)
        flip(spot_ref[0], incoming[...], low_t)
        flip(spot_ref[0], normed[...], normed_t)

    arrived(k, [block], sems)
    grad_mixed = nn(incoming[...].astype(BF16), block[k, :, 3 * inner :]).astype(BF16)
    lane = lax.broadcasted_iota(jnp.int32, (top, 128), 1)
    for h in range(heads):
        own_lanes = slice(h * HD, (h + 1) * HD)
        key_lanes = slice(inner + h * HD, inner + (h + 1) * HD)
        value_lanes = slice(2 * inner + h * HD, 2 * inner + (h + 1) * HD)
        queries = proj[0, :top, own_lanes] * jnp.asarray(HD**-0.5, BF16)
        keys = proj[0, :, key_lanes]
        values = proj[0, :, value_lanes]
        head_grad = grad_mixed[:, own_lanes]
        row_sum = jnp.sum(jnp.where(lane == k * heads + h, logsum[:top, :], 0.0), axis=-1, keepdims=True)
        weights = jnp.exp(nt(queries, keys) - row_sum)
        grad_weights = nt(head_grad, values)
        inner_sum = jnp.sum(weights * grad_weights, axis=-1, keepdims=True)
        grad_scores = (weights * (grad_weights - inner_sum)).astype(BF16)
        grad_proj[:top, own_lanes] = (nn(grad_scores, keys) * HD**-0.5).astype(BF16)
        grad_proj[:, key_lanes] = tn(grad_scores, queries).astype(BF16)
        grad_proj[:, value_lanes] = tn(weights.astype(BF16), head_grad).astype(BF16)
    total[...] += nt(grad_proj[...], block[k, :, : 3 * inner])
    put_block(nn(normed_t[...], grad_proj[...]), keep, send, slice(0, 3 * inner))
    put_block(nn(low_t[...], mixed[0, :top, :]), keep, send, slice(3 * inner, 4 * inner))

    @pl.when(k == pl.num_programs(0) - 1)
    def _():
        gain_grad[...] = jnp.zeros_like(gain_grad)
        bias_grad[...] = jnp.zeros_like(bias_grad)
        for r in range(0, x.shape[0], 16):
            rows = slice(r, r + 16)
            back = norm_back_rows(rows, x, gain, total, gain_grad, bias_grad)
            grad[rows, :] = back + incoming[rows, :] if r < top else back


def attention_backward(spot, incoming, x, gain, normed, proj, logsum, mixed, own, pieces):
    length, width = x.shape
    top = incoming.shape[0]
    n_t = len(pieces) + 1
    inner = own.shape[1] // 4
    flat = [v for pair in pieces for v in pair]
    out = [
        jax.ShapeDtypeStruct((length, width), F32),
        jax.ShapeDtypeStruct((1, width), F32),
        jax.ShapeDtypeStruct((1, width), F32),
    ] + [jax.ShapeDtypeStruct((GROUP // 2, n_t, width // GROUP, 4 * inner), BF16)] * 2
    return pl.pallas_call(
        attention_backward_kernel,
        grid=(n_t,),
        out_shape=out,
        in_specs=[
            smem_spec(),
            whole((top, width)),
            whole((length, width)),
            whole((1, width)),
            whole((length, width)),
            per_quarter((length, 3 * inner)),
            whole((length, 128)),
            per_quarter((length, inner)),
        ]
        + [any_spec()] * (1 + len(flat)),
        out_specs=[whole((length, width)), whole((1, width)), whole((1, width))] + block_specs(width // GROUP, 4 * inner),
        scratch_shapes=[
            pltpu.VMEM((n_t,) + own.shape, BF16),
            pltpu.VMEM((length, width), F32),
            pltpu.VMEM((length, 3 * inner), BF16),
            pltpu.SemaphoreType.DMA((n_t,)),
            pltpu.VMEM((width, top), BF16),
            pltpu.VMEM((width, length), BF16),
        ],
        compiler_params=params(),
        cost_estimate=cost(6_000_000_000, 20_000_000),
        name="attention_backward",
    )(spot, incoming, x, gain, normed, proj, logsum, mixed, own, *flat)


def swap(values, bit, size):
    return lax.ppermute(values, "dp", [(i, i ^ bit) for i in range(size)])


def shift(values, size):
    return lax.ppermute(values, "tensor", [(i, (i + 1) % size) for i in range(size)])


def pack_kernel(*refs):
    *sources, target, sems = refs
    at = 0
    copies = []
    for i, source in enumerate(sources):
        rows = source.shape[0]
        copies.append(pltpu.make_async_copy(source, target.at[pl.ds(at, rows)], sems.at[i]))
        at += rows
    for copy in copies:
        copy.start()
    for copy in copies:
        copy.wait()


def pack(sources):
    rows = sum(s.shape[0] for s in sources)
    width = sources[0].shape[1]
    return pl.pallas_call(
        pack_kernel,
        out_shape=jax.ShapeDtypeStruct((rows, width), BF16),
        in_specs=[any_spec()] * len(sources),
        out_specs=any_spec(),
        scratch_shapes=[pltpu.SemaphoreType.DMA((len(sources),))],
        cost_estimate=cost(0, 4 * rows * width),
        name="pack",
    )(*sources)


def gather_blocks(part, n_dp, n_t):
    half = part.shape[0] // 2
    quarters = []
    held = part
    for _ in range(n_t - 1):
        held = shift(held, n_t)
        along_x = swap(held, 2, n_dp)
        along_y = swap(held, 4, n_dp)
        corner_a = swap(along_x[:half], 4, n_dp)
        corner_b = swap(along_y[half:], 2, n_dp)
        plane = pack([held, along_x, along_y, corner_a, corner_b])
        quarters.append((plane, swap(plane, 1, n_dp)))
    return quarters


def reduce_blocks(keep, send, n_dp, n_t):
    half = n_t // 2
    got = swap(send, 1, n_dp)

    def both(i, k=slice(None)):
        return keep[i, k].astype(F32) + got[i, k].astype(F32)

    low, high = slice(0, half), slice(half, None)
    corner_a = swap(both(3, low).astype(BF16), 2, n_dp)
    corner_b = swap(both(3, high).astype(BF16), 4, n_dp)
    x_low = swap(both(1, low).astype(BF16), 2, n_dp)
    x_high = swap((both(1, high) + corner_b.astype(F32)).astype(BF16), 2, n_dp)
    y_low = swap((both(2, low) + corner_a.astype(F32)).astype(BF16), 4, n_dp)
    y_high = swap(both(2, high).astype(BF16), 4, n_dp)

    def mine(k):
        x, y = (x_low, y_low) if k < half else (x_high, y_high)
        return both(0, k) + x[k % half].astype(F32) + y[k % half].astype(F32)

    total = mine(1)
    for k in range(2, n_t):
        total = shift(total.astype(BF16), n_t).astype(F32) + mine(k)
    total = shift(total.astype(BF16), n_t).astype(F32) + mine(0)
    groups = n_dp // GROUP
    me = lax.axis_index("dp")
    rows = total.shape[0]
    bit = n_dp // 2
    while bit >= GROUP:
        rows //= 2
        mine_first = (me // bit) % 2
        kept = lax.dynamic_slice_in_dim(total, mine_first * rows, rows, 0)
        sent = lax.dynamic_slice_in_dim(total, (1 - mine_first) * rows, rows, 0)
        total = kept + swap(sent, bit, n_dp)
        bit //= 2
    if groups > 1:
        total = lax.ppermute(
            total, "dp", [(h * GROUP + s, s * groups + h) for h in range(groups) for s in range(GROUP)]
        )
    return total


def sum_all(values, n_dp, n_t):
    bit = 1
    while bit < n_dp:
        values = values + swap(values, bit, n_dp)
        bit *= 2
    bit = 1
    while bit < n_t:
        values = values + lax.ppermute(values, "tensor", [(i, i ^ bit) for i in range(n_t)])
        bit *= 2
    return values


def gather_rows(values, n_dp, n_t):
    held = [values[None]]
    for _ in range(n_t - 1):
        held.append(shift(held[-1], n_t))
    out = jnp.concatenate(held, 0)
    bit = 2
    while bit < n_dp:
        out = jnp.concatenate([out, swap(out, bit, n_dp)], 0)
        bit *= 2
    return jnp.concatenate([out, swap(out, 1, n_dp)], 0)


def shards(tokens, type_table, norm_gain, norm_bias, w_qkv, w_out, w_up, w_down, cotangent, positions, n_dp, n_t):
    total_rows, width = tokens.shape
    pair_count, slots = positions.shape
    assert pair_count == n_t
    length = total_rows // pair_count
    layers = w_qkv.shape[0]
    top = layers - 1
    inner = w_qkv.shape[3]
    me, quarter = lax.axis_index("dp"), lax.axis_index("tensor")
    rows = width // GROUP
    unit = width // n_dp
    spot = me % GROUP
    spots = jnp.reshape(spot, (1,)).astype(jnp.int32)

    def part_of(block):
        return lax.dynamic_slice_in_dim(block, spot * rows, rows, 0)

    own, attn_pieces, mlp_pieces = [], [], []
    for l in range(layers):
        own.append(jnp.concatenate([w_qkv[l].reshape(width, 3 * inner), w_out[l].T], 1))
        attn_pieces.append(gather_blocks(part_of(own[l]), n_dp, n_t))
        mlp_pieces.append(
            gather_blocks(jnp.concatenate([part_of(w_up[l]), part_of(w_down[l])], 0), n_dp, n_t)
        )

    mine = lax.dynamic_slice_in_dim(tokens, quarter * length, length, 0).astype(F32)
    row_ids = lax.broadcasted_iota(jnp.int32, (length, 1), 0)
    stream = mine + jnp.where(row_ids < WORDS, type_table[0], type_table[1])
    gains = [[norm_gain[l, i][None] for i in range(2)] for l in range(layers)]
    biases = [[norm_bias[l, i][None] for i in range(2)] for l in range(layers)]
    saved = []
    for l in range(layers):
        middle, normed, proj, logsum, mixed = attention_forward(
            spots, stream, gains[l][0], biases[l][0], own[l], attn_pieces[l]
        )
        following, normed_mlp, upward = mlp_forward(
            spots, middle, gains[l][1], biases[l][1], w_up[l], w_down[l], mlp_pieces[l],
            TOP_ROWS if l == top else length, l == top,
        )
        saved.append((stream, normed, proj, logsum, mixed, middle, normed_mlp, upward))
        stream = following

    def whole_pairs(values):
        held = values.astype(BF16)
        out = jnp.zeros((total_rows, width), F32)
        for k in range(n_t):
            out = lax.dynamic_update_slice(out, held.astype(F32), (((quarter - k) % n_t) * length, 0))
            if k < n_t - 1:
                held = shift(held, n_t)
        return out

    hidden_out = whole_pairs(stream)

    place = lax.dynamic_slice_in_dim(positions, quarter, 1, 0)[0]
    cot = lax.dynamic_slice_in_dim(cotangent, quarter, 1, 0)[0]
    onehot = (row_ids[:TOP_ROWS] == place[None, :]).astype(BF16)
    incoming = nn(onehot, cot)

    top_normed = saved[top][6][:TOP_ROWS]
    slot_rows = tn(onehot, top_normed).astype(BF16)
    slot_cot = jnp.where(place[:, None] >= 0, cot, 0)
    spare = jnp.zeros((SLOT_ROWS - slots, width), BF16)
    all_rows = gather_rows(jnp.concatenate([slot_cot, spare, slot_rows, spare], 0), n_dp, n_t)
    all_cot = all_rows[:, :SLOT_ROWS].reshape(-1, width)
    all_normed = all_rows[:, SLOT_ROWS:].reshape(-1, width)
    slot_up = nn(all_normed, w_up[top])
    slot_grad = (nt(all_cot, w_down[top]) * gelu_slope(slot_up)).astype(BF16)
    grad_up_top = tn(lax.dynamic_slice_in_dim(all_normed, me * unit, unit, 1), slot_grad)
    grad_down_top = tn(
        gelu(slot_up).astype(BF16), lax.dynamic_slice_in_dim(all_cot, me * unit, unit, 1)
    )

    sums = {}
    gain_grads = [[None, None] for _ in range(layers)]
    bias_grads = [[None, None] for _ in range(layers)]
    for l in range(top, -1, -1):
        stream_l, normed, proj, logsum, mixed, middle, normed_mlp, upward = saved[l]
        part = slice(0, incoming.shape[0])
        incoming, gain_grads[l][1], bias_grads[l][1], *blocks = mlp_backward(
            spots, incoming, middle[part], gains[l][1], normed_mlp[part], upward,
            w_up[l], w_down[l], mlp_pieces[l], l < top,
        )
        if l < top:
            sums["down", l] = reduce_blocks(blocks[0], blocks[1], n_dp, n_t)
            sums["up", l] = reduce_blocks(blocks[2], blocks[3], n_dp, n_t)
        incoming, gain_grads[l][0], bias_grads[l][0], keep, send = attention_backward(
            spots, incoming, stream_l, gains[l][0], normed, proj, logsum, mixed, own[l], attn_pieces[l]
        )
        sums["attn", l] = reduce_blocks(keep, send, n_dp, n_t)

    grad_tokens = whole_pairs(incoming)
    type_grad = jnp.stack([jnp.sum(incoming[:WORDS], 0), jnp.sum(incoming[WORDS:], 0)])
    rows_all = jnp.concatenate(
        [type_grad] + [g for pair in gain_grads for g in pair] + [b for pair in bias_grads for b in pair], 0
    )
    rows_all = sum_all(rows_all, n_dp, n_t)
    rows_mine = lax.dynamic_slice_in_dim(rows_all, me * unit, unit, 1)
    grad_gain = rows_mine[2 : 2 + 2 * layers].reshape(layers, 2, unit)
    grad_bias = rows_mine[2 + 2 * layers :].reshape(layers, 2, unit)
    grad_qkv = jnp.stack([sums["attn", l][:, : 3 * inner].reshape(unit, 3, inner) for l in range(layers)])
    grad_out = jnp.stack([sums["attn", l][:, 3 * inner :].T for l in range(layers)])
    grad_up = jnp.stack([grad_up_top if l == top else sums["up", l] for l in range(layers)])
    grad_down = jnp.stack([grad_down_top if l == top else sums["down", l].T for l in range(layers)])
    return hidden_out, grad_tokens, rows_mine[:2], grad_gain, grad_bias, grad_qkv, grad_out, grad_up, grad_down


def solution(mesh):
    n_dp, n_t = mesh.shape["dp"], mesh.shape["tensor"]
    placed = (
        P("dp", None),
        P(),
        P(),
        P(),
        P(None, None, None, "tensor"),
        P(None, "tensor", None),
        P(None, None, "tensor"),
        P(None, "tensor", None),
        P("dp", None, None),
        P("dp", None),
    )

    def run(*args):
        return shards(*args, n_dp, n_t)

    return jax.shard_map(
        run,
        mesh=mesh,
        in_specs=placed,
        out_specs=(
            P("dp", None),
            P("dp", None),
            P(None, "dp"),
            P(None, None, "dp"),
            P(None, None, "dp"),
            P(None, "dp", None, "tensor"),
            P(None, "tensor", "dp"),
            P(None, "dp", "tensor"),
            P(None, "tensor", "dp"),
        ),
        check_vma=False,
    )
```

```python
import functools

import jax
import jax.numpy as jnp
from jax import lax
from jax.experimental import pallas as pl
from jax.experimental.pallas import tpu as pltpu
from jax.sharding import PartitionSpec as P

HD = 64
WORDS = 40
TOP_ROWS = 48
SLOT_ROWS = 16
EPSILON = 1e-06
ROOT_HALF = 0.7071067811865476
ROOT_TWO_PI = 2.5066282746310002
GROUP = 8
STEP = 32
F32 = jnp.float32
BF16 = jnp.bfloat16
SMALL_VMEM = 16 * 1024 * 1024
VMEM_BYTES = 60 * 1024 * 1024


def dot(left, right, dims):
    return lax.dot_general(left, right, (dims, ((), ())), preferred_element_type=F32)


def nn(left, right):
    return dot(left, right, ((1,), (0,)))


def nt(left, right):
    return dot(left, right, ((1,), (1,)))


def tn(left, right):
    return dot(left, right, ((0,), (0,)))


def gelu(values):
    return 0.5 * values * (1.0 + lax.erf(values * ROOT_HALF))


def gelu_slope(values):
    return 0.5 * (1.0 + lax.erf(values * ROOT_HALF)) + values * jnp.exp(-0.5 * values * values) / ROOT_TWO_PI


def norm_parts(values):
    average = jnp.mean(values, axis=-1, keepdims=True)
    centred = values - average
    spread = jnp.mean(centred * centred, axis=-1, keepdims=True)
    rate = lax.rsqrt(spread + EPSILON)
    return centred * rate, rate


def norm_rows(source, gain, bias, target):
    for r in range(0, source.shape[0], STEP):
        rows = slice(r, r + STEP)
        target[rows, :] = (norm_parts(source[rows, :])[0] * gain[...] + bias[...]).astype(BF16)


def norm_back_rows(rows, values, gain, incoming, gain_grad, bias_grad):
    unit, rate = norm_parts(values[rows, :])
    e = incoming[rows, :]
    scaled = e * gain[...]
    inner = jnp.mean(scaled * unit, axis=-1, keepdims=True)
    gain_grad[...] += jnp.sum(e * unit, axis=0, keepdims=True)
    bias_grad[...] += jnp.sum(e, axis=0, keepdims=True)
    return rate * (scaled - jnp.mean(scaled, axis=-1, keepdims=True) - unit * inner)


KERNEL_COST = pl.CostEstimate(flops=40_000_000_000, bytes_accessed=1_000_000, transcendentals=0)
SMALL_COST = pl.CostEstimate(flops=1_000_000_000, bytes_accessed=1_000_000, transcendentals=0)


class Pieces:
    def __init__(self, at):
        self.arrays = []
        self.plan = []
        for matrix in at:
            for k, slices in enumerate(matrix, 1):
                for s, (array, lead, row) in enumerate(slices):
                    found = [i for i, v in enumerate(self.arrays) if v is array]
                    if not found:
                        self.arrays.append(array)
                        found = [len(self.arrays) - 1]
                    self.plan.append((len(self.plan) // (len(matrix) * GROUP), k, s, found[0], lead, row))


def fetch(spot, own, plan, sources, scratches, sems, quarters):
    rows = scratches[0].shape[1] // GROUP
    for k in quarters:
        for m, scratch in enumerate(scratches):
            if k == 0:
                pltpu.make_async_copy(own[m], scratch.at[0], sems.at[0]).start()
        for m, at_k, s, which, lead, row in plan:
            if at_k == k:
                source = sources[which] if lead is None else sources[which].at[lead]
                at = pl.multiple_of((spot ^ s) * rows, rows)
                pltpu.make_async_copy(
                    source.at[pl.ds(row, rows)],
                    scratches[m].at[k - quarters[0], pl.ds(at, rows)],
                    sems.at[k - quarters[0]],
                ).start()


def arrived(k, scratches, sems):
    for scratch in scratches:
        pltpu.make_async_copy(scratch.at[k], scratch.at[k], sems.at[k]).wait()


def flip(spot, source, target):
    width = source.shape[1]
    rows = width // GROUP
    turned = source.astype(F32).T.astype(BF16)
    for j in range(GROUP):
        s = spot ^ j
        at = pl.multiple_of(((s & 1) * (GROUP // 2) + (s >> 1)) * rows, rows)
        target[pl.ds(at, rows), :] = turned[j * rows : (j + 1) * rows, :]


def put_block(block, keep, send, part, columns=slice(None)):
    half = block.shape[0] // 2
    rows = half // (GROUP // 2)
    for i in range(GROUP // 2):
        keep[i, 0, part, :, columns] = block[i * rows : (i + 1) * rows].astype(BF16)
        send[i, 0, part, :, columns] = block[half + i * rows : half + (i + 1) * rows].astype(BF16)


def any_spec():
    return pl.BlockSpec(memory_space=pl.ANY)


def smem_spec():
    return pl.BlockSpec(memory_space=pltpu.SMEM)


def whole(shape):
    return pl.BlockSpec(shape, lambda k: (0,) * len(shape))


def per_quarter(shape, first=0):
    return pl.BlockSpec((1,) + shape, lambda k: (first + k,) + (0,) * len(shape))


def block_specs(matrices, rows, width):
    return [pl.BlockSpec((GROUP // 2, 1, matrices, rows, width), lambda k: (0, k, 0, 0, 0))] * 2


def block_shapes(quarters, matrices, rows, width):
    return [jax.ShapeDtypeStruct((GROUP // 2, quarters, matrices, rows, width), BF16)] * 2


def params(limit=VMEM_BYTES):
    return pltpu.CompilerParams(vmem_limit_bytes=limit, dimension_semantics=("arbitrary",))


def cost(flops, moved):
    return pl.CostEstimate(flops=flops, bytes_accessed=moved, transcendentals=0)


def attention_forward_kernel(plan, count, spot_ref, x, gain, bias, own, *rest):
    middle, normed, proj, logsum, mixed, block, sems = rest[count:]
    k = pl.program_id(0)
    inner = mixed.shape[-1]
    heads = inner // HD

    @pl.when(k == 0)
    def _():
        fetch(spot_ref[0], [own], plan, rest[:count], [block], sems, range(block.shape[0]))
        norm_rows(x, gain, bias, normed)
        middle[...] = x[...]
        logsum[...] = jnp.zeros_like(logsum)

    arrived(k, [block], sems)
    proj[0] = nn(normed[...], block[k, :, : 3 * inner]).astype(BF16)
    lane = lax.broadcasted_iota(jnp.int32, logsum.shape, 1)
    for h in range(heads):
        own_lanes = slice(h * HD, (h + 1) * HD)
        queries = proj[0, :, own_lanes] * jnp.asarray(HD**-0.5, BF16)
        keys = proj[0, :, inner + h * HD : inner + (h + 1) * HD]
        values = proj[0, :, 2 * inner + h * HD : 2 * inner + (h + 1) * HD]
        scores = nt(queries, keys)
        top = jnp.max(scores, axis=-1, keepdims=True)
        powers = jnp.exp(scores - top)
        total = jnp.sum(powers, axis=-1, keepdims=True)
        logsum[...] = jnp.where(lane == k * heads + h, top + jnp.log(total), logsum[...])
        weights = (powers * (1.0 / total)).astype(BF16)
        mixed[0, :, own_lanes] = nn(weights, values).astype(BF16)
    middle[...] += nt(mixed[0], block[k, :, 3 * inner :]).astype(BF16).astype(F32)


def attention_forward(spot, x, gain, bias, own, pieces, n_t):
    length, width = x.shape
    inner = own.shape[1] // 4
    count = len(pieces.arrays)
    out = [
        jax.ShapeDtypeStruct((length, width), F32),
        jax.ShapeDtypeStruct((length, width), BF16),
        jax.ShapeDtypeStruct((n_t, length, 3 * inner), BF16),
        jax.ShapeDtypeStruct((length, 128), F32),
        jax.ShapeDtypeStruct((n_t, length, inner), BF16),
    ]
    return pl.pallas_call(
        functools.partial(attention_forward_kernel, pieces.plan, count),
        grid=(n_t,),
        out_shape=out,
        in_specs=[smem_spec(), whole((length, width)), whole((1, width)), whole((1, width))] + [any_spec()] * (1 + count),
        out_specs=[
            whole((length, width)),
            whole((length, width)),
            per_quarter((length, 3 * inner)),
            whole((length, 128)),
            per_quarter((length, inner)),
        ],
        scratch_shapes=[pltpu.VMEM((n_t,) + own.shape, BF16), pltpu.SemaphoreType.DMA((n_t,))],
        compiler_params=params(),
        cost_estimate=KERNEL_COST,
        name="attention_forward",
    )(spot, x, gain, bias, own, *pieces.arrays)


def mlp_forward_kernel(kept_rows, plan, count, spot_ref, x, gain, bias, own_up, own_down, *rest):
    out, normed, upward, ups, downs, total, sems = rest[count:]
    k = pl.program_id(0)

    @pl.when(k == 0)
    def _():
        fetch(spot_ref[0], [own_up, own_down], plan, rest[:count], [ups, downs], sems, range(ups.shape[0]))
        norm_rows(x, gain, bias, normed)
        total[...] = x[...]

    arrived(k, [ups, downs], sems)
    up = nn(normed[...], ups[k])
    upward[0] = up[:kept_rows]
    active = gelu(up).astype(BF16)
    total[...] += nn(active, downs[k]).astype(BF16).astype(F32)

    @pl.when(k == pl.num_programs(0) - 1)
    def _():
        out[...] = total[...].astype(out.dtype)


def mlp_forward(spot, x, gain, bias, own, pieces, n_t, kept_rows, out_type):
    length, width = x.shape
    hidden = own[0].shape[1]
    count = len(pieces.arrays)
    out = [
        jax.ShapeDtypeStruct((length, width), out_type),
        jax.ShapeDtypeStruct((length, width), BF16),
        jax.ShapeDtypeStruct((n_t, kept_rows, hidden), F32),
    ]
    return pl.pallas_call(
        functools.partial(mlp_forward_kernel, kept_rows, pieces.plan, count),
        grid=(n_t,),
        out_shape=out,
        in_specs=[smem_spec(), whole((length, width)), whole((1, width)), whole((1, width))]
        + [any_spec()] * (2 + count),
        out_specs=[whole((length, width)), whole((length, width)), per_quarter((kept_rows, hidden))],
        scratch_shapes=[
            pltpu.VMEM((n_t,) + own[0].shape, BF16),
            pltpu.VMEM((n_t,) + own[1].shape, BF16),
            pltpu.VMEM((length, width), F32),
            pltpu.SemaphoreType.DMA((n_t,)),
        ],
        compiler_params=params(),
        cost_estimate=KERNEL_COST,
        name="mlp_forward",
    )(spot, x, gain, bias, *own, *pieces.arrays)


def mlp_backward_kernel(quarters, last, blocks, plan, count, spot_ref, incoming, x, gain, normed, upward, total_in, *rest):
    own, sources = rest[:2], rest[2 : 2 + count]
    rest = list(rest[2 + count :])
    total = rest.pop(0)
    if last:
        grad, gain_grad, bias_grad = (rest.pop(0) for _ in range(3))
    if blocks:
        keep, send = rest.pop(0), rest.pop(0)
    ups, downs, sems, *flipped = rest
    k = pl.program_id(0)

    @pl.when(k == 0)
    def _():
        fetch(spot_ref[0], own, plan, sources, [ups, downs], sems, quarters)
        total[...] = jnp.zeros_like(total) if quarters[0] == 0 else total_in[...]
        if blocks:
            flip(spot_ref[0], incoming[...], flipped[0])
            flip(spot_ref[0], normed[...], flipped[1])

    arrived(k, [ups, downs], sems)
    up = upward[0]
    grad_active = nt(incoming[...].astype(BF16), downs[k])
    bell = 0.5 * (1.0 + lax.erf(up * ROOT_HALF))
    grad_up = (grad_active * (bell + up * jnp.exp(-0.5 * up * up) * (1.0 / ROOT_TWO_PI))).astype(BF16)
    total[...] += nt(grad_up, ups[k])
    if blocks:
        put_block(nn(flipped[0][...], (up * bell).astype(BF16)), keep, send, 0)
        put_block(nn(flipped[1][...], grad_up), keep, send, 1)

    if last:

        @pl.when(k == pl.num_programs(0) - 1)
        def _():
            gain_grad[...] = jnp.zeros_like(gain_grad)
            bias_grad[...] = jnp.zeros_like(bias_grad)
            for r in range(0, x.shape[0], 16):
                rows = slice(r, r + 16)
                grad[rows, :] = incoming[rows, :] + norm_back_rows(rows, x, gain, total, gain_grad, bias_grad)


def mlp_backward(spot, incoming, x, gain, normed, upward, total, own, pieces, quarters, blocks):
    length, width = incoming.shape
    n_t, hidden = upward.shape[0], upward.shape[2]
    last = quarters[-1] == n_t - 1
    count = len(quarters)
    if total is None:
        total = jnp.zeros((8, 128), F32)
    out = [jax.ShapeDtypeStruct((length, width), F32)]
    out_specs = [whole((length, width))]
    if last:
        out += [jax.ShapeDtypeStruct(v, F32) for v in ((length, width), (1, width), (1, width))]
        out_specs += [whole((length, width)), whole((1, width)), whole((1, width))]
    scratch = [
        pltpu.VMEM((count,) + own[0].shape, BF16),
        pltpu.VMEM((count,) + own[1].shape, BF16),
        pltpu.SemaphoreType.DMA((count,)),
    ]
    if blocks:
        out += block_shapes(count, 2, width // GROUP, hidden)
        out_specs += block_specs(2, width // GROUP, hidden)
        scratch += [pltpu.VMEM((width, length), BF16)] * 2
    return pl.pallas_call(
        functools.partial(mlp_backward_kernel, quarters, last, blocks, pieces.plan, len(pieces.arrays)),
        grid=(count,),
        out_shape=out,
        in_specs=[
            smem_spec(),
            whole((length, width)),
            whole((length, width)),
            whole((1, width)),
            whole((length, width)),
            per_quarter((length, hidden), quarters[0]),
            whole(total.shape),
        ]
        + [any_spec()] * (2 + len(pieces.arrays)),
        out_specs=out_specs,
        scratch_shapes=scratch,
        compiler_params=params(),
        cost_estimate=KERNEL_COST,
        name="mlp_backward",
    )(spot, incoming, x, gain, normed, upward, total, *own, *pieces.arrays)


def attention_backward_kernel(
    quarters, last, plan, count, spot_ref, incoming, x, gain, normed, proj, logsum, mixed, total_in, own, *rest
):
    sources = rest[:count]
    rest = list(rest[count:])
    total = rest.pop(0)
    if last:
        grad, gain_grad, bias_grad = (rest.pop(0) for _ in range(3))
    keep, send, block, grad_proj, sems, low_t, normed_t = rest
    k = pl.program_id(0)
    top = incoming.shape[0]
    inner = mixed.shape[-1]
    heads = inner // HD

    @pl.when(k == 0)
    def _():
        fetch(spot_ref[0], [own], plan, sources, [block], sems, quarters)
        total[...] = jnp.zeros_like(total) if quarters[0] == 0 else total_in[...]
        grad_proj[...] = jnp.zeros_like(grad_proj)
        flip(spot_ref[0], incoming[...], low_t)
        flip(spot_ref[0], normed[...], normed_t)

    arrived(k, [block], sems)
    grad_mixed = nn(incoming[...].astype(BF16), block[k, :, 3 * inner :]).astype(BF16)
    lane = lax.broadcasted_iota(jnp.int32, (top, 128), 1)
    for h in range(heads):
        own_lanes = slice(h * HD, (h + 1) * HD)
        key_lanes = slice(inner + h * HD, inner + (h + 1) * HD)
        value_lanes = slice(2 * inner + h * HD, 2 * inner + (h + 1) * HD)
        queries = proj[0, :top, own_lanes] * jnp.asarray(HD**-0.5, BF16)
        keys = proj[0, :, key_lanes]
        values = proj[0, :, value_lanes]
        head_grad = grad_mixed[:, own_lanes]
        at = lane == (quarters[0] + k) * heads + h
        row_sum = jnp.sum(jnp.where(at, logsum[:top, :], 0.0), axis=-1, keepdims=True)
        weights = jnp.exp(nt(queries, keys) - row_sum)
        grad_weights = nt(head_grad, values)
        inner_sum = jnp.sum(weights * grad_weights, axis=-1, keepdims=True)
        grad_scores = (weights * (grad_weights - inner_sum)).astype(BF16)
        grad_proj[:top, own_lanes] = (nn(grad_scores, keys) * HD**-0.5).astype(BF16)
        grad_proj[:, key_lanes] = tn(grad_scores, queries).astype(BF16)
        grad_proj[:, value_lanes] = tn(weights.astype(BF16), head_grad).astype(BF16)
    total[...] += nt(grad_proj[...], block[k, :, : 3 * inner])
    put_block(nn(normed_t[...], grad_proj[...]), keep, send, 0, slice(0, 3 * inner))
    put_block(nn(low_t[...], mixed[0, :top, :]), keep, send, 0, slice(3 * inner, 4 * inner))

    if last:

        @pl.when(k == pl.num_programs(0) - 1)
        def _():
            gain_grad[...] = jnp.zeros_like(gain_grad)
            bias_grad[...] = jnp.zeros_like(bias_grad)
            for r in range(0, x.shape[0], 16):
                rows = slice(r, r + 16)
                back = norm_back_rows(rows, x, gain, total, gain_grad, bias_grad)
                grad[rows, :] = back + incoming[rows, :] if r < top else back


def attention_backward(spot, incoming, x, gain, normed, proj, logsum, mixed, total, own, pieces, quarters):
    length, width = x.shape
    top = incoming.shape[0]
    n_t = proj.shape[0]
    last = quarters[-1] == n_t - 1
    count = len(quarters)
    inner = own.shape[1] // 4
    if total is None:
        total = jnp.zeros((8, 128), F32)
    out = [jax.ShapeDtypeStruct((length, width), F32)]
    out_specs = [whole((length, width))]
    if last:
        out += [jax.ShapeDtypeStruct(v, F32) for v in ((length, width), (1, width), (1, width))]
        out_specs += [whole((length, width)), whole((1, width)), whole((1, width))]
    out += block_shapes(count, 1, width // GROUP, 4 * inner)
    out_specs += block_specs(1, width // GROUP, 4 * inner)
    return pl.pallas_call(
        functools.partial(attention_backward_kernel, quarters, last, pieces.plan, len(pieces.arrays)),
        grid=(count,),
        out_shape=out,
        in_specs=[
            smem_spec(),
            whole((top, width)),
            whole((length, width)),
            whole((1, width)),
            whole((length, width)),
            per_quarter((length, 3 * inner), quarters[0]),
            whole((length, 128)),
            per_quarter((length, inner), quarters[0]),
            whole(total.shape),
        ]
        + [any_spec()] * (1 + len(pieces.arrays)),
        out_specs=out_specs,
        scratch_shapes=[
            pltpu.VMEM((count,) + own.shape, BF16),
            pltpu.VMEM((length, 3 * inner), BF16),
            pltpu.SemaphoreType.DMA((count,)),
            pltpu.VMEM((width, top), BF16),
            pltpu.VMEM((width, length), BF16),
        ],
        compiler_params=params(),
        cost_estimate=KERNEL_COST,
        name="attention_backward",
    )(spot, incoming, x, gain, normed, proj, logsum, mixed, total, own, *pieces.arrays)


def swap(values, bit, size):
    return lax.ppermute(values, "dp", [(i, i ^ bit) for i in range(size)])


def shift(values, size):
    return lax.ppermute(values, "tensor", [(i, (i + 1) % size) for i in range(size)])


def after(values, *others):
    return lax.optimization_barrier((values, others))[0]


def small_call(kernel, grid, in_specs, out_specs, out_shape, name):
    return pl.pallas_call(
        kernel,
        grid=grid,
        in_specs=in_specs,
        out_specs=out_specs,
        out_shape=out_shape,
        compiler_params=params(SMALL_VMEM),
        cost_estimate=SMALL_COST,
        name=name,
    )


def pack_kernel(*refs):
    count = refs[-1].shape[0]
    sources, targets = refs[:count], refs[count:]
    rows = targets[0].shape[1]
    for k, source in enumerate(sources):
        for m, target in enumerate(targets):
            target[k] = source[m * rows : (m + 1) * rows, :]


def pack(sources, matrices):
    rows, width = sources[0].shape
    shape = (len(sources), rows // matrices, width)
    return small_call(
        pack_kernel,
        (1,),
        [whole((rows, width))] * len(sources),
        [whole(shape)] * matrices,
        [jax.ShapeDtypeStruct(shape, BF16)] * matrices,
        "pack",
    )(*sources)


def hops(part, n_t):
    out = []
    for _ in range(n_t - 1):
        part = shift(part, n_t)
        out.append(part)
    return out


def corner(x_piece, y_piece, n_dp, by_x):
    return swap(y_piece, 2, n_dp) if by_x else swap(x_piece, 4, n_dp)


def with_core(planes, n_dp):
    return [v for plane in planes for v in (plane, swap(plane, 1, n_dp))]


def at_plane(i, shape):
    return pl.BlockSpec((1, 1) + shape, lambda k: (i, k) + (0,) * len(shape))


def corner_kernel(kept, got, out):
    out[...] = (kept[0, 0].astype(F32) + got[0, 0].astype(F32)).astype(BF16)[None]


def sides_kernel(half, kx, gx, ky, gy, ca, cb, x_out, y_out):
    k = pl.program_id(0)
    x = kx[0, 0].astype(F32) + gx[0, 0].astype(F32)
    y = ky[0, 0].astype(F32) + gy[0, 0].astype(F32)
    a, b = ca[0].astype(F32), cb[0].astype(F32)
    x_out[0] = jnp.where(k < half, x, x + b).astype(BF16)
    y_out[0] = jnp.where(k < half, y + a, y).astype(BF16)


def mine_kernel(kept, got, fx, fy, out):
    total = kept[0, 0].astype(F32) + got[0, 0].astype(F32)
    out[0] = (total + fx[0].astype(F32) + fy[0].astype(F32)).astype(out.dtype)


def last_kernel(*refs):
    *parts, out = refs
    total = parts[0][...].astype(F32)
    for part in parts[1:]:
        total = total + part[...].astype(F32)
    out[...] = total


class Reduction:
    def __init__(self, keep, send, quarters, n_dp, n_t):
        self.keep, self.quarters, self.n_dp, self.n_t = keep, quarters, n_dp, n_t
        self.shape = keep.shape[2:]
        self.count = len(quarters)
        self.half = self.count // 2
        self.got = swap(send, 1, n_dp)
        self.stage = 0

    def spec(self, first=0, top=None):
        top = self.count - 1 if top is None else top
        shape = self.shape
        return pl.BlockSpec((1,) + shape, lambda k: (jnp.clip(k - first, 0, top),) + (0,) * len(shape))

    def corners(self, token):
        self.got = after(self.got, token)
        outs = []
        for first, bit in ((0, 2), (self.half, 4)):
            shape = self.shape
            spec = pl.BlockSpec((1, 1) + shape, lambda k, first=first: (3, first + k) + (0,) * len(shape))
            outs.append(
                small_call(
                    corner_kernel,
                    (self.half,),
                    [spec, spec],
                    pl.BlockSpec((1,) + shape, lambda k: (k,) + (0,) * len(shape)),
                    jax.ShapeDtypeStruct((self.half,) + shape, BF16),
                    "corner_sum",
                )(self.keep, self.got)
            )
        self.corner_a, self.corner_b = swap(outs[0], 2, self.n_dp), swap(outs[1], 4, self.n_dp)
        return outs

    def sides(self, token):
        self.corner_a, self.corner_b = after((self.corner_a, self.corner_b), token)
        full = jax.ShapeDtypeStruct((self.count,) + self.shape, BF16)
        x, y = small_call(
            functools.partial(sides_kernel, self.half),
            (self.count,),
            [at_plane(1, self.shape)] * 2
            + [at_plane(2, self.shape)] * 2
            + [self.spec(0, self.half - 1), self.spec(self.half, self.half - 1)],
            [self.spec()] * 2,
            [full, full],
            "side_sum",
        )(self.keep, self.got, self.keep, self.got, self.corner_a, self.corner_b)
        self.from_x, self.from_y = swap(x, 2, self.n_dp), swap(y, 4, self.n_dp)
        return [x, y]

    def quarters_out(self, token):
        self.from_x, self.from_y = after((self.from_x, self.from_y), token)
        self.parts, outs = [], []
        for i, k in enumerate(self.quarters):
            shape = self.shape
            plane = pl.BlockSpec((1, 1) + shape, lambda _, i=i: (0, i) + (0,) * len(shape))
            side = pl.BlockSpec((1,) + shape, lambda _, i=i: (i,) + (0,) * len(shape))
            part = small_call(
                mine_kernel,
                (1,),
                [plane, plane, side, side],
                whole((1,) + shape),
                jax.ShapeDtypeStruct((1,) + shape, F32 if k == 0 else BF16),
                "own_sum",
            )(self.keep, self.got, self.from_x, self.from_y)
            outs.append(part)
            if k:
                part = lax.ppermute(part, "tensor", [(j, (j - k) % self.n_t) for j in range(self.n_t)])
            self.parts.append(part)
        return outs


def finish(parts, n_dp):
    shape = parts[0].shape
    total = small_call(
        last_kernel, (1,), [whole(shape)] * len(parts), whole(shape), jax.ShapeDtypeStruct(shape, F32), "last_sum"
    )(*parts)
    return [spread_rows(total[0, m], n_dp) for m in range(shape[1])]


def spread_rows(total, n_dp):
    groups = n_dp // GROUP
    me = lax.axis_index("dp")
    rows = total.shape[0]
    bit = n_dp // 2
    while bit >= GROUP:
        rows //= 2
        second = (me // bit) % 2
        kept = lax.dynamic_slice_in_dim(total, second * rows, rows, 0)
        sent = lax.dynamic_slice_in_dim(total, (1 - second) * rows, rows, 0)
        total = kept + swap(sent, bit, n_dp)
        bit //= 2
    if groups > 1:
        total = lax.ppermute(
            total, "dp", [(h * GROUP + s, s * groups + h) for h in range(groups) for s in range(GROUP)]
        )
    return total


def sum_all(values, n_dp, n_t):
    bit = 1
    while bit < n_dp:
        values = values + swap(values, bit, n_dp)
        bit *= 2
    bit = 1
    while bit < n_t:
        values = values + lax.ppermute(values, "tensor", [(i, i ^ bit) for i in range(n_t)])
        bit *= 2
    return values


def shards(tokens, type_table, norm_gain, norm_bias, w_qkv, w_out, w_up, w_down, cotangent, positions, n_dp, n_t):
    total_rows, width = tokens.shape
    pair_count, slots = positions.shape
    assert pair_count == n_t
    length = total_rows // pair_count
    layers = w_qkv.shape[0]
    top = layers - 1
    inner = w_qkv.shape[3]
    me, quarter = lax.axis_index("dp"), lax.axis_index("tensor")
    rows = width // GROUP
    unit = width // n_dp
    spot = me % GROUP
    spots = jnp.reshape(spot, (1,)).astype(jnp.int32)

    def part_of(block):
        return lax.dynamic_slice_in_dim(block, spot * rows, rows, 0)

    mine = lax.dynamic_slice_in_dim(tokens, quarter * length, length, 0).astype(F32)
    row_ids = lax.broadcasted_iota(jnp.int32, (length, 1), 0)
    stream = mine + jnp.where(row_ids < WORDS, type_table[0], type_table[1])
    gains = [[norm_gain[l, i][None] for i in range(2)] for l in range(layers)]
    biases = [[norm_bias[l, i][None] for i in range(2)] for l in range(layers)]
    own = [jnp.concatenate([w_qkv[l].reshape(width, 3 * inner), w_out[l].T], 1) for l in range(layers)]

    def attn_part(l):
        left = lax.dynamic_slice(w_qkv, (l, spot * rows, 0, 0), (1, rows, 3, inner)).reshape(rows, 3 * inner)
        right = lax.dynamic_slice(w_out, (l, 0, spot * rows), (1, inner, rows))[0].T
        return jnp.concatenate([left, right], 1)

    def mlp_part(l):
        return jnp.concatenate(
            [lax.dynamic_slice(w, (l, spot * rows, 0), (1, rows, w.shape[2]))[0] for w in (w_up, w_down)], 0
        )

    attn_hops, mlp_hops = [], []
    token = None
    for l in range(layers):
        for part, out in ((attn_part(l), attn_hops), (mlp_part(l), mlp_hops)):
            out.append(hops(part if token is None else after(part, token), n_t))
            token = out[-1][-2]

    def by_hop(held, matrices):
        at = [[] for _ in range(matrices)]
        for k, v in enumerate(held):
            x_piece, y_piece = swap(v, 2, n_dp), swap(v, 4, n_dp)
            slices = with_core([v, x_piece, y_piece, corner(x_piece, y_piece, n_dp, k % 2 == 1)], n_dp)
            for m in range(matrices):
                at[m].append([(piece, None, m * rows) for piece in slices])
        return Pieces(at)

    def at_once(packed, token_of, first):
        sides = [(v, swap(v, 2, n_dp), swap(v, 4, n_dp)) for v in packed]
        token = token_of(after(first, *packed))
        at = []
        for m, (v, x_piece, y_piece) in enumerate(sides):
            x_piece, y_piece = after((x_piece, y_piece), token[0])
            slices = with_core([v, x_piece, y_piece, corner(x_piece, y_piece, n_dp, m % 2 == 1)], n_dp)
            at.append([[(piece, k, 0) for piece in slices] for k in range(n_t - 1)])
        return Pieces(at), token

    attn_pieces, mlp_pieces, saved = [by_hop(attn_hops[0], 1)], [], []
    for l in range(layers):
        pieces, (middle, normed, proj, logsum, mixed) = at_once(
            pack(mlp_hops[l], 2),
            lambda x: attention_forward(spots, x, gains[l][0], biases[l][0], own[l], attn_pieces[l], n_t),
            stream,
        )
        mlp_pieces.append(pieces)

        def feed_forward(x):
            return mlp_forward(
                spots, x, gains[l][1], biases[l][1], (w_up[l], w_down[l]), pieces, n_t,
                TOP_ROWS if l == top else length, BF16 if l == top else F32,
            )

        if l < top:
            pieces, (following, normed_mlp, upward) = at_once(pack(attn_hops[l + 1], 1), feed_forward, middle)
            attn_pieces.append(pieces)
        else:
            following, normed_mlp, upward = feed_forward(middle)
        saved.append((stream, normed, proj, logsum, mixed, middle, normed_mlp, upward))
        stream = following

    def put_pairs(held):
        out = jnp.zeros((total_rows, width), F32)
        for k, v in enumerate(held):
            out = lax.dynamic_update_slice(out, v.astype(F32), (((quarter - k) % n_t) * length, 0))
        return out

    hidden = [stream]

    place = lax.dynamic_slice_in_dim(positions, quarter, 1, 0)[0]
    cot = lax.dynamic_slice_in_dim(cotangent, quarter, 1, 0)[0]
    onehot = (row_ids[:TOP_ROWS] == place[None, :]).astype(BF16)
    incoming = nn(onehot, cot)

    top_normed = saved[top][6][:TOP_ROWS]
    slot_rows = tn(onehot, top_normed).astype(BF16)
    slot_cot = jnp.where(place[:, None] >= 0, cot, 0)
    spare = jnp.zeros((SLOT_ROWS - slots, width), BF16)
    masked = [jnp.concatenate([slot_cot, spare, slot_rows, spare], 0)[None]]

    everything = tuple(range(n_t))
    halves = (everything[: n_t // 2], everything[n_t // 2 :])
    gain_grads = [[None, None] for _ in range(layers)]
    bias_grads = [[None, None] for _ in range(layers)]
    attn_sums, mlp_sums = [None] * layers, [None] * layers
    pending = []

    def advance(token):
        outs = []
        for reduction in pending:
            outs += (reduction.corners, reduction.sides, reduction.quarters_out)[reduction.stage](token)
            reduction.stage += 1
        pending[:] = [r for r in pending if r.stage < 3]
        for held in (hidden, masked):
            if len(held) > 1:
                held[-1] = after(held[-1], token)
                outs.append(held[-1])
            if len(held) < n_t:
                held.append(shift(held[-1], n_t))
        return outs

    ready = advance(incoming)
    for l in range(top, -1, -1):
        stream_l, normed, proj, logsum, mixed, middle, normed_mlp, upward = saved[l]
        part = slice(0, incoming.shape[0])
        total = None
        mlp_sums[l] = []
        for quarters in [everything] if l == top else halves:
            outs = mlp_backward(
                spots, after(incoming, ready), middle[part], gains[l][1], normed_mlp[part], upward, total,
                (w_up[l], w_down[l]), mlp_pieces[l], quarters, l < top,
            )
            total = outs[0]
            ready = advance(total)
            if l < top:
                mlp_sums[l].append(Reduction(outs[-2], outs[-1], quarters, n_dp, n_t))
                pending.append(mlp_sums[l][-1])
        incoming, gain_grads[l][1], bias_grads[l][1] = outs[1:4]
        total = None
        attn_sums[l] = []
        for quarters in [everything] if l == top else halves:
            outs = attention_backward(
                spots, after(incoming, ready), stream_l, gains[l][0], normed, proj, logsum, mixed, total,
                own[l], attn_pieces[l], quarters,
            )
            total = outs[0]
            ready = advance(total)
            attn_sums[l].append(Reduction(outs[-2], outs[-1], quarters, n_dp, n_t))
            pending.append(attn_sums[l][-1])
        incoming, gain_grads[l][0], bias_grads[l][0] = outs[1:4]
    tokens_held = [incoming.astype(BF16)]
    tokens_held += hops(tokens_held[0], n_t)
    while pending:
        ready = advance(ready)

    all_rows = jnp.concatenate(masked, 0)
    bit = 2
    while bit < 2 * n_dp:
        all_rows = jnp.concatenate([all_rows, swap(all_rows, bit if bit < n_dp else 1, n_dp)], 0)
        bit *= 2
    all_cot = all_rows[:, :SLOT_ROWS].reshape(-1, width)
    all_normed = all_rows[:, SLOT_ROWS:].reshape(-1, width)
    slot_up = nn(all_normed, w_up[top])
    slot_grad = (nt(all_cot, w_down[top]) * gelu_slope(slot_up)).astype(BF16)
    grad_up_top = tn(lax.dynamic_slice_in_dim(all_normed, me * unit, unit, 1), slot_grad)
    grad_down_top = tn(
        gelu(slot_up).astype(BF16), lax.dynamic_slice_in_dim(all_cot, me * unit, unit, 1)
    )

    def finished(reductions):
        return finish([p for r in reductions for p in r.parts], n_dp)

    sums = {}
    for l in range(layers):
        (sums["attn", l],) = finished(attn_sums[l])
        if l < top:
            sums["down", l], sums["up", l] = finished(mlp_sums[l])

    hidden_out, grad_tokens = put_pairs(hidden), put_pairs(tokens_held)
    type_grad = jnp.stack([jnp.sum(incoming[:WORDS], 0), jnp.sum(incoming[WORDS:], 0)])
    rows_all = jnp.concatenate(
        [type_grad] + [g for pair in gain_grads for g in pair] + [b for pair in bias_grads for b in pair], 0
    )
    rows_all = sum_all(rows_all, n_dp, n_t)
    rows_mine = lax.dynamic_slice_in_dim(rows_all, me * unit, unit, 1)
    grad_gain = rows_mine[2 : 2 + 2 * layers].reshape(layers, 2, unit)
    grad_bias = rows_mine[2 + 2 * layers :].reshape(layers, 2, unit)
    grad_qkv = jnp.stack([sums["attn", l][:, : 3 * inner].reshape(unit, 3, inner) for l in range(layers)])
    grad_out = jnp.stack([sums["attn", l][:, 3 * inner :].T for l in range(layers)])
    grad_up = jnp.stack([grad_up_top if l == top else sums["up", l] for l in range(layers)])
    grad_down = jnp.stack([grad_down_top if l == top else sums["down", l].T for l in range(layers)])
    return hidden_out, grad_tokens, rows_mine[:2], grad_gain, grad_bias, grad_qkv, grad_out, grad_up, grad_down


def solution(mesh):
    n_dp, n_t = mesh.shape["dp"], mesh.shape["tensor"]
    placed = (
        P("dp", None),
        P(),
        P(),
        P(),
        P(None, None, None, "tensor"),
        P(None, "tensor", None),
        P(None, None, "tensor"),
        P(None, "tensor", None),
        P("dp", None, None),
        P("dp", None),
    )

    def run(*args):
        return shards(*args, n_dp, n_t)

    return jax.shard_map(
        run,
        mesh=mesh,
        in_specs=placed,
        out_specs=(
            P("dp", None),
            P("dp", None),
            P(None, "dp"),
            P(None, None, "dp"),
            P(None, None, "dp"),
            P(None, "dp", None, "tensor"),
            P(None, "tensor", "dp"),
            P(None, "dp", "tensor"),
            P(None, "tensor", "dp"),
        ),
        check_vma=False,
    )
```

```python
import functools

import jax
import jax.numpy as jnp
from jax import lax
from jax.experimental import pallas as pl
from jax.experimental.pallas import tpu as pltpu
from jax.sharding import PartitionSpec as P

HD = 64
WORDS = 40
TOP_ROWS = 48
SLOT_ROWS = 16
EPSILON = 1e-06
ROOT_HALF = 0.7071067811865476
ROOT_TWO_PI = 2.5066282746310002
GROUP = 8
STEP = 32
SIDES_FIRST = True
F32 = jnp.float32
BF16 = jnp.bfloat16
SMALL_VMEM = 16 * 1024 * 1024
VMEM_BYTES = 60 * 1024 * 1024


def dot(left, right, dims):
    return lax.dot_general(left, right, (dims, ((), ())), preferred_element_type=F32)


def nn(left, right):
    return dot(left, right, ((1,), (0,)))


def nt(left, right):
    return dot(left, right, ((1,), (1,)))


def tn(left, right):
    return dot(left, right, ((0,), (0,)))


def gelu(values):
    return 0.5 * values * (1.0 + lax.erf(values * ROOT_HALF))


def gelu_slope(values):
    return 0.5 * (1.0 + lax.erf(values * ROOT_HALF)) + values * jnp.exp(-0.5 * values * values) / ROOT_TWO_PI


def norm_parts(values):
    average = jnp.mean(values, axis=-1, keepdims=True)
    centred = values - average
    spread = jnp.mean(centred * centred, axis=-1, keepdims=True)
    rate = lax.rsqrt(spread + EPSILON)
    return centred * rate, rate


def norm_rows(source, gain, bias, target):
    step = STEP if source.shape[0] % STEP == 0 else STEP // 2
    for r in range(0, source.shape[0], step):
        rows = slice(r, r + step)
        target[rows, :] = (norm_parts(source[rows, :])[0] * gain[...] + bias[...]).astype(BF16)


def norm_back_rows(rows, values, gain, incoming, gain_grad, bias_grad):
    unit, rate = norm_parts(values[rows, :])
    e = incoming[rows, :]
    scaled = e * gain[...]
    inner = jnp.mean(scaled * unit, axis=-1, keepdims=True)
    gain_grad[...] += jnp.sum(e * unit, axis=0, keepdims=True)
    bias_grad[...] += jnp.sum(e, axis=0, keepdims=True)
    return rate * (scaled - jnp.mean(scaled, axis=-1, keepdims=True) - unit * inner)


def flops(count):
    return pl.CostEstimate(flops=count, bytes_accessed=1_000_000, transcendentals=0)


KERNEL_COST = pl.CostEstimate(flops=40_000_000_000, bytes_accessed=1_000_000, transcendentals=0)
SMALL_COST = pl.CostEstimate(flops=1_000_000_000, bytes_accessed=1_000_000, transcendentals=0)


class Pieces:
    def __init__(self, at):
        self.arrays = []
        self.plan = []
        for matrix in at:
            for k, slices in enumerate(matrix, 1):
                for s, (array, lead, row) in enumerate(slices):
                    found = [i for i, v in enumerate(self.arrays) if v is array]
                    if not found:
                        self.arrays.append(array)
                        found = [len(self.arrays) - 1]
                    self.plan.append((len(self.plan) // (len(matrix) * GROUP), k, s, found[0], lead, row))


def fetch(spot, layer, own, plan, sources, scratches, sems, quarters):
    rows = scratches[0].shape[1] // GROUP
    for k in quarters:
        for m, scratch in enumerate(scratches):
            if k == 0 and own:
                pltpu.make_async_copy(own[m].at[layer], scratch.at[0], sems.at[0]).start()
        for m, at_k, s, which, lead, row in plan:
            if at_k == k:
                source = sources[which].at[lead]
                at = pl.multiple_of((spot ^ s) * rows, rows)
                pltpu.make_async_copy(
                    source.at[pl.ds(row, rows)],
                    scratches[m].at[k - quarters[0], pl.ds(at, rows)],
                    sems.at[k - quarters[0]],
                ).start()


def arrived(k, scratches, sems):
    for scratch in scratches:
        pltpu.make_async_copy(scratch.at[k], scratch.at[k], sems.at[k]).wait()


def own_copies(layer, own_qkv, own_out, raw_qkv, raw_out, sem):
    return [
        pltpu.make_async_copy(own_qkv.at[layer], raw_qkv, sem),
        pltpu.make_async_copy(own_out.at[layer], raw_out, sem),
    ]


def own_block(copies, raw_qkv, raw_out, block):
    for copy in copies:
        copy.wait()
    inner = raw_qkv.shape[2]
    for c in range(3):
        block[0, :, c * inner : (c + 1) * inner] = raw_qkv[c]
    block[0, :, 3 * inner :] = raw_out[...].astype(F32).T.astype(BF16)


def flip(spot, source, target):
    width = source.shape[1]
    rows = width // GROUP
    turned = source.astype(F32).T.astype(BF16)
    for j in range(GROUP):
        s = spot ^ j
        at = pl.multiple_of(((s & 1) * (GROUP // 2) + (s >> 1)) * rows, rows)
        target[pl.ds(at, rows), :] = turned[j * rows : (j + 1) * rows, :]


def put_block(block, keep, send, part, columns=slice(None)):
    half = block.shape[0] // 2
    rows = half // (GROUP // 2)
    for i in range(GROUP // 2):
        keep[i, 0, part, :, columns] = block[i * rows : (i + 1) * rows].astype(BF16)
        send[i, 0, part, :, columns] = block[half + i * rows : half + (i + 1) * rows].astype(BF16)


def any_spec():
    return pl.BlockSpec(memory_space=pl.ANY)


def smem_spec():
    return pl.BlockSpec(memory_space=pltpu.SMEM)


def whole(shape):
    return pl.BlockSpec(shape, lambda k: (0,) * len(shape))


def per_quarter(shape, first=0):
    return pl.BlockSpec((1,) + shape, lambda k: (first + k,) + (0,) * len(shape))


def block_specs(matrices, rows, width):
    return [pl.BlockSpec((GROUP // 2, 1, matrices, rows, width), lambda k: (0, k, 0, 0, 0))] * 2


def block_shapes(quarters, matrices, rows, width):
    return [jax.ShapeDtypeStruct((GROUP // 2, quarters, matrices, rows, width), BF16)] * 2


def params(limit=VMEM_BYTES):
    return pltpu.CompilerParams(vmem_limit_bytes=limit)


def cost(flops, moved):
    return pl.CostEstimate(flops=flops, bytes_accessed=moved, transcendentals=0)


def attention_forward_kernel(layer, plan, count, spot_ref, x, gain, bias, own_qkv, own_out, *rest):
    middle, normed, proj, logsum, mixed, block, sems, raw_qkv, raw_out = rest[count:]
    k = pl.program_id(0)
    inner = mixed.shape[-1]
    heads = inner // HD

    @pl.when(k == 0)
    def _():
        copies = own_copies(layer, own_qkv, own_out, raw_qkv, raw_out, sems.at[0])
        for copy in copies:
            copy.start()
        fetch(spot_ref[0], layer, [], plan, rest[:count], [block], sems, range(block.shape[0]))
        norm_rows(x, gain, bias, normed)
        middle[...] = x[...]
        logsum[...] = jnp.zeros_like(logsum)
        own_block(copies, raw_qkv, raw_out, block)

    @pl.when(k > 0)
    def _():
        arrived(k, [block], sems)

    proj[0] = nn(normed[...], block[k, :, : 3 * inner]).astype(BF16)
    lane = lax.broadcasted_iota(jnp.int32, logsum.shape, 1)
    for h in range(heads):
        own_lanes = slice(h * HD, (h + 1) * HD)
        queries = proj[0, :, own_lanes] * jnp.asarray(HD**-0.5, BF16)
        keys = proj[0, :, inner + h * HD : inner + (h + 1) * HD]
        values = proj[0, :, 2 * inner + h * HD : 2 * inner + (h + 1) * HD]
        scores = nt(queries, keys)
        top = jnp.max(scores, axis=-1, keepdims=True)
        powers = jnp.exp(scores - top)
        total = jnp.sum(powers, axis=-1, keepdims=True)
        logsum[...] = jnp.where(lane == k * heads + h, top + jnp.log(total), logsum[...])
        weights = (powers * (1.0 / total)).astype(BF16)
        mixed[0, :, own_lanes] = nn(weights, values).astype(BF16)
    middle[...] += nt(mixed[0], block[k, :, 3 * inner :]).astype(BF16).astype(F32)


def attention_forward(spot, x, gain, bias, layer, own, pieces, n_t, work):
    length, width = x.shape
    inner = own[1].shape[1]
    count = len(pieces.arrays)
    out = [
        jax.ShapeDtypeStruct((length, width), F32),
        jax.ShapeDtypeStruct((length, width), BF16),
        jax.ShapeDtypeStruct((n_t, length, 3 * inner), BF16),
        jax.ShapeDtypeStruct((length, 128), F32),
        jax.ShapeDtypeStruct((n_t, length, inner), BF16),
    ]
    return pl.pallas_call(
        functools.partial(attention_forward_kernel, layer, pieces.plan, count),
        grid=(n_t,),
        out_shape=out,
        in_specs=[smem_spec(), whole((length, width)), whole((1, width)), whole((1, width))] + [any_spec()] * (2 + count),
        out_specs=[
            whole((length, width)),
            whole((length, width)),
            per_quarter((length, 3 * inner)),
            whole((length, 128)),
            per_quarter((length, inner)),
        ],
        scratch_shapes=[
            pltpu.VMEM((n_t, width, 4 * inner), BF16),
            pltpu.SemaphoreType.DMA((n_t,)),
            pltpu.VMEM((3, width, inner), BF16),
            pltpu.VMEM((inner, width), BF16),
        ],
        compiler_params=params(),
        cost_estimate=flops(work),
        name="attention_forward",
    )(spot, x, gain, bias, *own, *pieces.arrays)


def mlp_forward_kernel(kept_rows, layer, plan, count, spot_ref, x, gain, bias, own_up, own_down, *rest):
    if kept_rows:
        out, normed, upward, ups, downs, total, sems = rest[count:]
    else:
        out, ups, downs, total, sems, normed = rest[count:]
    k = pl.program_id(0)

    @pl.when(k == 0)
    def _():
        fetch(spot_ref[0], layer, [own_up, own_down], plan, rest[:count], [ups, downs], sems, range(ups.shape[0]))
        norm_rows(x, gain, bias, normed)
        total[...] = x[...]

    arrived(k, [ups, downs], sems)
    up = nn(normed[...], ups[k])
    if kept_rows:
        upward[0] = up
    active = gelu(up).astype(BF16)
    total[...] += nn(active, downs[k]).astype(BF16).astype(F32)

    @pl.when(k == pl.num_programs(0) - 1)
    def _():
        out[...] = total[...].astype(out.dtype)


def mlp_forward(spot, x, gain, bias, layer, own, pieces, n_t, kept_rows, out_type):
    length, width = x.shape
    hidden = own[0].shape[2]
    count = len(pieces.arrays)
    out = [jax.ShapeDtypeStruct((length, width), out_type)]
    out_specs = [whole((length, width))]
    scratch = []
    if kept_rows:
        out += [jax.ShapeDtypeStruct((length, width), BF16), jax.ShapeDtypeStruct((n_t, length, hidden), F32)]
        out_specs += [whole((length, width)), per_quarter((length, hidden))]
    else:
        scratch.append(pltpu.VMEM((length, width), BF16))
    return pl.pallas_call(
        functools.partial(mlp_forward_kernel, kept_rows, layer, pieces.plan, count),
        grid=(n_t,),
        out_shape=out,
        in_specs=[smem_spec(), whole((length, width)), whole((1, width)), whole((1, width))]
        + [any_spec()] * (2 + count),
        out_specs=out_specs,
        scratch_shapes=[
            pltpu.VMEM((n_t,) + own[0].shape[1:], BF16),
            pltpu.VMEM((n_t,) + own[1].shape[1:], BF16),
            pltpu.VMEM((length, width), F32),
            pltpu.SemaphoreType.DMA((n_t,)),
        ]
        + scratch,
        compiler_params=params(),
        cost_estimate=KERNEL_COST,
        name="mlp_forward",
    )(spot, x, gain, bias, *own, *pieces.arrays)


def mlp_backward_kernel(quarters, last, blocks, layer, plan, count, spot_ref, incoming, x, gain, normed, upward, total_in, *rest):
    own, sources = rest[:2], rest[2 : 2 + count]
    rest = list(rest[2 + count :])
    total = rest.pop(0)
    if last:
        grad, gain_grad, bias_grad = (rest.pop(0) for _ in range(3))
    if blocks:
        keep, send = rest.pop(0), rest.pop(0)
    ups, downs, sems, *flipped = rest
    k = pl.program_id(0)

    @pl.when(k == 0)
    def _():
        fetch(spot_ref[0], layer, own, plan, sources, [ups, downs], sems, quarters)
        total[...] = jnp.zeros_like(total) if quarters[0] == 0 else total_in[...]
        if blocks:
            flip(spot_ref[0], incoming[...], flipped[0])
            flip(spot_ref[0], normed[...], flipped[1])

    arrived(k, [ups, downs], sems)
    up = upward[0]
    grad_active = nt(incoming[...].astype(BF16), downs[k])
    bell = 0.5 * (1.0 + lax.erf(up * ROOT_HALF))
    grad_up = (grad_active * (bell + up * jnp.exp(-0.5 * up * up) * (1.0 / ROOT_TWO_PI))).astype(BF16)
    total[...] += nt(grad_up, ups[k])
    if blocks:
        put_block(nn(flipped[0][...], (up * bell).astype(BF16)), keep, send, 0)
        put_block(nn(flipped[1][...], grad_up), keep, send, 1)

    if last:

        @pl.when(k == pl.num_programs(0) - 1)
        def _():
            gain_grad[...] = jnp.zeros_like(gain_grad)
            bias_grad[...] = jnp.zeros_like(bias_grad)
            for r in range(0, x.shape[0], 16):
                rows = slice(r, r + 16)
                grad[rows, :] = incoming[rows, :] + norm_back_rows(rows, x, gain, total, gain_grad, bias_grad)


def mlp_backward(spot, incoming, x, gain, normed, upward, total, layer, own, pieces, quarters, blocks):
    length, width = incoming.shape
    n_t, hidden = upward.shape[0], upward.shape[2]
    last = quarters[-1] == n_t - 1
    count = len(quarters)
    if total is None:
        total = jnp.zeros((8, 128), F32)
    out = [jax.ShapeDtypeStruct((length, width), F32)]
    out_specs = [whole((length, width))]
    if last:
        out += [jax.ShapeDtypeStruct(v, F32) for v in ((length, width), (1, width), (1, width))]
        out_specs += [whole((length, width)), whole((1, width)), whole((1, width))]
    scratch = [
        pltpu.VMEM((count,) + own[0].shape[1:], BF16),
        pltpu.VMEM((count,) + own[1].shape[1:], BF16),
        pltpu.SemaphoreType.DMA((count,)),
    ]
    if blocks:
        out += block_shapes(count, 2, width // GROUP, hidden)
        out_specs += block_specs(2, width // GROUP, hidden)
        scratch += [pltpu.VMEM((width, length), BF16)] * 2
    return pl.pallas_call(
        functools.partial(mlp_backward_kernel, quarters, last, blocks, layer, pieces.plan, len(pieces.arrays)),
        grid=(count,),
        out_shape=out,
        in_specs=[
            smem_spec(),
            whole((length, width)),
            whole((length, width)),
            whole((1, width)),
            whole((length, width)),
            per_quarter((length, hidden), quarters[0]),
            whole(total.shape),
        ]
        + [any_spec()] * (2 + len(pieces.arrays)),
        out_specs=out_specs,
        scratch_shapes=scratch,
        compiler_params=params(),
        cost_estimate=KERNEL_COST,
        name="mlp_backward",
    )(spot, incoming, x, gain, normed, upward, total, *own, *pieces.arrays)


def top_kernel(layer, plan, count, spot_ref, incoming, x, gain, bias, own_up, own_down, *rest):
    grad, gain_grad, bias_grad, normed, ups, downs, total, sems = rest[count:]
    k = pl.program_id(0)

    @pl.when(k == 0)
    def _():
        fetch(spot_ref[0], layer, [own_up, own_down], plan, rest[:count], [ups, downs], sems, range(ups.shape[0]))
        norm_rows(x, gain, bias, normed)
        total[...] = jnp.zeros_like(total)

    arrived(k, [ups, downs], sems)
    up = nn(normed[...], ups[k])
    grad_up = (nt(incoming[...].astype(BF16), downs[k]) * gelu_slope(up)).astype(BF16)
    total[...] += nt(grad_up, ups[k])

    @pl.when(k == pl.num_programs(0) - 1)
    def _():
        gain_grad[...] = jnp.zeros_like(gain_grad)
        bias_grad[...] = jnp.zeros_like(bias_grad)
        for r in range(0, incoming.shape[0], 16):
            rows = slice(r, r + 16)
            grad[rows, :] = incoming[rows, :] + norm_back_rows(rows, x, gain, total, gain_grad, bias_grad)


def top_backward(spot, incoming, x, gain, bias, layer, own, pieces, n_t):
    length, width = incoming.shape
    rows = pl.BlockSpec((length, width), lambda k: (0, 0))
    row = whole((1, width))
    return pl.pallas_call(
        functools.partial(top_kernel, layer, pieces.plan, len(pieces.arrays)),
        grid=(n_t,),
        out_shape=[
            jax.ShapeDtypeStruct((length, width), F32),
            jax.ShapeDtypeStruct((1, width), F32),
            jax.ShapeDtypeStruct((1, width), F32),
            jax.ShapeDtypeStruct((length, width), BF16),
        ],
        in_specs=[smem_spec(), rows, rows, row, row] + [any_spec()] * (2 + len(pieces.arrays)),
        out_specs=[rows, row, row, rows],
        scratch_shapes=[
            pltpu.VMEM((n_t,) + own[0].shape[1:], BF16),
            pltpu.VMEM((n_t,) + own[1].shape[1:], BF16),
            pltpu.VMEM((length, width), F32),
            pltpu.SemaphoreType.DMA((n_t,)),
        ],
        compiler_params=params(),
        cost_estimate=KERNEL_COST,
        name="top_backward",
    )(spot, incoming, x, gain, bias, *own, *pieces.arrays)


def attention_backward_kernel(
    quarters, last, layer, plan, count, spot_ref, incoming, x, gain, normed, proj, logsum, mixed, total_in, own_qkv, own_out, *rest
):
    sources = rest[:count]
    rest = list(rest[count:])
    total = rest.pop(0)
    if last:
        grad, gain_grad, bias_grad = (rest.pop(0) for _ in range(3))
    keep, send, block, grad_proj, sems, low_t, normed_t, raw_qkv, raw_out = rest
    k = pl.program_id(0)
    top = incoming.shape[0]
    inner = mixed.shape[-1]
    heads = inner // HD

    @pl.when(k == 0)
    def _():
        if quarters[0] == 0:
            copies = own_copies(layer, own_qkv, own_out, raw_qkv, raw_out, sems.at[0])
            for copy in copies:
                copy.start()
        fetch(spot_ref[0], layer, [], plan, sources, [block], sems, quarters)
        total[...] = jnp.zeros_like(total) if quarters[0] == 0 else total_in[...]
        grad_proj[...] = jnp.zeros_like(grad_proj)
        flip(spot_ref[0], incoming[...], low_t)
        flip(spot_ref[0], normed[...], normed_t)
        if quarters[0] == 0:
            own_block(copies, raw_qkv, raw_out, block)

    @pl.when(quarters[0] + k > 0)
    def _():
        arrived(k, [block], sems)

    grad_mixed = nn(incoming[...].astype(BF16), block[k, :, 3 * inner :]).astype(BF16)
    lane = lax.broadcasted_iota(jnp.int32, (top, 128), 1)
    for h in range(heads):
        own_lanes = slice(h * HD, (h + 1) * HD)
        key_lanes = slice(inner + h * HD, inner + (h + 1) * HD)
        value_lanes = slice(2 * inner + h * HD, 2 * inner + (h + 1) * HD)
        queries = proj[0, :top, own_lanes] * jnp.asarray(HD**-0.5, BF16)
        keys = proj[0, :, key_lanes]
        values = proj[0, :, value_lanes]
        head_grad = grad_mixed[:, own_lanes]
        at = lane == (quarters[0] + k) * heads + h
        row_sum = jnp.sum(jnp.where(at, logsum[:top, :], 0.0), axis=-1, keepdims=True)
        weights = jnp.exp(nt(queries, keys) - row_sum)
        grad_weights = nt(head_grad, values)
        inner_sum = jnp.sum(weights * grad_weights, axis=-1, keepdims=True)
        grad_scores = (weights * (grad_weights - inner_sum)).astype(BF16)
        grad_proj[:top, own_lanes] = (nn(grad_scores, keys) * HD**-0.5).astype(BF16)
        grad_proj[:, key_lanes] = tn(grad_scores, queries).astype(BF16)
        grad_proj[:, value_lanes] = tn(weights.astype(BF16), head_grad).astype(BF16)
    total[...] += nt(grad_proj[...], block[k, :, : 3 * inner])
    put_block(nn(normed_t[...], grad_proj[...]), keep, send, 0, slice(0, 3 * inner))
    put_block(nn(low_t[...], mixed[0, :top, :]), keep, send, 0, slice(3 * inner, 4 * inner))

    if last:

        @pl.when(k == pl.num_programs(0) - 1)
        def _():
            gain_grad[...] = jnp.zeros_like(gain_grad)
            bias_grad[...] = jnp.zeros_like(bias_grad)
            for r in range(0, x.shape[0], 16):
                rows = slice(r, r + 16)
                back = norm_back_rows(rows, x, gain, total, gain_grad, bias_grad)
                grad[rows, :] = back + incoming[rows, :] if r < top else back


def attention_backward(spot, incoming, x, gain, normed, proj, logsum, mixed, total, layer, own, pieces, quarters):
    length, width = x.shape
    top = incoming.shape[0]
    n_t = proj.shape[0]
    last = quarters[-1] == n_t - 1
    count = len(quarters)
    inner = own[1].shape[1]
    if total is None:
        total = jnp.zeros((8, 128), F32)
    out = [jax.ShapeDtypeStruct((length, width), F32)]
    out_specs = [whole((length, width))]
    if last:
        out += [jax.ShapeDtypeStruct(v, F32) for v in ((length, width), (1, width), (1, width))]
        out_specs += [whole((length, width)), whole((1, width)), whole((1, width))]
    out += block_shapes(count, 1, width // GROUP, 4 * inner)
    out_specs += block_specs(1, width // GROUP, 4 * inner)
    return pl.pallas_call(
        functools.partial(attention_backward_kernel, quarters, last, layer, pieces.plan, len(pieces.arrays)),
        grid=(count,),
        out_shape=out,
        in_specs=[
            smem_spec(),
            whole((top, width)),
            whole((length, width)),
            whole((1, width)),
            whole((length, width)),
            per_quarter((length, 3 * inner), quarters[0]),
            whole((length, 128)),
            per_quarter((length, inner), quarters[0]),
            whole(total.shape),
        ]
        + [any_spec()] * (2 + len(pieces.arrays)),
        out_specs=out_specs,
        scratch_shapes=[
            pltpu.VMEM((count, width, 4 * inner), BF16),
            pltpu.VMEM((length, 3 * inner), BF16),
            pltpu.SemaphoreType.DMA((count,)),
            pltpu.VMEM((width, top), BF16),
            pltpu.VMEM((width, length), BF16),
            pltpu.VMEM((3, width, inner), BF16),
            pltpu.VMEM((inner, width), BF16),
        ],
        compiler_params=params(),
        cost_estimate=KERNEL_COST,
        name="attention_backward",
    )(spot, incoming, x, gain, normed, proj, logsum, mixed, total, *own, *pieces.arrays)


def swap(values, bit, size):
    return lax.ppermute(values, "dp", [(i, i ^ bit) for i in range(size)])


def after(values, *others):
    return lax.optimization_barrier((values, others))[0]


def gate(outs, *others):
    return lax.optimization_barrier((outs, others))


def small_call(kernel, grid, in_specs, out_specs, out_shape, name):
    return pl.pallas_call(
        kernel,
        grid=grid,
        in_specs=in_specs,
        out_specs=out_specs,
        out_shape=out_shape,
        compiler_params=params(SMALL_VMEM),
        cost_estimate=SMALL_COST,
        name=name,
    )


def pack_kernel(groups, *refs):
    sources, targets = refs[: -len(groups)], refs[-len(groups) :]
    rows = targets[0].shape[2]
    for k, source in enumerate(sources):
        for target, (first, count) in zip(targets, groups):
            for m in range(count):
                target[m, k] = source[(first + m) * rows : (first + m + 1) * rows, :]


def pack(sources, *counts):
    total, width = sources[0].shape
    rows = total // sum(counts)
    groups = [(sum(counts[:i]), count) for i, count in enumerate(counts)]
    shapes = [(count, len(sources), rows, width) for count in counts]
    return small_call(
        functools.partial(pack_kernel, groups),
        (1,),
        [whole((total, width))] * len(sources),
        [whole(shape) for shape in shapes],
        [jax.ShapeDtypeStruct(shape, BF16) for shape in shapes],
        "pack",
    )(*sources)


def corner(x_piece, y_piece, n_dp, by_x):
    return swap(y_piece, 2, n_dp) if by_x else swap(x_piece, 4, n_dp)


def sum_kernel(*refs):
    *operands, out = refs
    total = operands[0][...].astype(F32)
    for operand in operands[1:]:
        total = total + operand[...].astype(F32).reshape(total.shape)
    out[...] = total.astype(out.dtype).reshape(out.shape)


def mine_kernel(*refs):
    kept, got, first, second, *outs = refs
    for i, out in enumerate(outs):
        total = kept[0, i].astype(F32) + got[0, i].astype(F32) + first[0, i].astype(F32) + second[i].astype(F32)
        out[0] = total.astype(out.dtype)


def last_kernel(*refs):
    *parts, out = refs
    total = parts[0][...].astype(F32)
    for part in parts[1:]:
        total = total + part[...].astype(F32)
    out[...] = total


class Reduction:
    def __init__(self, keep, got, first, quarters, by_x, n_dp, n_t):
        self.keep, self.got, self.first, self.quarters = keep, got, first, quarters
        self.near, self.far = (2, 4) if by_x else (4, 2)
        self.n_dp, self.n_t = n_dp, n_t
        self.shape = keep.shape[2:]

    def plane(self, i):
        count = len(self.quarters)
        zeros = (0,) * len(self.shape)
        return pl.BlockSpec((1, count) + self.shape, lambda _: (i, self.first // count) + zeros)

    def near_sum(self, token):
        self.got = after(self.got, token)
        zeros = (0,) * len(self.shape)
        count = len(self.quarters)
        near = self.near // 2
        spec = pl.BlockSpec(
            (1, count) + self.shape, lambda i: (jnp.where(i == 0, near, 3), self.first // count) + zeros
        )
        out = small_call(
            sum_kernel,
            (2,),
            [spec, spec],
            pl.BlockSpec((1, count) + self.shape, lambda i: (i, 0) + zeros),
            jax.ShapeDtypeStruct((2, count) + self.shape, BF16),
            "near_sum",
        )(self.keep, self.got)
        self.from_near = swap(out, self.near, self.n_dp)
        return out

    def far_sum(self, token):
        self.from_near = after(self.from_near, token)
        zeros = (0,) * len(self.shape)
        count = len(self.quarters)
        full = (count,) + self.shape
        out = small_call(
            sum_kernel,
            (1,),
            [
                self.plane(self.far // 2),
                self.plane(self.far // 2),
                pl.BlockSpec((1,) + full, lambda _: (1, 0) + zeros),
            ],
            whole(full),
            jax.ShapeDtypeStruct(full, BF16),
            "far_sum",
        )(self.keep, self.got, self.from_near)
        self.from_far = swap(out, self.far, self.n_dp)
        return out

    def own_sum(self, token):
        self.from_far = after(self.from_far, token)
        zeros = (0,) * len(self.shape)
        full = (len(self.quarters),) + self.shape
        one = (1,) + self.shape
        outs = small_call(
            mine_kernel,
            (1,),
            [self.plane(0), self.plane(0), pl.BlockSpec((1,) + full, lambda _: (0, 0) + zeros), whole(full)],
            [whole(one)] * len(self.quarters),
            [jax.ShapeDtypeStruct(one, BF16 if k else F32) for k in self.quarters],
            "own_sum",
        )(self.keep, self.got, self.from_near, self.from_far)
        self.parts = [
            lax.ppermute(v, "tensor", [(j, (j - k) % self.n_t) for j in range(self.n_t)]) if k else v
            for k, v in zip(self.quarters, outs)
        ]
        return list(outs)


def finish(parts, n_dp):
    shape = parts[0].shape
    total = small_call(
        last_kernel, (1,), [whole(shape)] * len(parts), whole(shape), jax.ShapeDtypeStruct(shape, F32), "last_sum"
    )(*parts)
    return [spread_rows(total[0, m], n_dp) for m in range(shape[1])]


def spread_rows(total, n_dp):
    groups = n_dp // GROUP
    me = lax.axis_index("dp")
    rows = total.shape[0]
    bit = n_dp // 2
    while bit >= GROUP:
        rows //= 2
        second = (me // bit) % 2
        kept = lax.dynamic_slice_in_dim(total, second * rows, rows, 0)
        sent = lax.dynamic_slice_in_dim(total, (1 - second) * rows, rows, 0)
        total = kept + swap(sent, bit, n_dp)
        bit //= 2
    if groups > 1:
        total = lax.ppermute(
            total, "dp", [(h * GROUP + s, s * groups + h) for h in range(groups) for s in range(GROUP)]
        )
    return total


class SumAll:
    def __init__(self, values, n_dp, n_t):
        self.values, self.n_dp, self.n_t = values, n_dp, n_t
        self.bits = [("dp", 1 << i) for i in range(n_dp.bit_length() - 1)]
        self.bits += [("tensor", 1 << i) for i in range(n_t.bit_length() - 1)]
        self.got = None

    def step(self, token):
        if self.got is not None:
            self.values = self.values + after(self.got, token)
            self.got = None
        if self.bits:
            axis, bit = self.bits.pop(0)
            size = self.n_dp if axis == "dp" else self.n_t
            self.got = lax.ppermute(after(self.values, token), axis, [(i, i ^ bit) for i in range(size)])

    def result(self, token):
        while self.got is not None:
            self.step(token)
        return self.values


def shards(tokens, type_table, norm_gain, norm_bias, w_qkv, w_out, w_up, w_down, cotangent, positions, n_dp, n_t):
    total_rows, width = tokens.shape
    pair_count, slots = positions.shape
    assert pair_count == n_t
    length = total_rows // pair_count
    layers = w_qkv.shape[0]
    top = layers - 1
    inner = w_qkv.shape[3]
    me, quarter = lax.axis_index("dp"), lax.axis_index("tensor")
    rows = width // GROUP
    unit = width // n_dp
    spot = me % GROUP
    spots = jnp.reshape(spot, (1,)).astype(jnp.int32)

    def part_of(block):
        return lax.dynamic_slice_in_dim(block, spot * rows, rows, 0)

    mine = lax.dynamic_slice_in_dim(tokens, quarter * length, length, 0).astype(F32)
    row_ids = lax.broadcasted_iota(jnp.int32, (length, 1), 0)
    stream = mine + jnp.where(row_ids < WORDS, type_table[0], type_table[1])
    gains = [[norm_gain[l, i][None] for i in range(2)] for l in range(layers)]
    biases = [[norm_bias[l, i][None] for i in range(2)] for l in range(layers)]
    own_attn = (w_qkv.transpose(0, 2, 1, 3), w_out)
    own_mlp = (w_up, w_down)

    def attn_part(l):
        left = lax.dynamic_slice(w_qkv, (l, spot * rows, 0, 0), (1, rows, 3, inner)).reshape(rows, 3 * inner)
        right = lax.dynamic_slice(w_out, (l, 0, spot * rows), (1, inner, rows))[0].T
        return jnp.concatenate([left, right], 1)

    def mlp_part(l):
        return jnp.concatenate(
            [lax.dynamic_slice(w, (l, spot * rows, 0), (1, rows, w.shape[2]))[0] for w in (w_up, w_down)], 0
        )

    assert layers == 2
    near, far = 1, n_t - 1

    def hand_on(part, step):
        return lax.ppermute(part, "tensor", [(i, (i + step) % n_t) for i in range(n_t)])

    def to_neighbours(part):
        held = [None] * n_t
        held[near], held[far] = hand_on(part, 1), hand_on(part, -1)
        return held

    def passed_on(held):
        for k in range(2, far):
            held[k] = hand_on(held[k - 1], 1)
        return held[1:]

    def slices_of(matrices):
        return Pieces([[[(v, lead + (k,), 0) for v, lead in slices] for k in range(n_t - 1)] for slices in matrices])

    def core_swap(v):
        return swap(v, 1, n_dp)

    def one_matrix(own, x_piece, y_piece, way):
        own_c, x_c, y_c = core_swap(own), core_swap(x_piece), core_swap(y_piece)
        last = corner(x_piece, y_piece, n_dp, way)
        all_of = [own, own_c, x_piece, x_c, y_piece, y_c, last, core_swap(last)]
        return slices_of([[(v, (0,)) for v in all_of]])

    def two_matrices(own, x_piece, y_piece, token):
        own_c, x_c, y_c = core_swap(own), core_swap(x_piece), core_swap(y_piece)
        first, second = swap(after(x_piece, token)[0], 4, n_dp), swap(after(y_piece, token)[1], 2, n_dp)
        sides = [own, own_c, x_piece, x_c, y_piece, y_c]
        ends = [(first, core_swap(first)), (second, core_swap(second))]
        return slices_of(
            [[(v, (m,)) for v in sides] + [(v, ()) for v in ends[m]] for m in range(2)]
        )

    def sides_of(own):
        return swap(own, 2, n_dp), swap(own, 4, n_dp)

    def run_attention(l, x, pieces, work):
        return attention_forward(spots, x, gains[l][0], biases[l][0], l, own_attn, pieces, n_t, work)

    def run_feed_forward(l, x, pieces, keep, out_type):
        return mlp_forward(spots, x, gains[l][1], biases[l][1], l, own_mlp, pieces, n_t, keep, out_type)

    part_a, part_m = attn_part(0), mlp_part(0)
    part_l = jnp.concatenate([attn_part(1), mlp_part(1)], 0)
    held_a = to_neighbours(part_a)
    held_m = to_neighbours(after(part_m, (held_a[near], held_a[far])))
    hops_a = passed_on(held_a)
    hops_a[0] = after(hops_a[0], part_m)
    (own_a,) = pack(hops_a, 1)
    x_a, y_a = sides_of(own_a)
    held_m[near], held_m[far] = after((held_m[near], held_m[far]), (x_a, y_a))
    attn_pieces = [one_matrix(own_a, *after((x_a, y_a), held_m[near], held_m[far]), False)]
    held_l = to_neighbours(after(part_l, held_m[near], held_m[far]))
    hops_m = passed_on(held_m)
    hops_m[0] = after(hops_m[0], part_l)
    (own_m,) = pack(hops_m, 2)
    x_m, y_m = sides_of(own_m)
    first = run_attention(0, after(stream, own_m), attn_pieces[0], 40_000_000_000)
    first, ((held_l[near], held_l[far]),) = gate(first, (held_l[near], held_l[far]))
    x_m, y_m = after((x_m, y_m), first[0])
    mlp_pieces = [two_matrices(own_m, x_m, y_m, first[0])]
    hops_l = passed_on(held_l)
    own_a, own_m = pack(hops_l, 1, 2)
    x_a, y_a = sides_of(own_a)
    x_m, y_m = sides_of(own_m)
    second = run_feed_forward(0, after(first[0], own_a), mlp_pieces[0], True, F32)
    second, ((x_a, y_a),) = gate(second, (x_a, y_a))
    attn_pieces.append(one_matrix(own_a, x_a, y_a, True))
    third = run_attention(1, second[0], attn_pieces[1], 1_000_000)
    if SIDES_FIRST:
        x_m, y_m = after((x_m, y_m), third[0])
        third, ((x_m, y_m),) = gate(third, (x_m, y_m))
    mlp_pieces.append(two_matrices(own_m, x_m, y_m, third[0]))
    saved = [(stream, *first[1:], first[0], *second[1:]), (second[0], *third[1:], third[0])]

    def put_pairs(held):
        out = jnp.zeros((total_rows, width), F32)
        for k, v in enumerate(held):
            out = lax.dynamic_update_slice(out, v.astype(F32), (((quarter - k) % n_t) * length, 0))
        return out

    place = lax.dynamic_slice_in_dim(positions, quarter, 1, 0)[0]
    cot = lax.dynamic_slice_in_dim(cotangent, quarter, 1, 0)[0]
    onehot = (row_ids[:TOP_ROWS] == place[None, :]).astype(BF16)
    incoming = nn(onehot, cot)

    everything = tuple(range(n_t))
    halves = (everything[: n_t // 2], everything[n_t // 2 :])
    gain_grads = [[None, None] for _ in range(layers)]
    bias_grads = [[None, None] for _ in range(layers)]
    def reductions_of(keep, got, quarters):
        out = []
        for i, half in enumerate(halves):
            chosen = [k for k in half if k in quarters]
            if chosen:
                out.append(Reduction(keep, got, chosen[0] - quarters[0], chosen, i == 0, n_dp, n_t))
        return out

    stream_l, normed, proj, logsum, mixed, middle = saved[top]
    grad_middle, gain_grads[top][1], bias_grads[top][1], top_normed = top_backward(
        spots, incoming, middle, gains[top][1], biases[top][1], top, own_mlp, mlp_pieces[top], n_t
    )
    slot_rows = tn(onehot, top_normed).astype(BF16)
    slot_cot = jnp.where(place[:, None] >= 0, cot, 0)
    spare = jnp.zeros((SLOT_ROWS - slots, width), BF16)
    all_rows = lax.all_gather(jnp.concatenate([slot_cot, spare, slot_rows, spare], 0), ("dp", "tensor"))
    total, incoming, gain_grads[top][0], bias_grads[top][0], keep, send = attention_backward(
        spots, grad_middle, stream_l, gains[top][0], normed, proj, logsum, mixed, None,
        top, own_attn, attn_pieces[top], everything,
    )
    got = swap(send, 1, n_dp)
    (last_stream,) = run_feed_forward(top, after(middle, total), mlp_pieces[top], False, BF16)
    last_stream, (got,) = gate(last_stream, got)
    attn_top = reductions_of(keep, got, everything)
    ready = [r.near_sum(last_stream) for r in attn_top]
    hidden_held = to_neighbours(after(last_stream, ready))
    hidden_held[0] = last_stream

    stream_l, normed, proj, logsum, mixed, middle, normed_mlp, upward = saved[0]
    outs = mlp_backward(
        spots, after(incoming, ready), middle, gains[0][1], normed_mlp, upward, None,
        0, own_mlp, mlp_pieces[0], everything, True,
    )
    near_of = [r.from_near for r in attn_top]
    outs, (near_of, hidden_held) = gate(outs, near_of, hidden_held)
    for r, v in zip(attn_top, near_of):
        r.from_near = v
    incoming, gain_grads[0][1], bias_grads[0][1], keep, send = outs[1:]
    got = swap(send, 1, n_dp)
    hidden_held[1:] = passed_on(hidden_held)
    ready = [r.far_sum(incoming) for r in attn_top]

    outs = attention_backward(
        spots, after(incoming, ready), stream_l, gains[0][0], normed, proj, logsum, mixed, None,
        0, own_attn, attn_pieces[0], halves[0],
    )
    outs, (got, far_of, hidden_held) = gate(outs, got, [r.from_far for r in attn_top], hidden_held)
    for r, v in zip(attn_top, far_of):
        r.from_far = v
    total, keep_a, send_a = outs
    got_a = swap(send_a, 1, n_dp)
    mlp_low = reductions_of(keep, got, everything)
    ready = [r.near_sum(total) for r in mlp_low]
    ready += [r.own_sum(ready) for r in attn_top]

    outs = attention_backward(
        spots, after(incoming, ready), stream_l, gains[0][0], normed, proj, logsum, mixed, total,
        0, own_attn, attn_pieces[0], halves[1],
    )
    outs, (got_a,) = gate(outs, got_a)
    incoming, gain_grads[0][0], bias_grads[0][0], keep_b, send_b = outs[1:]
    (low_a,) = reductions_of(keep_a, got_a, halves[0])
    (low_b,) = reductions_of(keep_b, swap(send_b, 1, n_dp), halves[1])
    ready = low_a.near_sum(incoming)
    grad_tokens = lax.all_gather(incoming.astype(BF16), "tensor", tiled=True)

    all_rows = after(all_rows, ready)
    all_cot = all_rows[:, :SLOT_ROWS].reshape(-1, width)
    all_normed = all_rows[:, SLOT_ROWS:].reshape(-1, width)
    slot_up = nn(all_normed, w_up[top])
    slot_grad = (nt(all_cot, w_down[top]) * gelu_slope(slot_up)).astype(BF16)
    grad_up_top = tn(lax.dynamic_slice_in_dim(all_normed, me * unit, unit, 1), slot_grad)
    grad_down_top = tn(
        gelu(slot_up).astype(BF16), lax.dynamic_slice_in_dim(all_cot, me * unit, unit, 1)
    )

    ready = low_b.near_sum(ready)
    type_grad = jnp.stack([jnp.sum(incoming[:WORDS], 0), jnp.sum(incoming[WORDS:], 0)])
    rows_all = SumAll(
        jnp.concatenate(
            [type_grad] + [g for pair in gain_grads for g in pair] + [b for pair in bias_grads for b in pair], 0
        ),
        n_dp,
        n_t,
    )
    rows_all.step(ready)
    hidden_out = put_pairs(after(hidden_held, ready))
    ready = (hidden_out, grad_up_top, grad_down_top)
    for r in mlp_low:
        ready = r.far_sum(ready)
    rows_all.step(ready)
    sums = {}

    def finished(reductions, token):
        return finish(after([p for r in reductions for p in r.parts], token), n_dp)

    (sums["attn", top],) = finished(attn_top, ready)
    for r in (low_a, low_b):
        ready = r.far_sum(ready)
        rows_all.step(ready)
    for r in (*mlp_low, low_a, low_b):
        ready = r.own_sum(ready)
        rows_all.step(ready)
    rows_all = rows_all.result(ready)
    grad_tokens = after(grad_tokens, ready).astype(F32)
    sums["down", 0], sums["up", 0] = finished(mlp_low, ready)
    (sums["attn", 0],) = finished([low_a, low_b], (ready, grad_tokens, sums["down", 0], sums["up", 0]))

    rows_mine = lax.dynamic_slice_in_dim(rows_all, me * unit, unit, 1)
    grad_gain = rows_mine[2 : 2 + 2 * layers].reshape(layers, 2, unit)
    grad_bias = rows_mine[2 + 2 * layers :].reshape(layers, 2, unit)
    grad_qkv = jnp.stack([sums["attn", l][:, : 3 * inner].reshape(unit, 3, inner) for l in range(layers)])
    grad_out = jnp.stack([sums["attn", l][:, 3 * inner :].T for l in range(layers)])
    grad_up = jnp.stack([grad_up_top if l == top else sums["up", l] for l in range(layers)])
    grad_down = jnp.stack([grad_down_top if l == top else sums["down", l].T for l in range(layers)])
    return hidden_out, grad_tokens, rows_mine[:2], grad_gain, grad_bias, grad_qkv, grad_out, grad_up, grad_down


def solution(mesh):
    n_dp, n_t = mesh.shape["dp"], mesh.shape["tensor"]
    placed = (
        P("dp", None),
        P(),
        P(),
        P(),
        P(None, None, None, "tensor"),
        P(None, "tensor", None),
        P(None, None, "tensor"),
        P(None, "tensor", None),
        P("dp", None, None),
        P("dp", None),
    )

    def run(*args):
        return shards(*args, n_dp, n_t)

    return jax.shard_map(
        run,
        mesh=mesh,
        in_specs=placed,
        out_specs=(
            P("dp", None),
            P("dp", None),
            P(None, "dp"),
            P(None, None, "dp"),
            P(None, None, "dp"),
            P(None, "dp", None, "tensor"),
            P(None, "tensor", "dp"),
            P(None, "dp", "tensor"),
            P(None, "tensor", "dp"),
        ),
        check_vma=False,
    )
```

```python
import functools

import jax
import jax.numpy as jnp
from jax import lax
from jax.experimental import pallas as pl
from jax.experimental.pallas import tpu as pltpu
from jax.sharding import PartitionSpec as P

HD = 64
WORDS = 40
TOP_ROWS = 48
SLOT_ROWS = 16
EPSILON = 1e-06
ROOT_HALF = 0.7071067811865476
ROOT_TWO_PI = 2.5066282746310002
GROUP = 8
STEP = 32
SIDES_FIRST = True
F32 = jnp.float32
BF16 = jnp.bfloat16
SMALL_VMEM = 16 * 1024 * 1024
VMEM_BYTES = 60 * 1024 * 1024


def dot(left, right, dims):
    return lax.dot_general(left, right, (dims, ((), ())), preferred_element_type=F32)


def nn(left, right):
    return dot(left, right, ((1,), (0,)))


def nt(left, right):
    return dot(left, right, ((1,), (1,)))


def tn(left, right):
    return dot(left, right, ((0,), (0,)))


def gelu(values):
    return 0.5 * values * (1.0 + lax.erf(values * ROOT_HALF))


def gelu_slope(values):
    return 0.5 * (1.0 + lax.erf(values * ROOT_HALF)) + values * jnp.exp(-0.5 * values * values) / ROOT_TWO_PI


def norm_parts(values):
    average = jnp.mean(values, axis=-1, keepdims=True)
    centred = values - average
    spread = jnp.mean(centred * centred, axis=-1, keepdims=True)
    rate = lax.rsqrt(spread + EPSILON)
    return centred * rate, rate


def norm_rows(source, gain, bias, target):
    step = STEP if source.shape[0] % STEP == 0 else STEP // 2
    for r in range(0, source.shape[0], step):
        rows = slice(r, r + step)
        target[rows, :] = (norm_parts(source[rows, :])[0] * gain[...] + bias[...]).astype(BF16)


def norm_back_rows(rows, values, gain, incoming, gain_grad, bias_grad):
    unit, rate = norm_parts(values[rows, :])
    e = incoming[rows, :]
    scaled = e * gain[...]
    inner = jnp.mean(scaled * unit, axis=-1, keepdims=True)
    gain_grad[...] += jnp.sum(e * unit, axis=0, keepdims=True)
    bias_grad[...] += jnp.sum(e, axis=0, keepdims=True)
    return rate * (scaled - jnp.mean(scaled, axis=-1, keepdims=True) - unit * inner)


def flops(count):
    return pl.CostEstimate(flops=count, bytes_accessed=1_000_000, transcendentals=0)


KERNEL_COST = pl.CostEstimate(flops=40_000_000_000, bytes_accessed=1_000_000, transcendentals=0)
SMALL_COST = pl.CostEstimate(flops=1_000_000_000, bytes_accessed=1_000_000, transcendentals=0)


class Pieces:
    def __init__(self, at):
        self.arrays = []
        self.plan = []
        for matrix in at:
            for k, slices in enumerate(matrix, 1):
                for s, (array, lead, row) in enumerate(slices):
                    found = [i for i, v in enumerate(self.arrays) if v is array]
                    if not found:
                        self.arrays.append(array)
                        found = [len(self.arrays) - 1]
                    self.plan.append((len(self.plan) // (len(matrix) * GROUP), k, s, found[0], lead, row))


def fetch(spot, layer, own, plan, sources, scratches, sems, quarters):
    rows = scratches[0].shape[1] // GROUP
    for k in quarters:
        for m, scratch in enumerate(scratches):
            if k == 0 and own:
                pltpu.make_async_copy(own[m].at[layer], scratch.at[0], sems.at[0]).start()
        for m, at_k, s, which, lead, row in plan:
            if at_k == k:
                source = sources[which].at[lead]
                at = pl.multiple_of((spot ^ s) * rows, rows)
                pltpu.make_async_copy(
                    source.at[pl.ds(row, rows)],
                    scratches[m].at[k - quarters[0], pl.ds(at, rows)],
                    sems.at[k - quarters[0]],
                ).start()


def arrived(k, scratches, sems):
    for scratch in scratches:
        pltpu.make_async_copy(scratch.at[k], scratch.at[k], sems.at[k]).wait()


def own_copies(layer, own_qkv, own_out, raw_qkv, raw_out, sem):
    return [
        pltpu.make_async_copy(own_qkv.at[layer], raw_qkv, sem),
        pltpu.make_async_copy(own_out.at[layer], raw_out, sem),
    ]


def own_block(copies, raw_qkv, raw_out, block):
    for copy in copies:
        copy.wait()
    inner = raw_qkv.shape[2]
    for c in range(3):
        block[0, :, c * inner : (c + 1) * inner] = raw_qkv[c]
    block[0, :, 3 * inner :] = raw_out[...].astype(F32).T.astype(BF16)


def flip(spot, source, target):
    width = source.shape[1]
    rows = width // GROUP
    turned = source.astype(F32).T.astype(BF16)
    for j in range(GROUP):
        s = spot ^ j
        at = pl.multiple_of(((s & 1) * (GROUP // 2) + (s >> 1)) * rows, rows)
        target[pl.ds(at, rows), :] = turned[j * rows : (j + 1) * rows, :]


def put_block(block, keep, send, part, columns=slice(None)):
    half = block.shape[0] // 2
    rows = half // (GROUP // 2)
    for i in range(GROUP // 2):
        keep[i][0, part, :, columns] = block[i * rows : (i + 1) * rows].astype(BF16)
        send[i, 0, part, :, columns] = block[half + i * rows : half + (i + 1) * rows].astype(BF16)


def any_spec():
    return pl.BlockSpec(memory_space=pl.ANY)


def smem_spec():
    return pl.BlockSpec(memory_space=pltpu.SMEM)


def whole(shape):
    return pl.BlockSpec(shape, lambda k: (0,) * len(shape))


def per_quarter(shape, first=0):
    return pl.BlockSpec((1,) + shape, lambda k: (first + k,) + (0,) * len(shape))


def block_specs(matrices, rows, width):
    own = pl.BlockSpec((1, matrices, rows, width), lambda k: (k, 0, 0, 0))
    return [own] * (GROUP // 2) + [
        pl.BlockSpec((GROUP // 2, 1, matrices, rows, width), lambda k: (0, k, 0, 0, 0))
    ]


def block_shapes(quarters, matrices, rows, width):
    own = jax.ShapeDtypeStruct((quarters, matrices, rows, width), BF16)
    return [own] * (GROUP // 2) + [jax.ShapeDtypeStruct((GROUP // 2, quarters, matrices, rows, width), BF16)]


def params(limit=VMEM_BYTES):
    return pltpu.CompilerParams(vmem_limit_bytes=limit)


def cost(flops, moved):
    return pl.CostEstimate(flops=flops, bytes_accessed=moved, transcendentals=0)


def attention_forward_kernel(layer, plan, count, spot_ref, x, gain, bias, own_qkv, own_out, *rest):
    middle, normed, proj, logsum, mixed, block, sems, raw_qkv, raw_out = rest[count:]
    k = pl.program_id(0)
    inner = raw_out.shape[0]
    heads = inner // HD

    @pl.when(k == 0)
    def _():
        copies = own_copies(layer, own_qkv, own_out, raw_qkv, raw_out, sems.at[0])
        for copy in copies:
            copy.start()
        fetch(spot_ref[0], layer, [], plan, rest[:count], [block], sems, range(block.shape[0]))
        norm_rows(x, gain, bias, normed)
        middle[...] = x[...]
        logsum[...] = jnp.zeros_like(logsum)
        own_block(copies, raw_qkv, raw_out, block)

    @pl.when(k > 0)
    def _():
        arrived(k, [block], sems)

    proj[0] = nn(normed[...], block[k])[:, : 3 * inner].astype(BF16)
    lane = lax.broadcasted_iota(jnp.int32, logsum.shape, 1)
    every = range(heads)
    lanes = [slice(h * HD, (h + 1) * HD) for h in range(3 * heads)]
    scores = [
        nt(proj[0, :, lanes[h]] * jnp.asarray(HD**-0.5, BF16), proj[0, :, lanes[heads + h]]) for h in every
    ]
    tops = [jnp.max(v, axis=-1, keepdims=True) for v in scores]
    powers = [jnp.exp(v - t) for v, t in zip(scores, tops)]
    totals = [jnp.sum(v, axis=-1, keepdims=True) for v in powers]
    kept = logsum[...]
    for h in every:
        kept = jnp.where(lane == k * heads + h, tops[h] + jnp.log(totals[h]), kept)
    logsum[...] = kept
    weights = [(v * (1.0 / t)).astype(BF16) for v, t in zip(powers, totals)]
    mixes = [nn(weights[h], proj[0, :, lanes[2 * heads + h]]).astype(BF16) for h in every]
    pad = mixed.shape[2] - inner
    mixed[0] = jnp.concatenate([jnp.zeros((normed.shape[0], pad), BF16)] + mixes, 1)
    middle[...] += nt(mixed[0], block[k, :, 3 * inner - pad :]).astype(BF16).astype(F32)


def attention_forward(spot, x, gain, bias, layer, own, pieces, n_t, work):
    length, width = x.shape
    inner = own[1].shape[1]
    count = len(pieces.arrays)
    out = [
        jax.ShapeDtypeStruct((length, width), F32),
        jax.ShapeDtypeStruct((length, width), BF16),
        jax.ShapeDtypeStruct((n_t, length, 3 * inner), BF16),
        jax.ShapeDtypeStruct((length, 128), F32),
        jax.ShapeDtypeStruct((n_t, length, inner + inner % 128), BF16),
    ]
    return pl.pallas_call(
        functools.partial(attention_forward_kernel, layer, pieces.plan, count),
        grid=(n_t,),
        out_shape=out,
        in_specs=[smem_spec(), whole((length, width)), whole((1, width)), whole((1, width))] + [any_spec()] * (2 + count),
        out_specs=[
            whole((length, width)),
            whole((length, width)),
            per_quarter((length, 3 * inner)),
            whole((length, 128)),
            per_quarter((length, inner + inner % 128)),
        ],
        scratch_shapes=[
            pltpu.VMEM((n_t, width, 4 * inner), BF16),
            pltpu.SemaphoreType.DMA((n_t,)),
            pltpu.VMEM((3, width, inner), BF16),
            pltpu.VMEM((inner, width), BF16),
        ],
        compiler_params=params(),
        cost_estimate=flops(work),
        name="attention_forward",
    )(spot, x, gain, bias, *own, *pieces.arrays)


def mlp_forward_kernel(kept_rows, layer, plan, count, spot_ref, x, gain, bias, own_up, own_down, *rest):
    if kept_rows:
        out, normed, upward, ups, downs, total, sems = rest[count:]
    else:
        out, ups, downs, total, sems, normed = rest[count:]
    k = pl.program_id(0)

    @pl.when(k == 0)
    def _():
        fetch(spot_ref[0], layer, [own_up, own_down], plan, rest[:count], [ups, downs], sems, range(ups.shape[0]))
        norm_rows(x, gain, bias, normed)
        total[...] = x[...]

    arrived(k, [ups, downs], sems)
    up = nn(normed[...], ups[k])
    if kept_rows:
        upward[0] = up
    active = gelu(up).astype(BF16)
    total[...] += nn(active, downs[k]).astype(BF16).astype(F32)

    @pl.when(k == pl.num_programs(0) - 1)
    def _():
        out[...] = total[...].astype(out.dtype)


def mlp_forward(spot, x, gain, bias, layer, own, pieces, n_t, kept_rows, out_type):
    length, width = x.shape
    hidden = own[0].shape[2]
    count = len(pieces.arrays)
    out = [jax.ShapeDtypeStruct((length, width), out_type)]
    out_specs = [whole((length, width))]
    scratch = []
    if kept_rows:
        out += [jax.ShapeDtypeStruct((length, width), BF16), jax.ShapeDtypeStruct((n_t, length, hidden), F32)]
        out_specs += [whole((length, width)), per_quarter((length, hidden))]
    else:
        scratch.append(pltpu.VMEM((length, width), BF16))
    return pl.pallas_call(
        functools.partial(mlp_forward_kernel, kept_rows, layer, pieces.plan, count),
        grid=(n_t,),
        out_shape=out,
        in_specs=[smem_spec(), whole((length, width)), whole((1, width)), whole((1, width))]
        + [any_spec()] * (2 + count),
        out_specs=out_specs,
        scratch_shapes=[
            pltpu.VMEM((n_t,) + own[0].shape[1:], BF16),
            pltpu.VMEM((n_t,) + own[1].shape[1:], BF16),
            pltpu.VMEM((length, width), F32),
            pltpu.SemaphoreType.DMA((n_t,)),
        ]
        + scratch,
        compiler_params=params(),
        cost_estimate=KERNEL_COST,
        name="mlp_forward",
    )(spot, x, gain, bias, *own, *pieces.arrays)


def mlp_backward_kernel(quarters, last, blocks, layer, plan, count, spot_ref, incoming, x, gain, normed, upward, total_in, *rest):
    own, sources = rest[:2], rest[2 : 2 + count]
    rest = list(rest[2 + count :])
    total = rest.pop(0)
    if last:
        grad, gain_grad, bias_grad = (rest.pop(0) for _ in range(3))
    if blocks:
        keep, send = [rest.pop(0) for _ in range(GROUP // 2)], rest.pop(0)
    ups, downs, sems, *flipped = rest
    k = pl.program_id(0)

    @pl.when(k == 0)
    def _():
        fetch(spot_ref[0], layer, own, plan, sources, [ups, downs], sems, quarters)
        total[...] = jnp.zeros_like(total) if quarters[0] == 0 else total_in[...]
        if blocks:
            flip(spot_ref[0], incoming[...], flipped[0])
            flip(spot_ref[0], normed[...], flipped[1])

    arrived(k, [ups, downs], sems)
    up = upward[0]
    grad_active = nt(incoming[...].astype(BF16), downs[k])
    bell = 0.5 * (1.0 + lax.erf(up * ROOT_HALF))
    grad_up = (grad_active * (bell + up * jnp.exp(-0.5 * up * up) * (1.0 / ROOT_TWO_PI))).astype(BF16)
    total[...] += nt(grad_up, ups[k])
    if blocks:
        put_block(nn(flipped[0][...], (up * bell).astype(BF16)), keep, send, 0)
        put_block(nn(flipped[1][...], grad_up), keep, send, 1)

    if last:

        @pl.when(k == pl.num_programs(0) - 1)
        def _():
            gain_grad[...] = jnp.zeros_like(gain_grad)
            bias_grad[...] = jnp.zeros_like(bias_grad)
            for r in range(0, x.shape[0], 16):
                rows = slice(r, r + 16)
                grad[rows, :] = incoming[rows, :] + norm_back_rows(rows, x, gain, total, gain_grad, bias_grad)


def mlp_backward(spot, incoming, x, gain, normed, upward, total, layer, own, pieces, quarters, blocks):
    length, width = incoming.shape
    n_t, hidden = upward.shape[0], upward.shape[2]
    last = quarters[-1] == n_t - 1
    count = len(quarters)
    if total is None:
        total = gain
    out = [jax.ShapeDtypeStruct((length, width), F32)]
    out_specs = [whole((length, width))]
    if last:
        out += [jax.ShapeDtypeStruct(v, F32) for v in ((length, width), (1, width), (1, width))]
        out_specs += [whole((length, width)), whole((1, width)), whole((1, width))]
    scratch = [
        pltpu.VMEM((count,) + own[0].shape[1:], BF16),
        pltpu.VMEM((count,) + own[1].shape[1:], BF16),
        pltpu.SemaphoreType.DMA((count,)),
    ]
    if blocks:
        out += block_shapes(count, 2, width // GROUP, hidden)
        out_specs += block_specs(2, width // GROUP, hidden)
        scratch += [pltpu.VMEM((width, length), BF16)] * 2
    return pl.pallas_call(
        functools.partial(mlp_backward_kernel, quarters, last, blocks, layer, pieces.plan, len(pieces.arrays)),
        grid=(count,),
        out_shape=out,
        in_specs=[
            smem_spec(),
            whole((length, width)),
            whole((length, width)),
            whole((1, width)),
            whole((length, width)),
            per_quarter((length, hidden), quarters[0]),
            whole(total.shape),
        ]
        + [any_spec()] * (2 + len(pieces.arrays)),
        out_specs=out_specs,
        scratch_shapes=scratch,
        compiler_params=params(),
        cost_estimate=KERNEL_COST,
        name="mlp_backward",
    )(spot, incoming, x, gain, normed, upward, total, *own, *pieces.arrays)


def top_kernel(layer, plan, count, spot_ref, incoming, x, gain, bias, pick, slots, own_up, own_down, *rest):
    grad, gain_grad, bias_grad, packed, ups, downs, total, sems, normed = rest[count:]
    k = pl.program_id(0)

    @pl.when(k == 0)
    def _():
        fetch(spot_ref[0], layer, [own_up, own_down], plan, rest[:count], [ups, downs], sems, range(ups.shape[0]))
        norm_rows(x, gain, bias, normed)
        total[...] = jnp.zeros_like(total)
        packed[:SLOT_ROWS, :] = slots[...]
        packed[SLOT_ROWS:, :] = nn(pick[...], normed[...]).astype(BF16)

    arrived(k, [ups, downs], sems)
    up = nn(normed[...], ups[k])
    grad_up = (nt(incoming[...].astype(BF16), downs[k]) * gelu_slope(up)).astype(BF16)
    total[...] += nt(grad_up, ups[k])

    @pl.when(k == pl.num_programs(0) - 1)
    def _():
        gain_grad[...] = jnp.zeros_like(gain_grad)
        bias_grad[...] = jnp.zeros_like(bias_grad)
        for r in range(0, incoming.shape[0], 16):
            rows = slice(r, r + 16)
            grad[rows, :] = incoming[rows, :] + norm_back_rows(rows, x, gain, total, gain_grad, bias_grad)


def top_backward(spot, incoming, x, gain, bias, pick, slots, layer, own, pieces, n_t):
    length, width = incoming.shape
    rows = pl.BlockSpec((length, width), lambda k: (0, 0))
    row = whole((1, width))
    return pl.pallas_call(
        functools.partial(top_kernel, layer, pieces.plan, len(pieces.arrays)),
        grid=(n_t,),
        out_shape=[
            jax.ShapeDtypeStruct((length, width), F32),
            jax.ShapeDtypeStruct((1, width), F32),
            jax.ShapeDtypeStruct((1, width), F32),
            jax.ShapeDtypeStruct((2 * SLOT_ROWS, width), BF16),
        ],
        in_specs=[smem_spec(), rows, rows, row, row, whole(pick.shape), whole(slots.shape)] + [any_spec()] * (2 + len(pieces.arrays)),
        out_specs=[rows, row, row, whole((2 * SLOT_ROWS, width))],
        scratch_shapes=[
            pltpu.VMEM((n_t,) + own[0].shape[1:], BF16),
            pltpu.VMEM((n_t,) + own[1].shape[1:], BF16),
            pltpu.VMEM((length, width), F32),
            pltpu.SemaphoreType.DMA((n_t,)),
            pltpu.VMEM((length, width), BF16),
        ],
        compiler_params=params(),
        cost_estimate=KERNEL_COST,
        name="top_backward",
    )(spot, incoming, x, gain, bias, pick, slots, *own, *pieces.arrays)


def attention_backward_kernel(
    quarters, last, layer, plan, count, spot_ref, incoming, x, gain, normed, proj, logsum, mixed, total_in, own_qkv, own_out, *rest
):
    sources = rest[:count]
    rest = list(rest[count:])
    total = rest.pop(0)
    if last:
        grad, gain_grad, bias_grad, types = (rest.pop(0) for _ in range(4))
    keep = [rest.pop(0) for _ in range(GROUP // 2)]
    send, block, grad_proj, sems, low_t, normed_t, raw_qkv, raw_out = rest
    k = pl.program_id(0)
    top = incoming.shape[0]
    inner = raw_out.shape[0]
    heads = inner // HD

    @pl.when(k == 0)
    def _():
        if quarters[0] == 0:
            copies = own_copies(layer, own_qkv, own_out, raw_qkv, raw_out, sems.at[0])
            for copy in copies:
                copy.start()
        fetch(spot_ref[0], layer, [], plan, sources, [block], sems, quarters)
        total[...] = jnp.zeros_like(total) if quarters[0] == 0 else total_in[...]
        grad_proj[...] = jnp.zeros_like(grad_proj)
        flip(spot_ref[0], incoming[...], low_t)
        flip(spot_ref[0], normed[...], normed_t)
        if quarters[0] == 0:
            own_block(copies, raw_qkv, raw_out, block)

    @pl.when(quarters[0] + k > 0)
    def _():
        arrived(k, [block], sems)

    pad = mixed.shape[2] - inner
    grad_mixed = nn(incoming[...].astype(BF16), block[k, :, 3 * inner - pad :]).astype(BF16)
    lane = lax.broadcasted_iota(jnp.int32, (top, 128), 1)
    every = range(heads)
    lanes = [slice(h * HD, (h + 1) * HD) for h in range(3 * heads)]
    queries = [proj[0, :top, lanes[h]] * jnp.asarray(HD**-0.5, BF16) for h in every]
    keys = [proj[0, :, lanes[heads + h]] for h in every]
    head_grads = [grad_mixed[:, pad + h * HD : pad + (h + 1) * HD] for h in every]
    scores = [nt(queries[h], keys[h]) for h in every]
    grad_weights = [nt(head_grads[h], proj[0, :, lanes[2 * heads + h]]) for h in every]
    row_sums = [
        jnp.sum(
            jnp.where(lane == (quarters[0] + k) * heads + h, logsum[:top, :], 0.0), axis=-1, keepdims=True
        )
        for h in every
    ]
    weights = [jnp.exp(scores[h] - row_sums[h]) for h in every]
    for h in every:
        grad_proj[:, lanes[2 * heads + h]] = tn(weights[h].astype(BF16), head_grads[h]).astype(BF16)
    inner_sums = [jnp.sum(weights[h] * grad_weights[h], axis=-1, keepdims=True) for h in every]
    grad_scores = [(weights[h] * (grad_weights[h] - inner_sums[h])).astype(BF16) for h in every]
    for h in every:
        grad_proj[:top, lanes[h]] = (nn(grad_scores[h], keys[h]) * HD**-0.5).astype(BF16)
        grad_proj[:, lanes[heads + h]] = tn(grad_scores[h], queries[h]).astype(BF16)
    wide = grad_proj.shape[1]
    total[...] += nt(grad_proj[...], block[k, :, :wide])
    left = nn(normed_t[...], grad_proj[...])
    right = nn(low_t[...], mixed[0, :top, :])
    at = 3 * inner - pad
    put_block(left[:, :at], keep, send, 0, slice(0, at))
    put_block(left[:, at:] + right[:, : wide - at], keep, send, 0, slice(at, wide))
    put_block(right[:, wide - at :], keep, send, 0, slice(wide, 4 * inner))

    if last:

        @pl.when(k == pl.num_programs(0) - 1)
        def _():
            gain_grad[...] = jnp.zeros_like(gain_grad)
            bias_grad[...] = jnp.zeros_like(bias_grad)
            types[...] = jnp.zeros_like(types)
            step = 8
            for r in range(0, x.shape[0], step):
                rows = slice(r, r + step)
                back = norm_back_rows(rows, x, gain, total, gain_grad, bias_grad)
                if r < top:
                    back = back + incoming[rows, :]
                grad[rows, :] = back.astype(grad.dtype)
                which = slice(0, 1) if r < WORDS else slice(1, 2)
                types[which, :] += jnp.sum(back, axis=0, keepdims=True)


def attention_backward(
    spot, incoming, x, gain, normed, proj, logsum, mixed, total, layer, own, pieces, quarters, out_type=F32
):
    length, width = x.shape
    top = incoming.shape[0]
    n_t = proj.shape[0]
    last = quarters[-1] == n_t - 1
    count = len(quarters)
    inner = own[1].shape[1]
    if total is None:
        total = gain
    out = [jax.ShapeDtypeStruct((length, width), F32)]
    out_specs = [whole((length, width))]
    if last:
        out.append(jax.ShapeDtypeStruct((length, width), out_type))
        out += [jax.ShapeDtypeStruct(v, F32) for v in ((1, width), (1, width), (2, width))]
        out_specs += [whole(v.shape) for v in out[1:]]
    out += block_shapes(count, 1, width // GROUP, 4 * inner)
    out_specs += block_specs(1, width // GROUP, 4 * inner)
    return pl.pallas_call(
        functools.partial(attention_backward_kernel, quarters, last, layer, pieces.plan, len(pieces.arrays)),
        grid=(count,),
        out_shape=out,
        in_specs=[
            smem_spec(),
            whole((top, width)),
            whole((length, width)),
            whole((1, width)),
            whole((length, width)),
            per_quarter((length, 3 * inner), quarters[0]),
            whole((length, 128)),
            per_quarter((length, inner + inner % 128), quarters[0]),
            whole(total.shape),
        ]
        + [any_spec()] * (2 + len(pieces.arrays)),
        out_specs=out_specs,
        scratch_shapes=[
            pltpu.VMEM((count, width, 4 * inner), BF16),
            pltpu.VMEM((length, 3 * inner + (3 * inner) % 128), BF16),
            pltpu.SemaphoreType.DMA((count,)),
            pltpu.VMEM((width, top), BF16),
            pltpu.VMEM((width, length), BF16),
            pltpu.VMEM((3, width, inner), BF16),
            pltpu.VMEM((inner, width), BF16),
        ],
        compiler_params=params(),
        cost_estimate=KERNEL_COST,
        name="attention_backward",
    )(spot, incoming, x, gain, normed, proj, logsum, mixed, total, *own, *pieces.arrays)


def swap(values, bit, size):
    return lax.ppermute(values, "dp", [(i, i ^ bit) for i in range(size)])


def after(values, *others):
    return lax.optimization_barrier((values, others))[0]


def gate(outs, *others):
    return lax.optimization_barrier((outs, others))


def small_call(kernel, grid, in_specs, out_specs, out_shape, name):
    return pl.pallas_call(
        kernel,
        grid=grid,
        in_specs=in_specs,
        out_specs=out_specs,
        out_shape=out_shape,
        compiler_params=params(SMALL_VMEM),
        cost_estimate=SMALL_COST,
        name=name,
    )


def pack_kernel(groups, *refs):
    sources, targets = refs[: -len(groups)], refs[-len(groups) :]
    rows = targets[0].shape[2]
    for k, source in enumerate(sources):
        for target, (first, count) in zip(targets, groups):
            for m in range(count):
                target[m, k] = source[(first + m) * rows : (first + m + 1) * rows, :]


def pack(sources, *counts):
    total, width = sources[0].shape
    rows = total // sum(counts)
    groups = [(sum(counts[:i]), count) for i, count in enumerate(counts)]
    shapes = [(count, len(sources), rows, width) for count in counts]
    return small_call(
        functools.partial(pack_kernel, groups),
        (1,),
        [whole((total, width))] * len(sources),
        [whole(shape) for shape in shapes],
        [jax.ShapeDtypeStruct(shape, BF16) for shape in shapes],
        "pack",
    )(*sources)


def corner(x_piece, y_piece, n_dp, by_x):
    return swap(y_piece, 2, n_dp) if by_x else swap(x_piece, 4, n_dp)


def near_kernel(*refs):
    *operands, x_out, y_out = refs
    for out, four in ((x_out, operands[:4]), (y_out, operands[4:])):
        for i in range(2):
            out[i] = (four[2 * i][...].astype(F32) + four[2 * i + 1][0].astype(F32)).astype(BF16)


def far_kernel(*refs):
    *operands, x_out, y_out = refs
    for out, (kept, got, near) in ((x_out, operands[:3]), (y_out, operands[3:])):
        out[...] = (kept[...].astype(F32) + got[0].astype(F32) + near[0].astype(F32)).astype(BF16)


def own_kernel(*refs):
    operands, outs = refs[:8], refs[8:]
    half = len(outs) // 2
    for i, out in enumerate(outs):
        kept, got, near, far = operands[4 * (i // half) : 4 * (i // half) + 4]
        j = i % half
        total = kept[j].astype(F32) + got[0, j].astype(F32) + near[0, j].astype(F32) + far[j].astype(F32)
        out[0] = total.astype(out.dtype)


def rows_kernel(*refs):
    *sources, target = refs
    target[...] = jnp.zeros_like(target)
    at = 0
    for source in sources:
        count = source.shape[0]
        target[at : at + count, :] = source[...]
        at += count


def stack_rows(sources):
    width = sources[0].shape[1]
    count = -(-sum(v.shape[0] for v in sources) // 8) * 8
    return small_call(
        rows_kernel,
        (1,),
        [whole(v.shape) for v in sources],
        whole((count, width)),
        jax.ShapeDtypeStruct((count, width), F32),
        "stack_rows",
    )(*sources)


def relay_kernel(first, second, out):
    out[...] = (first[...].astype(F32) + second[...].astype(F32)).astype(BF16)


def last_kernel(*refs):
    *parts, out = refs
    total = parts[0][...].astype(F32)
    for part in parts[1:]:
        total = total + part[...].astype(F32)
    out[...] = total


class Reduction:
    def __init__(self, blocks, n_dp, n_t):
        self.keep, self.got = [], []
        self.n_dp, self.n_t = n_dp, n_t
        self.half = n_t // 2
        for keep, send in blocks:
            self.add(keep, send)
        self.shape = self.keep[0][0].shape[1:]
        self.zeros = (0,) * len(self.shape)

    def add(self, keep, send):
        self.keep.append(keep)
        self.got.append(swap(send, 1, self.n_dp))

    def pair(self, plane, half):
        n = len(self.keep)
        at = half // n
        specs = [
            pl.BlockSpec((self.half,) + self.shape, lambda _: (at,) + self.zeros),
            pl.BlockSpec((1, self.half) + self.shape, lambda _: (plane, at) + self.zeros),
        ]
        return list(zip([self.keep[half % n][plane], self.got[half % n]], specs))

    def call(self, kernel, operands, shapes, name):
        return small_call(
            kernel,
            (1,),
            [spec for _, spec in operands],
            [whole(v.shape) for v in shapes],
            shapes,
            name,
        )(*[v for v, _ in operands])

    def near(self):
        shape = jax.ShapeDtypeStruct((2, self.half) + self.shape, BF16)
        x, y = self.call(
            near_kernel,
            self.pair(1, 0) + self.pair(3, 0) + self.pair(2, 1) + self.pair(3, 1),
            [shape, shape],
            "near_sum",
        )
        self.from_near = [swap(x, 2, self.n_dp), swap(y, 4, self.n_dp)]
        return [x, y]

    def came(self, half, i):
        spec = pl.BlockSpec((1, self.half) + self.shape, lambda _: (i, 0) + self.zeros)
        return [(self.from_near[half], spec)]

    def far(self):
        shape = jax.ShapeDtypeStruct((self.half,) + self.shape, BF16)
        x, y = self.call(
            far_kernel,
            self.pair(2, 0) + self.came(0, 1) + self.pair(1, 1) + self.came(1, 1),
            [shape, shape],
            "far_sum",
        )
        self.from_far = [swap(x, 4, self.n_dp), swap(y, 2, self.n_dp)]
        return [x, y]

    def own(self, all_at_once=False):
        full = whole((self.half,) + self.shape)
        outs = self.call(
            own_kernel,
            [v for i in range(2) for v in self.pair(0, i) + self.came(i, 0) + [(self.from_far[i], full)]],
            [jax.ShapeDtypeStruct((1,) + self.shape, BF16 if k else F32) for k in range(self.n_t)],
            "own_sum",
        )
        if all_at_once:
            self.parts = [self.along(v, -k) if k else v for k, v in enumerate(outs)]
        else:
            self.waiting = outs[1]
            self.passed = self.along(outs[2], -1)
            self.parts = [outs[0], self.along(outs[3], 1)]
        return list(outs)

    def along(self, part, step):
        return lax.ppermute(part, "tensor", [(j, (j + step) % self.n_t) for j in range(self.n_t)])

    def pass_on(self):
        full = whole(self.waiting.shape)
        (out,) = self.call(
            relay_kernel,
            [(self.waiting, full), (self.passed, full)],
            [jax.ShapeDtypeStruct(self.waiting.shape, BF16)],
            "relay_sum",
        )
        self.parts.append(self.along(out, -1))
        return out


def finish(parts, n_dp):
    shape = parts[0].shape
    total = small_call(
        last_kernel, (1,), [whole(shape)] * len(parts), whole(shape), jax.ShapeDtypeStruct(shape, F32), "last_sum"
    )(*parts)
    return [spread_rows(total[0, m], n_dp) for m in range(shape[1])]


def spread_rows(total, n_dp):
    groups = n_dp // GROUP
    me = lax.axis_index("dp")
    rows = total.shape[0]
    bit = n_dp // 2
    while bit >= GROUP:
        rows //= 2
        second = (me // bit) % 2
        kept = lax.dynamic_slice_in_dim(total, second * rows, rows, 0)
        sent = lax.dynamic_slice_in_dim(total, (1 - second) * rows, rows, 0)
        total = kept + swap(sent, bit, n_dp)
        bit //= 2
    if groups > 1:
        total = lax.ppermute(
            total, "dp", [(h * GROUP + s, s * groups + h) for h in range(groups) for s in range(GROUP)]
        )
    return total


class SumAll:
    def __init__(self, values, n_dp, n_t):
        self.values, self.n_dp, self.n_t = values, n_dp, n_t
        self.bits = [("tensor", 1 << i) for i in range(n_t.bit_length() - 1)]
        self.bits += [("dp", 1 << i) for i in range(n_dp.bit_length() - 1)]
        self.got = None

    def step(self, token):
        if self.got is not None:
            self.values = self.values + after(self.got, token)
            self.got = None
        if self.bits:
            axis, bit = self.bits.pop(0)
            size = self.n_dp if axis == "dp" else self.n_t
            self.got = lax.ppermute(after(self.values, token), axis, [(i, i ^ bit) for i in range(size)])

    def result(self, token):
        while self.got is not None:
            self.step(token)
        return self.values


def shards(tokens, type_table, norm_gain, norm_bias, w_qkv, w_out, w_up, w_down, cotangent, positions, n_dp, n_t):
    total_rows, width = tokens.shape
    pair_count, slots = positions.shape
    assert pair_count == n_t
    length = total_rows // pair_count
    layers = w_qkv.shape[0]
    top = layers - 1
    inner = w_qkv.shape[3]
    me, quarter = lax.axis_index("dp"), lax.axis_index("tensor")
    rows = width // GROUP
    unit = width // n_dp
    spot = me % GROUP
    spots = jnp.reshape(spot, (1,)).astype(jnp.int32)

    def part_of(block):
        return lax.dynamic_slice_in_dim(block, spot * rows, rows, 0)

    mine = lax.dynamic_slice_in_dim(tokens, quarter * length, length, 0).astype(F32)
    row_ids = lax.broadcasted_iota(jnp.int32, (length, 1), 0)
    stream = mine + jnp.where(row_ids < WORDS, type_table[0], type_table[1])
    gains = [[norm_gain[l, i][None] for i in range(2)] for l in range(layers)]
    biases = [[norm_bias[l, i][None] for i in range(2)] for l in range(layers)]
    own_attn = (w_qkv.transpose(0, 2, 1, 3), w_out)
    own_mlp = (w_up, w_down)

    def attn_part(l):
        left = lax.dynamic_slice(w_qkv, (l, spot * rows, 0, 0), (1, rows, 3, inner)).reshape(rows, 3 * inner)
        right = lax.dynamic_slice(w_out, (l, 0, spot * rows), (1, inner, rows))[0].T
        return jnp.concatenate([left, right], 1)

    def mlp_part(l):
        return jnp.concatenate(
            [lax.dynamic_slice(w, (l, spot * rows, 0), (1, rows, w.shape[2]))[0] for w in (w_up, w_down)], 0
        )

    assert layers == 2
    near, far = 1, n_t - 1

    def hand_on(part, step):
        return lax.ppermute(part, "tensor", [(i, (i + step) % n_t) for i in range(n_t)])

    def to_neighbours(part):
        held = [None] * n_t
        held[near], held[far] = hand_on(part, 1), hand_on(part, -1)
        return held

    def passed_on(held):
        for k in range(2, far):
            held[k] = hand_on(held[k - 1], 1)
        return held[1:]

    def slices_of(matrices):
        return Pieces([[[(v, lead + (k,), 0) for v, lead in slices] for k in range(n_t - 1)] for slices in matrices])

    def core_swap(v):
        return swap(v, 1, n_dp)

    def one_matrix(own, x_piece, y_piece, way):
        own_c, x_c, y_c = core_swap(own), core_swap(x_piece), core_swap(y_piece)
        last = corner(x_piece, y_piece, n_dp, way)
        all_of = [own, own_c, x_piece, x_c, y_piece, y_c, last, core_swap(last)]
        return slices_of([[(v, (0,)) for v in all_of]])

    def two_matrices(own, x_piece, y_piece, token):
        own_c, x_c, y_c = core_swap(own), core_swap(x_piece), core_swap(y_piece)
        first, second = swap(after(x_piece, token)[0], 4, n_dp), swap(after(y_piece, token)[1], 2, n_dp)
        sides = [own, own_c, x_piece, x_c, y_piece, y_c]
        ends = [(first, core_swap(first)), (second, core_swap(second))]
        return slices_of(
            [[(v, (m,)) for v in sides] + [(v, ()) for v in ends[m]] for m in range(2)]
        )

    def sides_of(own):
        return swap(own, 2, n_dp), swap(own, 4, n_dp)

    def run_attention(l, x, pieces, work):
        return attention_forward(spots, x, gains[l][0], biases[l][0], l, own_attn, pieces, n_t, work)

    def run_feed_forward(l, x, pieces, keep, out_type):
        return mlp_forward(spots, x, gains[l][1], biases[l][1], l, own_mlp, pieces, n_t, keep, out_type)

    part_a, part_m = attn_part(0), mlp_part(0)
    part_l = jnp.concatenate([attn_part(1), mlp_part(1)], 0)
    held_a = to_neighbours(part_a)
    held_m = to_neighbours(after(part_m, (held_a[near], held_a[far])))
    hops_a = passed_on(held_a)
    hops_a[0] = after(hops_a[0], part_m, stream, own_attn)
    (own_a,) = pack(hops_a, 1)
    x_a, y_a = sides_of(own_a)
    held_m[near], held_m[far] = after((held_m[near], held_m[far]), (x_a, y_a))
    attn_pieces = [one_matrix(own_a, *after((x_a, y_a), held_m[near], held_m[far]), False)]
    held_l = to_neighbours(after(part_l, held_m[near], held_m[far]))
    hops_m = passed_on(held_m)
    hops_m[0] = after(hops_m[0], part_l)
    (own_m,) = pack(hops_m, 2)
    x_m, y_m = sides_of(own_m)
    first = run_attention(0, after(stream, own_m), attn_pieces[0], 40_000_000_000)
    first, ((held_l[near], held_l[far]),) = gate(first, (held_l[near], held_l[far]))
    x_m, y_m = after((x_m, y_m), first[0])
    mlp_pieces = [two_matrices(own_m, x_m, y_m, first[0])]
    hops_l = passed_on(held_l)
    own_a, own_m = pack(hops_l, 1, 2)
    x_a, y_a = sides_of(own_a)
    x_m, y_m = sides_of(own_m)
    second = run_feed_forward(0, after(first[0], own_a), mlp_pieces[0], True, F32)
    second, ((x_a, y_a),) = gate(second, (x_a, y_a))
    attn_pieces.append(one_matrix(own_a, x_a, y_a, True))
    third = run_attention(1, second[0], attn_pieces[1], 1_000_000)
    if SIDES_FIRST:
        x_m, y_m = after((x_m, y_m), third[0])
        third, ((x_m, y_m),) = gate(third, (x_m, y_m))
    mlp_pieces.append(two_matrices(own_m, x_m, y_m, third[0]))
    saved = [(stream, *first[1:], first[0], *second[1:]), (second[0], *third[1:], third[0])]

    def put_pairs(held):
        out = jnp.zeros((total_rows, width), F32)
        for k, v in enumerate(held):
            out = lax.dynamic_update_slice(out, v.astype(F32), (((quarter - k) % n_t) * length, 0))
        return out

    place = lax.dynamic_slice_in_dim(positions, quarter, 1, 0)[0]
    cot = lax.dynamic_slice_in_dim(cotangent, quarter, 1, 0)[0]
    pick = (lax.broadcasted_iota(jnp.int32, (1, TOP_ROWS), 1) == place[:, None]).astype(BF16)
    pick = jnp.concatenate([pick, jnp.zeros((SLOT_ROWS - slots, TOP_ROWS), BF16)], 0)
    slot_cot = jnp.concatenate(
        [jnp.where(place[:, None] >= 0, cot, 0), jnp.zeros((SLOT_ROWS - slots, width), BF16)], 0
    )
    incoming = tn(pick, slot_cot)

    everything = tuple(range(n_t))
    halves = (everything[: n_t // 2], everything[n_t // 2 :])
    gain_grads = [[None, None] for _ in range(layers)]
    bias_grads = [[None, None] for _ in range(layers)]
    stream_l, normed, proj, logsum, mixed, middle = saved[top]
    grad_middle, gain_grads[top][1], bias_grads[top][1], slot_rows = top_backward(
        spots, incoming, middle, gains[top][1], biases[top][1], pick, slot_cot, top, own_mlp, mlp_pieces[top], n_t
    )
    all_rows = lax.all_gather(slot_rows, ("dp", "tensor"))
    total, incoming, gain_grads[top][0], bias_grads[top][0], _, *keep, send = attention_backward(
        spots, grad_middle, stream_l, gains[top][0], normed, proj, logsum, mixed, None,
        top, own_attn, attn_pieces[top], everything,
    )
    top_attn = Reduction([(keep, send)], n_dp, n_t)

    (last_stream,) = run_feed_forward(top, after(middle, total), mlp_pieces[top], False, BF16)
    last_stream, (top_attn.got,) = gate(last_stream, top_attn.got)
    hidden_held = to_neighbours(last_stream)
    hidden_held[0] = last_stream
    ready = top_attn.near()

    stream_l, normed, proj, logsum, mixed, middle_l, normed_mlp, upward = saved[0]
    outs = mlp_backward(
        spots, after(incoming, ready), middle_l, gains[0][1], normed_mlp, upward, None,
        0, own_mlp, mlp_pieces[0], everything, True,
    )
    outs, (top_attn.from_near, hidden_held) = gate(outs, top_attn.from_near, hidden_held)
    grad_middle, gain_grads[0][1], bias_grads[0][1], *keep, send = outs[1:]
    low_mlp = Reduction([(keep, send)], n_dp, n_t)
    hidden_held[1:] = passed_on(hidden_held)
    ready = top_attn.far()

    outs = attention_backward(
        spots, after(grad_middle, ready), stream_l, gains[0][0], normed, proj, logsum, mixed, None,
        0, own_attn, attn_pieces[0], halves[0],
    )
    outs, (low_mlp.got, top_attn.from_far, hidden_held) = gate(
        outs, low_mlp.got, top_attn.from_far, hidden_held
    )
    total, *keep, send = outs
    first_half = (keep, send)
    ready = low_mlp.near()
    top_attn.from_far = after(top_attn.from_far, ready)
    ready = top_attn.own(True)

    outs = attention_backward(
        spots, after(grad_middle, ready), stream_l, gains[0][0], normed, proj, logsum, mixed, total,
        0, own_attn, attn_pieces[0], halves[1], BF16,
    )
    outs, (low_mlp.from_near, top_attn.parts) = gate(outs, low_mlp.from_near, top_attn.parts)
    incoming, gain_grads[0][0], bias_grads[0][0], type_grad, *keep, send = outs[1:]
    low_attn = Reduction([after(first_half, send), (keep, send)], n_dp, n_t)
    grad_tokens = lax.all_gather(incoming, "tensor", tiled=True)
    ready = low_mlp.far()
    low_attn.got = after(low_attn.got, ready)
    ready = low_attn.near()

    rows_all = SumAll(
        stack_rows(
            [after(type_grad, ready)]
            + [g for pair in gain_grads for g in pair]
            + [g for pair in bias_grads for g in pair]
        ),
        n_dp,
        n_t,
    )

    def finished(reduction, token):
        return finish(after(reduction.parts, token), n_dp)

    sums = {}
    rows_all.step(ready)
    hidden_out = put_pairs(after(hidden_held, ready))
    rows_all.step(hidden_out)
    low_mlp.from_far = after(low_mlp.from_far, hidden_out)
    ready = low_mlp.own()
    rows_all.step(ready)
    low_attn.from_near = after(low_attn.from_near, rows_all.values)
    ready = low_attn.far()

    all_rows = after(all_rows, ready)
    all_cot = all_rows[:, :SLOT_ROWS].reshape(-1, width)
    all_normed = all_rows[:, SLOT_ROWS:].reshape(-1, width)
    slot_up = nn(all_normed, w_up[top])
    slot_grad = (nt(all_cot, w_down[top]) * gelu_slope(slot_up)).astype(BF16)
    grad_up_top = tn(lax.dynamic_slice_in_dim(all_normed, me * unit, unit, 1), slot_grad)
    grad_down_top = tn(
        gelu(slot_up).astype(BF16), lax.dynamic_slice_in_dim(all_cot, me * unit, unit, 1)
    )
    ready = (grad_up_top, grad_down_top)
    ready, (low_attn.from_far, low_mlp.passed) = gate(ready, low_attn.from_far, low_mlp.passed)
    ready = low_mlp.pass_on()
    low_attn.from_far = after(low_attn.from_far, ready)
    ready = low_attn.own()
    rows_all.step(ready)
    (sums["attn", top],) = finished(top_attn, ready)
    low_attn.passed = after(low_attn.passed, rows_all.got if rows_all.got is not None else ready)
    ready = low_attn.pass_on()
    rows_all.step(ready)
    rows_all = rows_all.result(ready)
    grad_tokens = after(grad_tokens, rows_all).astype(F32)
    sums["down", 0], sums["up", 0] = finished(low_mlp, grad_tokens)
    (sums["attn", 0],) = finished(low_attn, (sums["down", 0], sums["up", 0]))

    rows_mine = lax.dynamic_slice_in_dim(rows_all, me * unit, unit, 1)
    grad_gain = rows_mine[2 : 2 + 2 * layers].reshape(layers, 2, unit)
    grad_bias = rows_mine[2 + 2 * layers : 2 + 4 * layers].reshape(layers, 2, unit)
    grad_qkv = jnp.stack([sums["attn", l][:, : 3 * inner].reshape(unit, 3, inner) for l in range(layers)])
    grad_out = jnp.stack([sums["attn", l][:, 3 * inner :].T for l in range(layers)])
    grad_up = jnp.stack([grad_up_top if l == top else sums["up", l] for l in range(layers)])
    grad_down = jnp.stack([grad_down_top if l == top else sums["down", l].T for l in range(layers)])
    return hidden_out, grad_tokens, rows_mine[:2], grad_gain, grad_bias, grad_qkv, grad_out, grad_up, grad_down


def solution(mesh):
    n_dp, n_t = mesh.shape["dp"], mesh.shape["tensor"]
    placed = (
        P("dp", None),
        P(),
        P(),
        P(),
        P(None, None, None, "tensor"),
        P(None, "tensor", None),
        P(None, None, "tensor"),
        P(None, "tensor", None),
        P("dp", None, None),
        P("dp", None),
    )

    def run(*args):
        return shards(*args, n_dp, n_t)

    return jax.shard_map(
        run,
        mesh=mesh,
        in_specs=placed,
        out_specs=(
            P("dp", None),
            P("dp", None),
            P(None, "dp"),
            P(None, None, "dp"),
            P(None, None, "dp"),
            P(None, "dp", None, "tensor"),
            P(None, "tensor", "dp"),
            P(None, "dp", "tensor"),
            P(None, "tensor", "dp"),
        ),
        check_vma=False,
    )
```

```python
import functools

import jax
import jax.numpy as jnp
from jax import lax
from jax.experimental import pallas as pl
from jax.experimental.pallas import tpu as pltpu
from jax.sharding import PartitionSpec as P

HD = 64
WORDS = 40
TOP_ROWS = 48
SLOT_ROWS = 16
EPSILON = 1e-06
ROOT_HALF = 0.7071067811865476
ROOT_TWO_PI = 2.5066282746310002
GROUP = 8
STEP = 32
SIDES_FIRST = True
F32 = jnp.float32
BF16 = jnp.bfloat16
SMALL_VMEM = 16 * 1024 * 1024
VMEM_BYTES = 60 * 1024 * 1024


def dot(left, right, dims):
    return lax.dot_general(left, right, (dims, ((), ())), preferred_element_type=F32)


def nn(left, right):
    return dot(left, right, ((1,), (0,)))


def nt(left, right):
    return dot(left, right, ((1,), (1,)))


def tn(left, right):
    return dot(left, right, ((0,), (0,)))


def gelu(values):
    return 0.5 * values * (1.0 + lax.erf(values * ROOT_HALF))


def gelu_slope(values):
    return 0.5 * (1.0 + lax.erf(values * ROOT_HALF)) + values * jnp.exp(-0.5 * values * values) / ROOT_TWO_PI


def norm_parts(values):
    average = jnp.mean(values, axis=-1, keepdims=True)
    centred = values - average
    spread = jnp.mean(centred * centred, axis=-1, keepdims=True)
    rate = lax.rsqrt(spread + EPSILON)
    return centred * rate, rate


def norm_rows(source, gain, bias, target):
    step = STEP if source.shape[0] % STEP == 0 else STEP // 2
    for r in range(0, source.shape[0], step):
        rows = slice(r, r + step)
        target[rows, :] = (norm_parts(source[rows, :])[0] * gain[...] + bias[...]).astype(BF16)


def norm_back_rows(rows, values, gain, incoming, gain_grad, bias_grad):
    unit, rate = norm_parts(values[rows, :])
    e = incoming[rows, :]
    scaled = e * gain[...]
    inner = jnp.mean(scaled * unit, axis=-1, keepdims=True)
    gain_grad[...] += jnp.sum(e * unit, axis=0, keepdims=True)
    bias_grad[...] += jnp.sum(e, axis=0, keepdims=True)
    return rate * (scaled - jnp.mean(scaled, axis=-1, keepdims=True) - unit * inner)


def flops(count):
    return pl.CostEstimate(flops=count, bytes_accessed=1_000_000, transcendentals=0)


KERNEL_COST = pl.CostEstimate(flops=40_000_000_000, bytes_accessed=1_000_000, transcendentals=0)
SMALL_COST = pl.CostEstimate(flops=1_000_000_000, bytes_accessed=1_000_000, transcendentals=0)


class Pieces:
    def __init__(self, at):
        self.arrays = []
        self.plan = []
        for matrix in at:
            for k, slices in enumerate(matrix, 1):
                for s, (array, lead, row) in enumerate(slices):
                    found = [i for i, v in enumerate(self.arrays) if v is array]
                    if not found:
                        self.arrays.append(array)
                        found = [len(self.arrays) - 1]
                    self.plan.append((len(self.plan) // (len(matrix) * GROUP), k, s, found[0], lead, row))


def fetch(spot, layer, own, plan, sources, scratches, sems, quarters):
    rows = scratches[0].shape[1] // GROUP
    for k in quarters:
        for m, scratch in enumerate(scratches):
            if k == 0 and own:
                pltpu.make_async_copy(own[m].at[layer], scratch.at[0], sems.at[0]).start()
        for m, at_k, s, which, lead, row in plan:
            if at_k == k:
                source = sources[which] if lead is None else sources[which].at[lead]
                at = pl.multiple_of((spot ^ s) * rows, rows)
                pltpu.make_async_copy(
                    source.at[pl.ds(row, rows)],
                    scratches[m].at[k - quarters[0], pl.ds(at, rows)],
                    sems.at[k - quarters[0]],
                ).start()


def arrived(k, scratches, sems):
    for scratch in scratches:
        pltpu.make_async_copy(scratch.at[k], scratch.at[k], sems.at[k]).wait()


def own_copies(layer, own_qkv, own_out, raw_qkv, raw_out, sem):
    return [
        pltpu.make_async_copy(own_qkv.at[layer], raw_qkv, sem),
        pltpu.make_async_copy(own_out.at[layer], raw_out, sem),
    ]


def own_block(copies, raw_qkv, raw_out, block):
    for copy in copies:
        copy.wait()
    inner = raw_qkv.shape[2]
    for c in range(3):
        block[0, :, c * inner : (c + 1) * inner] = raw_qkv[c]
    block[0, :, 3 * inner :] = raw_out[...].astype(F32).T.astype(BF16)


def flip(spot, source, target):
    width = source.shape[1]
    rows = width // GROUP
    turned = source.astype(F32).T.astype(BF16)
    for j in range(GROUP):
        s = spot ^ j
        at = pl.multiple_of(((s & 1) * (GROUP // 2) + (s >> 1)) * rows, rows)
        target[pl.ds(at, rows), :] = turned[j * rows : (j + 1) * rows, :]


def put_block(block, keep, send, part, columns=slice(None)):
    half = block.shape[0] // 2
    rows = half // (GROUP // 2)
    for i in range(GROUP // 2):
        keep[i][0, part, :, columns] = block[i * rows : (i + 1) * rows].astype(BF16)
        send[i, 0, part, :, columns] = block[half + i * rows : half + (i + 1) * rows].astype(BF16)


def any_spec():
    return pl.BlockSpec(memory_space=pl.ANY)


def smem_spec():
    return pl.BlockSpec(memory_space=pltpu.SMEM)


def whole(shape):
    return pl.BlockSpec(shape, lambda k: (0,) * len(shape))


def per_quarter(shape, first=0):
    return pl.BlockSpec((1,) + shape, lambda k: (first + k,) + (0,) * len(shape))


def block_specs(matrices, rows, width):
    own = pl.BlockSpec((1, matrices, rows, width), lambda k: (k, 0, 0, 0))
    return [own] * (GROUP // 2) + [
        pl.BlockSpec((GROUP // 2, 1, matrices, rows, width), lambda k: (0, k, 0, 0, 0))
    ]


def block_shapes(quarters, matrices, rows, width):
    own = jax.ShapeDtypeStruct((quarters, matrices, rows, width), BF16)
    return [own] * (GROUP // 2) + [jax.ShapeDtypeStruct((GROUP // 2, quarters, matrices, rows, width), BF16)]


def params(limit=VMEM_BYTES):
    return pltpu.CompilerParams(vmem_limit_bytes=limit)


def cost(flops, moved):
    return pl.CostEstimate(flops=flops, bytes_accessed=moved, transcendentals=0)


def attention_forward_kernel(layer, plan, count, spot_ref, x, gain, bias, own_qkv, own_out, *rest):
    middle, normed, proj, logsum, mixed, block, sems, raw_qkv, raw_out = rest[count:]
    k = pl.program_id(0)
    inner = raw_out.shape[0]
    heads = inner // HD

    @pl.when(k == 0)
    def _():
        copies = own_copies(layer, own_qkv, own_out, raw_qkv, raw_out, sems.at[0])
        for copy in copies:
            copy.start()
        fetch(spot_ref[0], layer, [], plan, rest[:count], [block], sems, range(block.shape[0]))
        norm_rows(x, gain, bias, normed)
        middle[...] = x[...]
        logsum[...] = jnp.zeros_like(logsum)
        own_block(copies, raw_qkv, raw_out, block)

    @pl.when(k > 0)
    def _():
        arrived(k, [block], sems)

    proj[0] = nn(normed[...], block[k])[:, : 3 * inner].astype(BF16)
    lane = lax.broadcasted_iota(jnp.int32, logsum.shape, 1)
    every = range(heads)
    lanes = [slice(h * HD, (h + 1) * HD) for h in range(3 * heads)]
    scores = [
        nt(proj[0, :, lanes[h]] * jnp.asarray(HD**-0.5, BF16), proj[0, :, lanes[heads + h]]) for h in every
    ]
    tops = [jnp.max(v, axis=-1, keepdims=True) for v in scores]
    powers = [jnp.exp(v - t) for v, t in zip(scores, tops)]
    totals = [jnp.sum(v, axis=-1, keepdims=True) for v in powers]
    kept = logsum[...]
    for h in every:
        kept = jnp.where(lane == k * heads + h, tops[h] + jnp.log(totals[h]), kept)
    logsum[...] = kept
    weights = [(v * (1.0 / t)).astype(BF16) for v, t in zip(powers, totals)]
    mixes = [nn(weights[h], proj[0, :, lanes[2 * heads + h]]).astype(BF16) for h in every]
    pad = mixed.shape[2] - inner
    mixed[0] = jnp.concatenate([jnp.zeros((normed.shape[0], pad), BF16)] + mixes, 1)
    middle[...] += nt(mixed[0], block[k, :, 3 * inner - pad :]).astype(BF16).astype(F32)


def attention_forward(spot, x, gain, bias, layer, own, pieces, n_t, work):
    length, width = x.shape
    inner = own[1].shape[1]
    count = len(pieces.arrays)
    out = [
        jax.ShapeDtypeStruct((length, width), F32),
        jax.ShapeDtypeStruct((length, width), BF16),
        jax.ShapeDtypeStruct((n_t, length, 3 * inner), BF16),
        jax.ShapeDtypeStruct((length, 128), F32),
        jax.ShapeDtypeStruct((n_t, length, inner + inner % 128), BF16),
    ]
    return pl.pallas_call(
        functools.partial(attention_forward_kernel, layer, pieces.plan, count),
        grid=(n_t,),
        out_shape=out,
        in_specs=[smem_spec(), whole((length, width)), whole((1, width)), whole((1, width))] + [any_spec()] * (2 + count),
        out_specs=[
            whole((length, width)),
            whole((length, width)),
            per_quarter((length, 3 * inner)),
            whole((length, 128)),
            per_quarter((length, inner + inner % 128)),
        ],
        scratch_shapes=[
            pltpu.VMEM((n_t, width, 4 * inner), BF16),
            pltpu.SemaphoreType.DMA((n_t,)),
            pltpu.VMEM((3, width, inner), BF16),
            pltpu.VMEM((inner, width), BF16),
        ],
        compiler_params=params(),
        cost_estimate=flops(work),
        name="attention_forward",
    )(spot, x, gain, bias, *own, *pieces.arrays)


def mlp_forward_kernel(kept_rows, layer, plan, count, spot_ref, x, gain, bias, own_up, own_down, *rest):
    if kept_rows:
        out, normed, upward, ups, downs, total, sems = rest[count:]
    else:
        out, ups, downs, total, sems, normed = rest[count:]
    k = pl.program_id(0)

    @pl.when(k == 0)
    def _():
        fetch(spot_ref[0], layer, [own_up, own_down], plan, rest[:count], [ups, downs], sems, range(ups.shape[0]))
        norm_rows(x, gain, bias, normed)
        total[...] = x[...]

    arrived(k, [ups, downs], sems)
    up = nn(normed[...], ups[k])
    if kept_rows:
        upward[0] = up
    active = gelu(up).astype(BF16)
    total[...] += nn(active, downs[k]).astype(BF16).astype(F32)

    @pl.when(k == pl.num_programs(0) - 1)
    def _():
        out[...] = total[...].astype(out.dtype)


def mlp_forward(spot, x, gain, bias, layer, own, pieces, n_t, kept_rows, out_type):
    length, width = x.shape
    hidden = own[0].shape[2]
    count = len(pieces.arrays)
    out = [jax.ShapeDtypeStruct((length, width), out_type)]
    out_specs = [whole((length, width))]
    scratch = []
    if kept_rows:
        out += [jax.ShapeDtypeStruct((length, width), BF16), jax.ShapeDtypeStruct((n_t, length, hidden), F32)]
        out_specs += [whole((length, width)), per_quarter((length, hidden))]
    else:
        scratch.append(pltpu.VMEM((length, width), BF16))
    return pl.pallas_call(
        functools.partial(mlp_forward_kernel, kept_rows, layer, pieces.plan, count),
        grid=(n_t,),
        out_shape=out,
        in_specs=[smem_spec(), whole((length, width)), whole((1, width)), whole((1, width))]
        + [any_spec()] * (2 + count),
        out_specs=out_specs,
        scratch_shapes=[
            pltpu.VMEM((n_t,) + own[0].shape[1:], BF16),
            pltpu.VMEM((n_t,) + own[1].shape[1:], BF16),
            pltpu.VMEM((length, width), F32),
            pltpu.SemaphoreType.DMA((n_t,)),
        ]
        + scratch,
        compiler_params=params(),
        cost_estimate=KERNEL_COST,
        name="mlp_forward",
    )(spot, x, gain, bias, *own, *pieces.arrays)


def mlp_backward_kernel(quarters, last, blocks, layer, plan, count, spot_ref, incoming, x, gain, normed, upward, total_in, *rest):
    own, sources = rest[:2], rest[2 : 2 + count]
    rest = list(rest[2 + count :])
    total = rest.pop(0)
    if last:
        grad, gain_grad, bias_grad = (rest.pop(0) for _ in range(3))
    if blocks:
        keep, send = [rest.pop(0) for _ in range(GROUP // 2)], rest.pop(0)
    ups, downs, sems, *flipped = rest
    k = pl.program_id(0)

    @pl.when(k == 0)
    def _():
        fetch(spot_ref[0], layer, own, plan, sources, [ups, downs], sems, quarters)
        total[...] = jnp.zeros_like(total) if quarters[0] == 0 else total_in[...]
        if blocks:
            flip(spot_ref[0], incoming[...], flipped[0])
            flip(spot_ref[0], normed[...], flipped[1])

    arrived(k, [ups, downs], sems)
    up = upward[0]
    grad_active = nt(incoming[...].astype(BF16), downs[k])
    bell = 0.5 * (1.0 + lax.erf(up * ROOT_HALF))
    grad_up = (grad_active * (bell + up * jnp.exp(-0.5 * up * up) * (1.0 / ROOT_TWO_PI))).astype(BF16)
    total[...] += nt(grad_up, ups[k])
    if blocks:
        put_block(nn(flipped[0][...], (up * bell).astype(BF16)), keep, send, 0)
        put_block(nn(flipped[1][...], grad_up), keep, send, 1)

    if last:

        @pl.when(k == pl.num_programs(0) - 1)
        def _():
            gain_grad[...] = jnp.zeros_like(gain_grad)
            bias_grad[...] = jnp.zeros_like(bias_grad)
            for r in range(0, x.shape[0], 16):
                rows = slice(r, r + 16)
                grad[rows, :] = incoming[rows, :] + norm_back_rows(rows, x, gain, total, gain_grad, bias_grad)


def mlp_backward(spot, incoming, x, gain, normed, upward, total, layer, own, pieces, quarters, blocks):
    length, width = incoming.shape
    n_t, hidden = upward.shape[0], upward.shape[2]
    last = quarters[-1] == n_t - 1
    count = len(quarters)
    if total is None:
        total = gain
    out = [jax.ShapeDtypeStruct((length, width), F32)]
    out_specs = [whole((length, width))]
    if last:
        out += [jax.ShapeDtypeStruct(v, F32) for v in ((length, width), (1, width), (1, width))]
        out_specs += [whole((length, width)), whole((1, width)), whole((1, width))]
    scratch = [
        pltpu.VMEM((count,) + own[0].shape[1:], BF16),
        pltpu.VMEM((count,) + own[1].shape[1:], BF16),
        pltpu.SemaphoreType.DMA((count,)),
    ]
    if blocks:
        out += block_shapes(count, 2, width // GROUP, hidden)
        out_specs += block_specs(2, width // GROUP, hidden)
        scratch += [pltpu.VMEM((width, length), BF16)] * 2
    return pl.pallas_call(
        functools.partial(mlp_backward_kernel, quarters, last, blocks, layer, pieces.plan, len(pieces.arrays)),
        grid=(count,),
        out_shape=out,
        in_specs=[
            smem_spec(),
            whole((length, width)),
            whole((length, width)),
            whole((1, width)),
            whole((length, width)),
            per_quarter((length, hidden), quarters[0]),
            whole(total.shape),
        ]
        + [any_spec()] * (2 + len(pieces.arrays)),
        out_specs=out_specs,
        scratch_shapes=scratch,
        compiler_params=params(),
        cost_estimate=KERNEL_COST,
        name="mlp_backward",
    )(spot, incoming, x, gain, normed, upward, total, *own, *pieces.arrays)


def top_kernel(layer, plan, count, spot_ref, incoming, x, gain, bias, pick, slots, own_up, own_down, *rest):
    grad, gain_grad, bias_grad, packed, ups, downs, total, sems, normed = rest[count:]
    k = pl.program_id(0)

    @pl.when(k == 0)
    def _():
        fetch(spot_ref[0], layer, [own_up, own_down], plan, rest[:count], [ups, downs], sems, range(ups.shape[0]))
        norm_rows(x, gain, bias, normed)
        total[...] = jnp.zeros_like(total)
        packed[:SLOT_ROWS, :] = slots[...]
        packed[SLOT_ROWS:, :] = nn(pick[...], normed[...]).astype(BF16)

    arrived(k, [ups, downs], sems)
    up = nn(normed[...], ups[k])
    grad_up = (nt(incoming[...].astype(BF16), downs[k]) * gelu_slope(up)).astype(BF16)
    total[...] += nt(grad_up, ups[k])

    @pl.when(k == pl.num_programs(0) - 1)
    def _():
        gain_grad[...] = jnp.zeros_like(gain_grad)
        bias_grad[...] = jnp.zeros_like(bias_grad)
        for r in range(0, incoming.shape[0], 16):
            rows = slice(r, r + 16)
            grad[rows, :] = incoming[rows, :] + norm_back_rows(rows, x, gain, total, gain_grad, bias_grad)


def top_backward(spot, incoming, x, gain, bias, pick, slots, layer, own, pieces, n_t):
    length, width = incoming.shape
    rows = pl.BlockSpec((length, width), lambda k: (0, 0))
    row = whole((1, width))
    return pl.pallas_call(
        functools.partial(top_kernel, layer, pieces.plan, len(pieces.arrays)),
        grid=(n_t,),
        out_shape=[
            jax.ShapeDtypeStruct((length, width), F32),
            jax.ShapeDtypeStruct((1, width), F32),
            jax.ShapeDtypeStruct((1, width), F32),
            jax.ShapeDtypeStruct((2 * SLOT_ROWS, width), BF16),
        ],
        in_specs=[smem_spec(), rows, rows, row, row, whole(pick.shape), whole(slots.shape)] + [any_spec()] * (2 + len(pieces.arrays)),
        out_specs=[rows, row, row, whole((2 * SLOT_ROWS, width))],
        scratch_shapes=[
            pltpu.VMEM((n_t,) + own[0].shape[1:], BF16),
            pltpu.VMEM((n_t,) + own[1].shape[1:], BF16),
            pltpu.VMEM((length, width), F32),
            pltpu.SemaphoreType.DMA((n_t,)),
            pltpu.VMEM((length, width), BF16),
        ],
        compiler_params=params(),
        cost_estimate=KERNEL_COST,
        name="top_backward",
    )(spot, incoming, x, gain, bias, pick, slots, *own, *pieces.arrays)


def attention_backward_kernel(
    quarters, last, layer, plan, count, spot_ref, incoming, x, gain, normed, proj, logsum, mixed, total_in, own_qkv, own_out, *rest
):
    sources = rest[:count]
    rest = list(rest[count:])
    total = rest.pop(0)
    if last:
        grad, gain_grad, bias_grad, types = (rest.pop(0) for _ in range(4))
    keep = [rest.pop(0) for _ in range(GROUP // 2)]
    send, block, grad_proj, sems, low_t, normed_t, raw_qkv, raw_out = rest
    k = pl.program_id(0)
    top = incoming.shape[0]
    inner = raw_out.shape[0]
    heads = inner // HD

    @pl.when(k == 0)
    def _():
        if quarters[0] == 0:
            copies = own_copies(layer, own_qkv, own_out, raw_qkv, raw_out, sems.at[0])
            for copy in copies:
                copy.start()
        fetch(spot_ref[0], layer, [], plan, sources, [block], sems, quarters)
        total[...] = jnp.zeros_like(total) if quarters[0] == 0 else total_in[...]
        grad_proj[...] = jnp.zeros_like(grad_proj)
        flip(spot_ref[0], incoming[...], low_t)
        flip(spot_ref[0], normed[...], normed_t)
        if quarters[0] == 0:
            own_block(copies, raw_qkv, raw_out, block)

    @pl.when(quarters[0] + k > 0)
    def _():
        arrived(k, [block], sems)

    pad = mixed.shape[2] - inner
    grad_mixed = nn(incoming[...].astype(BF16), block[k, :, 3 * inner - pad :]).astype(BF16)
    lane = lax.broadcasted_iota(jnp.int32, (top, 128), 1)
    every = range(heads)
    lanes = [slice(h * HD, (h + 1) * HD) for h in range(3 * heads)]
    queries = [proj[0, :top, lanes[h]] * jnp.asarray(HD**-0.5, BF16) for h in every]
    keys = [proj[0, :, lanes[heads + h]] for h in every]
    head_grads = [grad_mixed[:, pad + h * HD : pad + (h + 1) * HD] for h in every]
    scores = [nt(queries[h], keys[h]) for h in every]
    grad_weights = [nt(head_grads[h], proj[0, :, lanes[2 * heads + h]]) for h in every]
    row_sums = [
        jnp.sum(
            jnp.where(lane == (quarters[0] + k) * heads + h, logsum[:top, :], 0.0), axis=-1, keepdims=True
        )
        for h in every
    ]
    weights = [jnp.exp(scores[h] - row_sums[h]) for h in every]
    for h in every:
        grad_proj[:, lanes[2 * heads + h]] = tn(weights[h].astype(BF16), head_grads[h]).astype(BF16)
    inner_sums = [jnp.sum(weights[h] * grad_weights[h], axis=-1, keepdims=True) for h in every]
    grad_scores = [(weights[h] * (grad_weights[h] - inner_sums[h])).astype(BF16) for h in every]
    for h in every:
        grad_proj[:top, lanes[h]] = (nn(grad_scores[h], keys[h]) * HD**-0.5).astype(BF16)
        grad_proj[:, lanes[heads + h]] = tn(grad_scores[h], queries[h]).astype(BF16)
    wide = grad_proj.shape[1]
    total[...] += nt(grad_proj[...], block[k, :, :wide])
    left = nn(normed_t[...], grad_proj[...])
    right = nn(low_t[...], mixed[0, :top, :])
    at = 3 * inner - pad
    put_block(left[:, :at], keep, send, 0, slice(0, at))
    put_block(left[:, at:] + right[:, : wide - at], keep, send, 0, slice(at, wide))
    put_block(right[:, wide - at :], keep, send, 0, slice(wide, 4 * inner))

    if last:

        @pl.when(k == pl.num_programs(0) - 1)
        def _():
            gain_grad[...] = jnp.zeros_like(gain_grad)
            bias_grad[...] = jnp.zeros_like(bias_grad)
            types[...] = jnp.zeros_like(types)
            step = 8
            for r in range(0, x.shape[0], step):
                rows = slice(r, r + step)
                back = norm_back_rows(rows, x, gain, total, gain_grad, bias_grad)
                if r < top:
                    back = back + incoming[rows, :]
                grad[rows, :] = back.astype(grad.dtype)
                which = slice(0, 1) if r < WORDS else slice(1, 2)
                types[which, :] += jnp.sum(back, axis=0, keepdims=True)


def attention_backward(
    spot, incoming, x, gain, normed, proj, logsum, mixed, total, layer, own, pieces, quarters, out_type=F32
):
    length, width = x.shape
    top = incoming.shape[0]
    n_t = proj.shape[0]
    last = quarters[-1] == n_t - 1
    count = len(quarters)
    inner = own[1].shape[1]
    if total is None:
        total = gain
    out = [jax.ShapeDtypeStruct((length, width), F32)]
    out_specs = [whole((length, width))]
    if last:
        out.append(jax.ShapeDtypeStruct((length, width), out_type))
        out += [jax.ShapeDtypeStruct(v, F32) for v in ((1, width), (1, width), (2, width))]
        out_specs += [whole(v.shape) for v in out[1:]]
    out += block_shapes(count, 1, width // GROUP, 4 * inner)
    out_specs += block_specs(1, width // GROUP, 4 * inner)
    return pl.pallas_call(
        functools.partial(attention_backward_kernel, quarters, last, layer, pieces.plan, len(pieces.arrays)),
        grid=(count,),
        out_shape=out,
        in_specs=[
            smem_spec(),
            whole((top, width)),
            whole((length, width)),
            whole((1, width)),
            whole((length, width)),
            per_quarter((length, 3 * inner), quarters[0]),
            whole((length, 128)),
            per_quarter((length, inner + inner % 128), quarters[0]),
            whole(total.shape),
        ]
        + [any_spec()] * (2 + len(pieces.arrays)),
        out_specs=out_specs,
        scratch_shapes=[
            pltpu.VMEM((count, width, 4 * inner), BF16),
            pltpu.VMEM((length, 3 * inner + (3 * inner) % 128), BF16),
            pltpu.SemaphoreType.DMA((count,)),
            pltpu.VMEM((width, top), BF16),
            pltpu.VMEM((width, length), BF16),
            pltpu.VMEM((3, width, inner), BF16),
            pltpu.VMEM((inner, width), BF16),
        ],
        compiler_params=params(),
        cost_estimate=KERNEL_COST,
        name="attention_backward",
    )(spot, incoming, x, gain, normed, proj, logsum, mixed, total, *own, *pieces.arrays)


def swap(values, bit, size):
    return lax.ppermute(values, "dp", [(i, i ^ bit) for i in range(size)])


def after(values, *others):
    return lax.optimization_barrier((values, others))[0]


def gate(outs, *others):
    return lax.optimization_barrier((outs, others))


def small_call(kernel, grid, in_specs, out_specs, out_shape, name):
    return pl.pallas_call(
        kernel,
        grid=grid,
        in_specs=in_specs,
        out_specs=out_specs,
        out_shape=out_shape,
        compiler_params=params(SMALL_VMEM),
        cost_estimate=SMALL_COST,
        name=name,
    )


def pack_kernel(groups, *refs):
    sources, targets = refs[: -len(groups)], refs[-len(groups) :]
    rows = targets[0].shape[2]
    for k, source in enumerate(sources):
        for target, (first, count) in zip(targets, groups):
            for m in range(count):
                target[m, k] = source[(first + m) * rows : (first + m + 1) * rows, :]


def pack(sources, *counts):
    total, width = sources[0].shape
    rows = total // sum(counts)
    groups = [(sum(counts[:i]), count) for i, count in enumerate(counts)]
    shapes = [(count, len(sources), rows, width) for count in counts]
    return small_call(
        functools.partial(pack_kernel, groups),
        (1,),
        [whole((total, width))] * len(sources),
        [whole(shape) for shape in shapes],
        [jax.ShapeDtypeStruct(shape, BF16) for shape in shapes],
        "pack",
    )(*sources)


def corner(x_piece, y_piece, n_dp, by_x):
    return swap(y_piece, 2, n_dp) if by_x else swap(x_piece, 4, n_dp)


def near_kernel(*refs):
    *operands, x_out, y_out = refs
    for out, four in ((x_out, operands[:4]), (y_out, operands[4:])):
        for i in range(2):
            out[i] = (four[2 * i][...].astype(F32) + four[2 * i + 1][0].astype(F32)).astype(BF16)


def far_kernel(*refs):
    *operands, x_out, y_out = refs
    for out, (kept, got, near) in ((x_out, operands[:3]), (y_out, operands[3:])):
        out[...] = (kept[...].astype(F32) + got[0].astype(F32) + near[0].astype(F32)).astype(BF16)


def own_kernel(*refs):
    operands, outs = refs[:8], refs[8:]
    half = len(outs) // 2
    for i, out in enumerate(outs):
        kept, got, near, far = operands[4 * (i // half) : 4 * (i // half) + 4]
        j = i % half
        total = kept[j].astype(F32) + got[0, j].astype(F32) + near[0, j].astype(F32) + far[j].astype(F32)
        out[0] = total.astype(out.dtype)


def rows_kernel(*refs):
    *sources, target = refs
    target[...] = jnp.zeros_like(target)
    at = 0
    for source in sources:
        count = source.shape[0]
        target[at : at + count, :] = source[...]
        at += count


def stack_rows(sources):
    width = sources[0].shape[1]
    count = -(-sum(v.shape[0] for v in sources) // 8) * 8
    return small_call(
        rows_kernel,
        (1,),
        [whole(v.shape) for v in sources],
        whole((count, width)),
        jax.ShapeDtypeStruct((count, width), F32),
        "stack_rows",
    )(*sources)


def relay_kernel(first, second, out):
    out[...] = (first[...].astype(F32) + second[...].astype(F32)).astype(BF16)


def last_kernel(*refs):
    *parts, out = refs
    total = parts[0][...].astype(F32)
    for part in parts[1:]:
        total = total + part[...].astype(F32)
    out[...] = total


class Reduction:
    def __init__(self, blocks, n_dp, n_t):
        self.keep, self.got = [], []
        self.n_dp, self.n_t = n_dp, n_t
        self.half = n_t // 2
        for keep, send in blocks:
            self.add(keep, send)
        self.shape = self.keep[0][0].shape[1:]
        self.zeros = (0,) * len(self.shape)

    def add(self, keep, send):
        self.keep.append(keep)
        self.got.append(swap(send, 1, self.n_dp))

    def pair(self, plane, half):
        n = len(self.keep)
        at = half // n
        specs = [
            pl.BlockSpec((self.half,) + self.shape, lambda _: (at,) + self.zeros),
            pl.BlockSpec((1, self.half) + self.shape, lambda _: (plane, at) + self.zeros),
        ]
        return list(zip([self.keep[half % n][plane], self.got[half % n]], specs))

    def call(self, kernel, operands, shapes, name):
        return small_call(
            kernel,
            (1,),
            [spec for _, spec in operands],
            [whole(v.shape) for v in shapes],
            shapes,
            name,
        )(*[v for v, _ in operands])

    def near(self):
        shape = jax.ShapeDtypeStruct((2, self.half) + self.shape, BF16)
        x, y = self.call(
            near_kernel,
            self.pair(1, 0) + self.pair(3, 0) + self.pair(2, 1) + self.pair(3, 1),
            [shape, shape],
            "near_sum",
        )
        self.from_near = [swap(x, 2, self.n_dp), swap(y, 4, self.n_dp)]
        return [x, y]

    def came(self, half, i):
        spec = pl.BlockSpec((1, self.half) + self.shape, lambda _: (i, 0) + self.zeros)
        return [(self.from_near[half], spec)]

    def far(self):
        shape = jax.ShapeDtypeStruct((self.half,) + self.shape, BF16)
        x, y = self.call(
            far_kernel,
            self.pair(2, 0) + self.came(0, 1) + self.pair(1, 1) + self.came(1, 1),
            [shape, shape],
            "far_sum",
        )
        self.from_far = [swap(x, 4, self.n_dp), swap(y, 2, self.n_dp)]
        return [x, y]

    def own(self, all_at_once=False):
        full = whole((self.half,) + self.shape)
        outs = self.call(
            own_kernel,
            [v for i in range(2) for v in self.pair(0, i) + self.came(i, 0) + [(self.from_far[i], full)]],
            [jax.ShapeDtypeStruct((1,) + self.shape, BF16 if k else F32) for k in range(self.n_t)],
            "own_sum",
        )
        if all_at_once:
            self.parts = [self.along(v, -k) if k else v for k, v in enumerate(outs)]
        else:
            self.waiting = outs[1]
            self.passed = self.along(outs[2], -1)
            self.parts = [outs[0], self.along(outs[3], 1)]
        return list(outs)

    def along(self, part, step):
        return lax.ppermute(part, "tensor", [(j, (j + step) % self.n_t) for j in range(self.n_t)])

    def pass_on(self):
        full = whole(self.waiting.shape)
        (out,) = self.call(
            relay_kernel,
            [(self.waiting, full), (self.passed, full)],
            [jax.ShapeDtypeStruct(self.waiting.shape, BF16)],
            "relay_sum",
        )
        self.parts.append(self.along(out, -1))
        return out


def finish(parts, n_dp):
    shape = parts[0].shape
    total = small_call(
        last_kernel, (1,), [whole(shape)] * len(parts), whole(shape), jax.ShapeDtypeStruct(shape, F32), "last_sum"
    )(*parts)
    return [spread_rows(total[0, m], n_dp) for m in range(shape[1])]


def spread_rows(total, n_dp):
    groups = n_dp // GROUP
    me = lax.axis_index("dp")
    rows = total.shape[0]
    bit = n_dp // 2
    while bit >= GROUP:
        rows //= 2
        second = (me // bit) % 2
        kept = lax.dynamic_slice_in_dim(total, second * rows, rows, 0)
        sent = lax.dynamic_slice_in_dim(total, (1 - second) * rows, rows, 0)
        total = kept + swap(sent, bit, n_dp)
        bit //= 2
    if groups > 1:
        total = lax.ppermute(
            total, "dp", [(h * GROUP + s, s * groups + h) for h in range(groups) for s in range(GROUP)]
        )
    return total


class SumAll:
    def __init__(self, values, n_dp, n_t):
        self.values, self.n_dp, self.n_t = values, n_dp, n_t
        self.bits = [("tensor", 1 << i) for i in range(n_t.bit_length() - 1)]
        self.bits += [("dp", 1 << i) for i in range(n_dp.bit_length() - 1)]
        self.got = None

    def step(self, token):
        if self.got is not None:
            self.values = self.values + after(self.got, token)
            self.got = None
        if self.bits:
            axis, bit = self.bits.pop(0)
            size = self.n_dp if axis == "dp" else self.n_t
            self.got = lax.ppermute(after(self.values, token), axis, [(i, i ^ bit) for i in range(size)])

    def result(self, token):
        while self.got is not None:
            self.step(token)
        return self.values


def shards(tokens, type_table, norm_gain, norm_bias, w_qkv, w_out, w_up, w_down, cotangent, positions, n_dp, n_t):
    total_rows, width = tokens.shape
    pair_count, slots = positions.shape
    assert pair_count == n_t
    length = total_rows // pair_count
    layers = w_qkv.shape[0]
    top = layers - 1
    inner = w_qkv.shape[3]
    me, quarter = lax.axis_index("dp"), lax.axis_index("tensor")
    rows = width // GROUP
    unit = width // n_dp
    spot = me % GROUP
    spots = jnp.reshape(spot, (1,)).astype(jnp.int32)

    def part_of(block):
        return lax.dynamic_slice_in_dim(block, spot * rows, rows, 0)

    mine = lax.dynamic_slice_in_dim(tokens, quarter * length, length, 0).astype(F32)
    row_ids = lax.broadcasted_iota(jnp.int32, (length, 1), 0)
    stream = mine + jnp.where(row_ids < WORDS, type_table[0], type_table[1])
    gains = [[norm_gain[l, i][None] for i in range(2)] for l in range(layers)]
    biases = [[norm_bias[l, i][None] for i in range(2)] for l in range(layers)]
    own_attn = (w_qkv.transpose(0, 2, 1, 3), w_out)
    own_mlp = (w_up, w_down)

    def attn_part(l):
        at = spot * rows
        left = lax.dynamic_slice(w_qkv, (l, at, 0, 0), (1, rows, 3, inner)).reshape(rows, 3 * inner)
        right = lax.dynamic_slice(w_out, (l, 0, at), (1, inner, rows))[0].T
        return jnp.concatenate([left, right], 1)

    def mlp_part(l, s=0):
        at = (spot ^ s) * rows
        return jnp.concatenate(
            [lax.dynamic_slice(w, (l, at, 0), (1, rows, w.shape[2]))[0] for w in (w_up, w_down)], 0
        )

    assert layers == 2
    near, far = 1, n_t - 1

    def hand_on(part, step):
        return lax.ppermute(part, "tensor", [(i, (i + step) % n_t) for i in range(n_t)])

    def to_neighbours(part):
        held = [None] * n_t
        held[near], held[far] = hand_on(part, 1), hand_on(part, -1)
        return held

    def passed_on(held):
        for k in range(2, far):
            held[k] = hand_on(held[k - 1], 1)
        return held[1:]

    def slices_of(matrices):
        return Pieces(
            [
                [
                    [(v[k], None, at) if isinstance(v, list) else (v, at + (k,), 0) for v, at in slices]
                    for k in range(n_t - 1)
                ]
                for slices in matrices
            ]
        )

    def core_swap(v):
        return swap(v, 1, n_dp)

    def one_matrix(own, x_piece, y_piece, way):
        own_c, x_c, y_c = core_swap(own), core_swap(x_piece), core_swap(y_piece)
        last = corner(x_piece, y_piece, n_dp, way)
        all_of = [own, own_c, x_piece, x_c, y_piece, y_c, last, core_swap(last)]
        return slices_of([[(v, (0,)) for v in all_of]])

    def two_matrices(own, x_piece, y_piece, token):
        own_c, x_c, y_c = core_swap(own), core_swap(x_piece), core_swap(y_piece)
        first, second = swap(after(x_piece, token)[0], 4, n_dp), swap(after(y_piece, token)[1], 2, n_dp)
        sides = [own, own_c, x_piece, x_c, y_piece, y_c]
        ends = [(first, core_swap(first)), (second, core_swap(second))]
        return slices_of(
            [[(v, (m,)) for v in sides] + [(v, ()) for v in ends[m]] for m in range(2)]
        )

    def two_with_corners(own, x_piece, y_piece, last):
        own_c, x_c, y_c = core_swap(own), core_swap(x_piece), core_swap(y_piece)
        last_c = [core_swap(v) for v in last]
        sides = [own, own_c, x_piece, x_c, y_piece, y_c]
        return slices_of(
            [[(v, (m,)) for v in sides] + [(last, m * rows), (last_c, m * rows)] for m in range(2)]
        )

    def sides_of(own):
        return swap(own, 2, n_dp), swap(own, 4, n_dp)

    def run_attention(l, x, pieces, work):
        return attention_forward(spots, x, gains[l][0], biases[l][0], l, own_attn, pieces, n_t, work)

    def run_feed_forward(l, x, pieces, keep, out_type):
        return mlp_forward(spots, x, gains[l][1], biases[l][1], l, own_mlp, pieces, n_t, keep, out_type)

    part_a, part_m = attn_part(0), mlp_part(0)
    part_l = jnp.concatenate([attn_part(1), mlp_part(1)], 0)
    held_a = to_neighbours(part_a)
    held_m = to_neighbours(after(part_m, (held_a[near], held_a[far])))
    hops_a = passed_on(held_a)
    hops_a[0] = after(hops_a[0], part_m, stream, own_attn)
    (own_a,) = pack(hops_a, 1)
    x_a, y_a = sides_of(own_a)
    held_m[near], held_m[far] = after((held_m[near], held_m[far]), (x_a, y_a))
    attn_pieces = [one_matrix(own_a, *after((x_a, y_a), held_m[near], held_m[far]), False)]
    held_l = to_neighbours(after(part_l, held_m[near], held_m[far]))
    hops_m = passed_on(held_m)
    hops_m[0] = after(hops_m[0], part_l)
    (own_m,) = pack(hops_m, 2)
    x_m, y_m = sides_of(own_m)
    first = run_attention(0, after(stream, own_m), attn_pieces[0], 40_000_000_000)
    first, ((held_l[near], held_l[far]),) = gate(first, (held_l[near], held_l[far]))
    x_m, y_m = after((x_m, y_m), first[0])
    mlp_pieces = [two_matrices(own_m, x_m, y_m, first[0])]
    hops_l = passed_on(held_l)
    own_a, own_m = pack(hops_l, 1, 2)
    held_c = to_neighbours(after(mlp_part(1, 6), hops_l))
    x_a, y_a = sides_of(own_a)
    x_m, y_m = sides_of(own_m)
    second = run_feed_forward(0, after(first[0], own_a), mlp_pieces[0], True, F32)
    second, ((x_a, y_a), held_c) = gate(second, (x_a, y_a), held_c)
    attn_pieces.append(one_matrix(own_a, x_a, y_a, True))
    hops_c = passed_on(held_c)
    third = run_attention(1, second[0], attn_pieces[1], 1_000_000)
    third, ((x_m, y_m), hops_c) = gate(third, (x_m, y_m), hops_c)
    mlp_pieces.append(two_with_corners(own_m, x_m, y_m, hops_c))
    saved = [(stream, *first[1:], first[0], *second[1:]), (second[0], *third[1:], third[0])]

    def put_pairs(held):
        out = jnp.zeros((total_rows, width), F32)
        for k, v in enumerate(held):
            out = lax.dynamic_update_slice(out, v.astype(F32), (((quarter - k) % n_t) * length, 0))
        return out

    place = lax.dynamic_slice_in_dim(positions, quarter, 1, 0)[0]
    cot = lax.dynamic_slice_in_dim(cotangent, quarter, 1, 0)[0]
    pick = (lax.broadcasted_iota(jnp.int32, (1, TOP_ROWS), 1) == place[:, None]).astype(BF16)
    pick = jnp.concatenate([pick, jnp.zeros((SLOT_ROWS - slots, TOP_ROWS), BF16)], 0)
    slot_cot = jnp.concatenate(
        [jnp.where(place[:, None] >= 0, cot, 0), jnp.zeros((SLOT_ROWS - slots, width), BF16)], 0
    )
    incoming = tn(pick, slot_cot)

    everything = tuple(range(n_t))
    halves = (everything[: n_t // 2], everything[n_t // 2 :])
    gain_grads = [[None, None] for _ in range(layers)]
    bias_grads = [[None, None] for _ in range(layers)]
    stream_l, normed, proj, logsum, mixed, middle = saved[top]
    grad_middle, gain_grads[top][1], bias_grads[top][1], slot_rows = top_backward(
        spots, incoming, middle, gains[top][1], biases[top][1], pick, slot_cot, top, own_mlp, mlp_pieces[top], n_t
    )
    all_rows = lax.all_gather(slot_rows, ("dp", "tensor"))
    total, incoming, gain_grads[top][0], bias_grads[top][0], _, *keep, send = attention_backward(
        spots, grad_middle, stream_l, gains[top][0], normed, proj, logsum, mixed, None,
        top, own_attn, attn_pieces[top], everything,
    )
    top_attn = Reduction([(keep, send)], n_dp, n_t)

    (last_stream,) = run_feed_forward(top, after(middle, total), mlp_pieces[top], False, BF16)
    last_stream, (top_attn.got,) = gate(last_stream, top_attn.got)
    hidden_held = to_neighbours(last_stream)
    hidden_held[0] = last_stream
    ready = top_attn.near()

    stream_l, normed, proj, logsum, mixed, middle_l, normed_mlp, upward = saved[0]
    outs = mlp_backward(
        spots, after(incoming, ready), middle_l, gains[0][1], normed_mlp, upward, None,
        0, own_mlp, mlp_pieces[0], everything, True,
    )
    outs, (top_attn.from_near, hidden_held) = gate(outs, top_attn.from_near, hidden_held)
    grad_middle, gain_grads[0][1], bias_grads[0][1], *keep, send = outs[1:]
    low_mlp = Reduction([(keep, send)], n_dp, n_t)
    hidden_held[1:] = passed_on(hidden_held)
    ready = top_attn.far()

    outs = attention_backward(
        spots, after(grad_middle, ready), stream_l, gains[0][0], normed, proj, logsum, mixed, None,
        0, own_attn, attn_pieces[0], halves[0],
    )
    outs, (low_mlp.got, top_attn.from_far, hidden_held) = gate(
        outs, low_mlp.got, top_attn.from_far, hidden_held
    )
    total, *keep, send = outs
    first_half = (keep, send)
    ready = low_mlp.near()
    top_attn.from_far = after(top_attn.from_far, ready)
    ready = top_attn.own(True)

    outs = attention_backward(
        spots, after(grad_middle, ready), stream_l, gains[0][0], normed, proj, logsum, mixed, total,
        0, own_attn, attn_pieces[0], halves[1], BF16,
    )
    outs, (low_mlp.from_near, top_attn.parts) = gate(outs, low_mlp.from_near, top_attn.parts)
    incoming, gain_grads[0][0], bias_grads[0][0], type_grad, *keep, send = outs[1:]
    low_attn = Reduction([after(first_half, send), (keep, send)], n_dp, n_t)
    grad_tokens = lax.all_gather(incoming, "tensor", tiled=True)
    ready = low_mlp.far()
    low_attn.got = after(low_attn.got, ready)
    ready = low_attn.near()

    rows_all = SumAll(
        stack_rows(
            [after(type_grad, ready)]
            + [g for pair in gain_grads for g in pair]
            + [g for pair in bias_grads for g in pair]
        ),
        n_dp,
        n_t,
    )

    def finished(reduction, token):
        return finish(after(reduction.parts, token), n_dp)

    sums = {}
    rows_all.step(ready)
    hidden_out = put_pairs(after(hidden_held, ready))
    rows_all.step(hidden_out)
    low_mlp.from_far = after(low_mlp.from_far, hidden_out)
    ready = low_mlp.own()
    rows_all.step(ready)
    low_attn.from_near = after(low_attn.from_near, rows_all.values)
    ready = low_attn.far()

    all_rows = after(all_rows, ready)
    all_cot = all_rows[:, :SLOT_ROWS].reshape(-1, width)
    all_normed = all_rows[:, SLOT_ROWS:].reshape(-1, width)
    slot_up = nn(all_normed, w_up[top])
    slot_grad = (nt(all_cot, w_down[top]) * gelu_slope(slot_up)).astype(BF16)
    grad_up_top = tn(lax.dynamic_slice_in_dim(all_normed, me * unit, unit, 1), slot_grad)
    grad_down_top = tn(
        gelu(slot_up).astype(BF16), lax.dynamic_slice_in_dim(all_cot, me * unit, unit, 1)
    )
    ready = (grad_up_top, grad_down_top)
    ready, (low_attn.from_far, low_mlp.passed) = gate(ready, low_attn.from_far, low_mlp.passed)
    ready = low_mlp.pass_on()
    low_attn.from_far = after(low_attn.from_far, ready)
    ready = low_attn.own()
    rows_all.step(ready)
    (sums["attn", top],) = finished(top_attn, ready)
    low_attn.passed = after(low_attn.passed, rows_all.got if rows_all.got is not None else ready)
    ready = low_attn.pass_on()
    rows_all.step(ready)
    rows_all = rows_all.result(ready)
    grad_tokens = after(grad_tokens, rows_all).astype(F32)
    sums["down", 0], sums["up", 0] = finished(low_mlp, grad_tokens)
    (sums["attn", 0],) = finished(low_attn, (sums["down", 0], sums["up", 0]))

    rows_mine = lax.dynamic_slice_in_dim(rows_all, me * unit, unit, 1)
    grad_gain = rows_mine[2 : 2 + 2 * layers].reshape(layers, 2, unit)
    grad_bias = rows_mine[2 + 2 * layers : 2 + 4 * layers].reshape(layers, 2, unit)
    grad_qkv = jnp.stack([sums["attn", l][:, : 3 * inner].reshape(unit, 3, inner) for l in range(layers)])
    grad_out = jnp.stack([sums["attn", l][:, 3 * inner :].T for l in range(layers)])
    grad_up = jnp.stack([grad_up_top if l == top else sums["up", l] for l in range(layers)])
    grad_down = jnp.stack([grad_down_top if l == top else sums["down", l].T for l in range(layers)])
    return hidden_out, grad_tokens, rows_mine[:2], grad_gain, grad_bias, grad_qkv, grad_out, grad_up, grad_down


def solution(mesh):
    n_dp, n_t = mesh.shape["dp"], mesh.shape["tensor"]
    placed = (
        P("dp", None),
        P(),
        P(),
        P(),
        P(None, None, None, "tensor"),
        P(None, "tensor", None),
        P(None, None, "tensor"),
        P(None, "tensor", None),
        P("dp", None, None),
        P("dp", None),
    )

    def run(*args):
        return shards(*args, n_dp, n_t)

    return jax.shard_map(
        run,
        mesh=mesh,
        in_specs=placed,
        out_specs=(
            P("dp", None),
            P("dp", None),
            P(None, "dp"),
            P(None, None, "dp"),
            P(None, None, "dp"),
            P(None, "dp", None, "tensor"),
            P(None, "tensor", "dp"),
            P(None, "dp", "tensor"),
            P(None, "tensor", "dp"),
        ),
        check_vma=False,
    )
```

```python
import functools

import jax
import jax.numpy as jnp
from jax import lax
from jax.experimental import pallas as pl
from jax.experimental.pallas import tpu as pltpu
from jax.sharding import PartitionSpec as P

HD = 64
WORDS = 40
TOP_ROWS = 48
SLOT_ROWS = 16
EPSILON = 1e-06
ROOT_HALF = 0.7071067811865476
ROOT_TWO_PI = 2.5066282746310002
GROUP = 8
STEP = 32
SIDES_FIRST = True
F32 = jnp.float32
BF16 = jnp.bfloat16
SMALL_VMEM = 16 * 1024 * 1024
VMEM_BYTES = 60 * 1024 * 1024


def dot(left, right, dims):
    return lax.dot_general(left, right, (dims, ((), ())), preferred_element_type=F32)


def nn(left, right):
    return dot(left, right, ((1,), (0,)))


def nt(left, right):
    return dot(left, right, ((1,), (1,)))


def tn(left, right):
    return dot(left, right, ((0,), (0,)))


def gelu(values):
    return 0.5 * values * (1.0 + lax.erf(values * ROOT_HALF))


def gelu_slope(values):
    return 0.5 * (1.0 + lax.erf(values * ROOT_HALF)) + values * jnp.exp(-0.5 * values * values) / ROOT_TWO_PI


def norm_parts(values):
    average = jnp.mean(values, axis=-1, keepdims=True)
    centred = values - average
    spread = jnp.mean(centred * centred, axis=-1, keepdims=True)
    rate = lax.rsqrt(spread + EPSILON)
    return centred * rate, rate


def norm_rows(source, gain, bias, target):
    step = STEP if source.shape[0] % STEP == 0 else STEP // 2
    for r in range(0, source.shape[0], step):
        rows = slice(r, r + step)
        target[rows, :] = (norm_parts(source[rows, :])[0] * gain[...] + bias[...]).astype(BF16)


def norm_back_rows(rows, values, gain, incoming, gain_grad, bias_grad):
    unit, rate = norm_parts(values[rows, :])
    e = incoming[rows, :]
    scaled = e * gain[...]
    inner = jnp.mean(scaled * unit, axis=-1, keepdims=True)
    gain_grad[...] += jnp.sum(e * unit, axis=0, keepdims=True)
    bias_grad[...] += jnp.sum(e, axis=0, keepdims=True)
    return rate * (scaled - jnp.mean(scaled, axis=-1, keepdims=True) - unit * inner)


def flops(count):
    return pl.CostEstimate(flops=count, bytes_accessed=1_000_000, transcendentals=0)


KERNEL_COST = pl.CostEstimate(flops=40_000_000_000, bytes_accessed=1_000_000, transcendentals=0)
SMALL_COST = pl.CostEstimate(flops=1_000_000_000, bytes_accessed=1_000_000, transcendentals=0)


class Pieces:
    def __init__(self, at):
        self.arrays = []
        self.plan = []
        for matrix in at:
            for k, slices in enumerate(matrix, 1):
                for s, (array, lead, row) in enumerate(slices):
                    found = [i for i, v in enumerate(self.arrays) if v is array]
                    if not found:
                        self.arrays.append(array)
                        found = [len(self.arrays) - 1]
                    self.plan.append((len(self.plan) // (len(matrix) * GROUP), k, s, found[0], lead, row))


def fetch(spot, layer, own, plan, sources, scratches, sems, quarters):
    rows = scratches[0].shape[1] // GROUP
    for k in quarters:
        for m, scratch in enumerate(scratches):
            if k == 0 and own:
                pltpu.make_async_copy(own[m].at[layer], scratch.at[0], sems.at[0]).start()
        for m, at_k, s, which, lead, row in plan:
            if at_k == k:
                source = sources[which] if lead is None else sources[which].at[lead]
                at = pl.multiple_of((spot ^ s) * rows, rows)
                pltpu.make_async_copy(
                    source.at[pl.ds(row, rows)],
                    scratches[m].at[k - quarters[0], pl.ds(at, rows)],
                    sems.at[k - quarters[0]],
                ).start()


def arrived(k, scratches, sems):
    for scratch in scratches:
        pltpu.make_async_copy(scratch.at[k], scratch.at[k], sems.at[k]).wait()


def own_copies(layer, own_qkv, own_out, raw_qkv, raw_out, sem):
    return [
        pltpu.make_async_copy(own_qkv.at[layer], raw_qkv, sem),
        pltpu.make_async_copy(own_out.at[layer], raw_out, sem),
    ]


def own_block(copies, raw_qkv, raw_out, block):
    for copy in copies:
        copy.wait()
    inner = raw_qkv.shape[2]
    for c in range(3):
        block[0, :, c * inner : (c + 1) * inner] = raw_qkv[c]
    block[0, :, 3 * inner :] = raw_out[...].astype(F32).T.astype(BF16)


def flip(spot, source, target):
    width = source.shape[1]
    rows = width // GROUP
    turned = source.astype(F32).T.astype(BF16)
    for j in range(GROUP):
        s = spot ^ j
        at = pl.multiple_of(((s & 1) * (GROUP // 2) + (s >> 1)) * rows, rows)
        target[pl.ds(at, rows), :] = turned[j * rows : (j + 1) * rows, :]


def put_block(block, keep, send, part, columns=slice(None)):
    half = block.shape[0] // 2
    rows = half // (GROUP // 2)
    for i in range(GROUP // 2):
        keep[i][0, part, :, columns] = block[i * rows : (i + 1) * rows].astype(BF16)
        send[i, 0, part, :, columns] = block[half + i * rows : half + (i + 1) * rows].astype(BF16)


def any_spec():
    return pl.BlockSpec(memory_space=pl.ANY)


def smem_spec():
    return pl.BlockSpec(memory_space=pltpu.SMEM)


def whole(shape):
    return pl.BlockSpec(shape, lambda k: (0,) * len(shape))


def per_quarter(shape, first=0):
    return pl.BlockSpec((1,) + shape, lambda k: (first + k,) + (0,) * len(shape))


def block_specs(matrices, rows, width):
    own = pl.BlockSpec((1, matrices, rows, width), lambda k: (k, 0, 0, 0))
    return [own] * (GROUP // 2) + [
        pl.BlockSpec((GROUP // 2, 1, matrices, rows, width), lambda k: (0, k, 0, 0, 0))
    ]


def block_shapes(quarters, matrices, rows, width):
    own = jax.ShapeDtypeStruct((quarters, matrices, rows, width), BF16)
    return [own] * (GROUP // 2) + [jax.ShapeDtypeStruct((GROUP // 2, quarters, matrices, rows, width), BF16)]


def params(limit=VMEM_BYTES):
    return pltpu.CompilerParams(vmem_limit_bytes=limit)


def cost(flops, moved):
    return pl.CostEstimate(flops=flops, bytes_accessed=moved, transcendentals=0)


def attention_forward_kernel(layer, plan, count, spot_ref, x, gain, bias, own_qkv, own_out, *rest):
    middle, normed, proj, logsum, mixed, block, sems, raw_qkv, raw_out = rest[count:]
    k = pl.program_id(0)
    inner = raw_out.shape[0]
    heads = inner // HD

    @pl.when(k == 0)
    def _():
        copies = own_copies(layer, own_qkv, own_out, raw_qkv, raw_out, sems.at[0])
        for copy in copies:
            copy.start()
        fetch(spot_ref[0], layer, [], plan, rest[:count], [block], sems, range(block.shape[0]))
        norm_rows(x, gain, bias, normed)
        middle[...] = x[...]
        logsum[...] = jnp.zeros_like(logsum)
        own_block(copies, raw_qkv, raw_out, block)

    @pl.when(k > 0)
    def _():
        arrived(k, [block], sems)

    proj[0] = nn(normed[...], block[k])[:, : 3 * inner].astype(BF16)
    lane = lax.broadcasted_iota(jnp.int32, logsum.shape, 1)
    every = range(heads)
    lanes = [slice(h * HD, (h + 1) * HD) for h in range(3 * heads)]
    scores = [
        nt(proj[0, :, lanes[h]] * jnp.asarray(HD**-0.5, BF16), proj[0, :, lanes[heads + h]]) for h in every
    ]
    tops = [jnp.max(v, axis=-1, keepdims=True) for v in scores]
    powers = [jnp.exp(v - t) for v, t in zip(scores, tops)]
    totals = [jnp.sum(v, axis=-1, keepdims=True) for v in powers]
    kept = logsum[...]
    for h in every:
        kept = jnp.where(lane == k * heads + h, tops[h] + jnp.log(totals[h]), kept)
    logsum[...] = kept
    weights = [(v * (1.0 / t)).astype(BF16) for v, t in zip(powers, totals)]
    mixes = [nn(weights[h], proj[0, :, lanes[2 * heads + h]]).astype(BF16) for h in every]
    pad = mixed.shape[2] - inner
    mixed[0] = jnp.concatenate([jnp.zeros((normed.shape[0], pad), BF16)] + mixes, 1)
    middle[...] += nt(mixed[0], block[k, :, 3 * inner - pad :]).astype(BF16).astype(F32)


def attention_forward(spot, x, gain, bias, layer, own, pieces, n_t, work):
    length, width = x.shape
    inner = own[1].shape[1]
    count = len(pieces.arrays)
    out = [
        jax.ShapeDtypeStruct((length, width), F32),
        jax.ShapeDtypeStruct((length, width), BF16),
        jax.ShapeDtypeStruct((n_t, length, 3 * inner), BF16),
        jax.ShapeDtypeStruct((length, 128), F32),
        jax.ShapeDtypeStruct((n_t, length, inner + inner % 128), BF16),
    ]
    return pl.pallas_call(
        functools.partial(attention_forward_kernel, layer, pieces.plan, count),
        grid=(n_t,),
        out_shape=out,
        in_specs=[smem_spec(), whole((length, width)), whole((1, width)), whole((1, width))] + [any_spec()] * (2 + count),
        out_specs=[
            whole((length, width)),
            whole((length, width)),
            per_quarter((length, 3 * inner)),
            whole((length, 128)),
            per_quarter((length, inner + inner % 128)),
        ],
        scratch_shapes=[
            pltpu.VMEM((n_t, width, 4 * inner), BF16),
            pltpu.SemaphoreType.DMA((n_t,)),
            pltpu.VMEM((3, width, inner), BF16),
            pltpu.VMEM((inner, width), BF16),
        ],
        compiler_params=params(),
        cost_estimate=flops(work),
        name="attention_forward",
    )(spot, x, gain, bias, *own, *pieces.arrays)


def mlp_forward_kernel(kept_rows, layer, plan, count, spot_ref, x, gain, bias, own_up, own_down, *rest):
    if kept_rows:
        out, normed, upward, ups, downs, total, sems = rest[count:]
    else:
        out, ups, downs, total, sems, normed = rest[count:]
    k = pl.program_id(0)

    @pl.when(k == 0)
    def _():
        fetch(spot_ref[0], layer, [own_up, own_down], plan, rest[:count], [ups, downs], sems, range(ups.shape[0]))
        norm_rows(x, gain, bias, normed)
        total[...] = x[...]

    arrived(k, [ups, downs], sems)
    up = nn(normed[...], ups[k])
    if kept_rows:
        upward[0] = up
    active = gelu(up).astype(BF16)
    total[...] += nn(active, downs[k]).astype(BF16).astype(F32)

    @pl.when(k == pl.num_programs(0) - 1)
    def _():
        out[...] = total[...].astype(out.dtype)


def mlp_forward(spot, x, gain, bias, layer, own, pieces, n_t, kept_rows, out_type):
    length, width = x.shape
    hidden = own[0].shape[2]
    count = len(pieces.arrays)
    out = [jax.ShapeDtypeStruct((length, width), out_type)]
    out_specs = [whole((length, width))]
    scratch = []
    if kept_rows:
        out += [jax.ShapeDtypeStruct((length, width), BF16), jax.ShapeDtypeStruct((n_t, length, hidden), F32)]
        out_specs += [whole((length, width)), per_quarter((length, hidden))]
    else:
        scratch.append(pltpu.VMEM((length, width), BF16))
    return pl.pallas_call(
        functools.partial(mlp_forward_kernel, kept_rows, layer, pieces.plan, count),
        grid=(n_t,),
        out_shape=out,
        in_specs=[smem_spec(), whole((length, width)), whole((1, width)), whole((1, width))]
        + [any_spec()] * (2 + count),
        out_specs=out_specs,
        scratch_shapes=[
            pltpu.VMEM((n_t,) + own[0].shape[1:], BF16),
            pltpu.VMEM((n_t,) + own[1].shape[1:], BF16),
            pltpu.VMEM((length, width), F32),
            pltpu.SemaphoreType.DMA((n_t,)),
        ]
        + scratch,
        compiler_params=params(),
        cost_estimate=KERNEL_COST,
        name="mlp_forward",
    )(spot, x, gain, bias, *own, *pieces.arrays)


def mlp_backward_kernel(quarters, last, blocks, layer, plan, count, spot_ref, incoming, x, gain, normed, upward, total_in, *rest):
    own, sources = rest[:2], rest[2 : 2 + count]
    rest = list(rest[2 + count :])
    total = rest.pop(0)
    if last:
        grad, gain_grad, bias_grad = (rest.pop(0) for _ in range(3))
    if blocks:
        keep, send = [rest.pop(0) for _ in range(GROUP // 2)], rest.pop(0)
    ups, downs, sems, *flipped = rest
    k = pl.program_id(0)

    @pl.when(k == 0)
    def _():
        fetch(spot_ref[0], layer, own, plan, sources, [ups, downs], sems, quarters)
        total[...] = jnp.zeros_like(total) if quarters[0] == 0 else total_in[...]
        if blocks:
            flip(spot_ref[0], incoming[...], flipped[0])
            flip(spot_ref[0], normed[...], flipped[1])

    arrived(k, [ups, downs], sems)
    up = upward[0]
    grad_active = nt(incoming[...].astype(BF16), downs[k])
    bell = 0.5 * (1.0 + lax.erf(up * ROOT_HALF))
    grad_up = (grad_active * (bell + up * jnp.exp(-0.5 * up * up) * (1.0 / ROOT_TWO_PI))).astype(BF16)
    total[...] += nt(grad_up, ups[k])
    if blocks:
        put_block(nn(flipped[0][...], (up * bell).astype(BF16)), keep, send, 0)
        put_block(nn(flipped[1][...], grad_up), keep, send, 1)

    if last:

        @pl.when(k == pl.num_programs(0) - 1)
        def _():
            gain_grad[...] = jnp.zeros_like(gain_grad)
            bias_grad[...] = jnp.zeros_like(bias_grad)
            for r in range(0, x.shape[0], 16):
                rows = slice(r, r + 16)
                grad[rows, :] = incoming[rows, :] + norm_back_rows(rows, x, gain, total, gain_grad, bias_grad)


def mlp_backward(spot, incoming, x, gain, normed, upward, total, layer, own, pieces, quarters, blocks):
    length, width = incoming.shape
    n_t, hidden = upward.shape[0], upward.shape[2]
    last = quarters[-1] == n_t - 1
    count = len(quarters)
    if total is None:
        total = gain
    out = [jax.ShapeDtypeStruct((length, width), F32)]
    out_specs = [whole((length, width))]
    if last:
        out += [jax.ShapeDtypeStruct(v, F32) for v in ((length, width), (1, width), (1, width))]
        out_specs += [whole((length, width)), whole((1, width)), whole((1, width))]
    scratch = [
        pltpu.VMEM((count,) + own[0].shape[1:], BF16),
        pltpu.VMEM((count,) + own[1].shape[1:], BF16),
        pltpu.SemaphoreType.DMA((count,)),
    ]
    if blocks:
        out += block_shapes(count, 2, width // GROUP, hidden)
        out_specs += block_specs(2, width // GROUP, hidden)
        scratch += [pltpu.VMEM((width, length), BF16)] * 2
    return pl.pallas_call(
        functools.partial(mlp_backward_kernel, quarters, last, blocks, layer, pieces.plan, len(pieces.arrays)),
        grid=(count,),
        out_shape=out,
        in_specs=[
            smem_spec(),
            whole((length, width)),
            whole((length, width)),
            whole((1, width)),
            whole((length, width)),
            per_quarter((length, hidden), quarters[0]),
            whole(total.shape),
        ]
        + [any_spec()] * (2 + len(pieces.arrays)),
        out_specs=out_specs,
        scratch_shapes=scratch,
        compiler_params=params(),
        cost_estimate=KERNEL_COST,
        name="mlp_backward",
    )(spot, incoming, x, gain, normed, upward, total, *own, *pieces.arrays)


def top_kernel(layer, plan, count, spot_ref, incoming, x, gain, bias, pick, slots, own_up, own_down, *rest):
    grad, gain_grad, bias_grad, packed, ups, downs, total, sems, normed = rest[count:]
    k = pl.program_id(0)

    @pl.when(k == 0)
    def _():
        fetch(spot_ref[0], layer, [own_up, own_down], plan, rest[:count], [ups, downs], sems, range(ups.shape[0]))
        norm_rows(x, gain, bias, normed)
        total[...] = jnp.zeros_like(total)
        packed[:SLOT_ROWS, :] = slots[...]
        packed[SLOT_ROWS:, :] = nn(pick[...], normed[...]).astype(BF16)

    arrived(k, [ups, downs], sems)
    up = nn(normed[...], ups[k])
    grad_up = (nt(incoming[...].astype(BF16), downs[k]) * gelu_slope(up)).astype(BF16)
    total[...] += nt(grad_up, ups[k])

    @pl.when(k == pl.num_programs(0) - 1)
    def _():
        gain_grad[...] = jnp.zeros_like(gain_grad)
        bias_grad[...] = jnp.zeros_like(bias_grad)
        for r in range(0, incoming.shape[0], 16):
            rows = slice(r, r + 16)
            grad[rows, :] = incoming[rows, :] + norm_back_rows(rows, x, gain, total, gain_grad, bias_grad)


def top_backward(spot, incoming, x, gain, bias, pick, slots, layer, own, pieces, n_t):
    length, width = incoming.shape
    rows = pl.BlockSpec((length, width), lambda k: (0, 0))
    row = whole((1, width))
    return pl.pallas_call(
        functools.partial(top_kernel, layer, pieces.plan, len(pieces.arrays)),
        grid=(n_t,),
        out_shape=[
            jax.ShapeDtypeStruct((length, width), F32),
            jax.ShapeDtypeStruct((1, width), F32),
            jax.ShapeDtypeStruct((1, width), F32),
            jax.ShapeDtypeStruct((2 * SLOT_ROWS, width), BF16),
        ],
        in_specs=[smem_spec(), rows, rows, row, row, whole(pick.shape), whole(slots.shape)] + [any_spec()] * (2 + len(pieces.arrays)),
        out_specs=[rows, row, row, whole((2 * SLOT_ROWS, width))],
        scratch_shapes=[
            pltpu.VMEM((n_t,) + own[0].shape[1:], BF16),
            pltpu.VMEM((n_t,) + own[1].shape[1:], BF16),
            pltpu.VMEM((length, width), F32),
            pltpu.SemaphoreType.DMA((n_t,)),
            pltpu.VMEM((length, width), BF16),
        ],
        compiler_params=params(),
        cost_estimate=KERNEL_COST,
        name="top_backward",
    )(spot, incoming, x, gain, bias, pick, slots, *own, *pieces.arrays)


def attention_backward_kernel(
    quarters, last, layer, plan, count, spot_ref, incoming, x, gain, normed, proj, logsum, mixed, total_in, own_qkv, own_out, *rest
):
    sources = rest[:count]
    rest = list(rest[count:])
    total = rest.pop(0)
    if last:
        grad, gain_grad, bias_grad, types = (rest.pop(0) for _ in range(4))
    keep = [rest.pop(0) for _ in range(GROUP // 2)]
    send, block, grad_proj, sems, low_t, normed_t, raw_qkv, raw_out = rest
    k = pl.program_id(0)
    top = incoming.shape[0]
    inner = raw_out.shape[0]
    heads = inner // HD

    @pl.when(k == 0)
    def _():
        if quarters[0] == 0:
            copies = own_copies(layer, own_qkv, own_out, raw_qkv, raw_out, sems.at[0])
            for copy in copies:
                copy.start()
        fetch(spot_ref[0], layer, [], plan, sources, [block], sems, quarters)
        total[...] = jnp.zeros_like(total) if quarters[0] == 0 else total_in[...]
        grad_proj[...] = jnp.zeros_like(grad_proj)
        flip(spot_ref[0], incoming[...], low_t)
        flip(spot_ref[0], normed[...], normed_t)
        if quarters[0] == 0:
            own_block(copies, raw_qkv, raw_out, block)

    @pl.when(quarters[0] + k > 0)
    def _():
        arrived(k, [block], sems)

    pad = mixed.shape[2] - inner
    grad_mixed = nn(incoming[...].astype(BF16), block[k, :, 3 * inner - pad :]).astype(BF16)
    lane = lax.broadcasted_iota(jnp.int32, (top, 128), 1)
    every = range(heads)
    lanes = [slice(h * HD, (h + 1) * HD) for h in range(3 * heads)]
    queries = [proj[0, :top, lanes[h]] * jnp.asarray(HD**-0.5, BF16) for h in every]
    keys = [proj[0, :, lanes[heads + h]] for h in every]
    head_grads = [grad_mixed[:, pad + h * HD : pad + (h + 1) * HD] for h in every]
    scores = [nt(queries[h], keys[h]) for h in every]
    grad_weights = [nt(head_grads[h], proj[0, :, lanes[2 * heads + h]]) for h in every]
    row_sums = [
        jnp.sum(
            jnp.where(lane == (quarters[0] + k) * heads + h, logsum[:top, :], 0.0), axis=-1, keepdims=True
        )
        for h in every
    ]
    weights = [jnp.exp(scores[h] - row_sums[h]) for h in every]
    for h in every:
        grad_proj[:, lanes[2 * heads + h]] = tn(weights[h].astype(BF16), head_grads[h]).astype(BF16)
    inner_sums = [jnp.sum(weights[h] * grad_weights[h], axis=-1, keepdims=True) for h in every]
    grad_scores = [(weights[h] * (grad_weights[h] - inner_sums[h])).astype(BF16) for h in every]
    for h in every:
        grad_proj[:top, lanes[h]] = (nn(grad_scores[h], keys[h]) * HD**-0.5).astype(BF16)
        grad_proj[:, lanes[heads + h]] = tn(grad_scores[h], queries[h]).astype(BF16)
    wide = grad_proj.shape[1]
    total[...] += nt(grad_proj[...], block[k, :, :wide])
    left = nn(normed_t[...], grad_proj[...])
    right = nn(low_t[...], mixed[0, :top, :])
    at = 3 * inner - pad
    put_block(left[:, :at], keep, send, 0, slice(0, at))
    put_block(left[:, at:] + right[:, : wide - at], keep, send, 0, slice(at, wide))
    put_block(right[:, wide - at :], keep, send, 0, slice(wide, 4 * inner))

    if last:

        @pl.when(k == pl.num_programs(0) - 1)
        def _():
            gain_grad[...] = jnp.zeros_like(gain_grad)
            bias_grad[...] = jnp.zeros_like(bias_grad)
            types[...] = jnp.zeros_like(types)
            step = 8
            for r in range(0, x.shape[0], step):
                rows = slice(r, r + step)
                back = norm_back_rows(rows, x, gain, total, gain_grad, bias_grad)
                if r < top:
                    back = back + incoming[rows, :]
                grad[rows, :] = back.astype(grad.dtype)
                which = slice(0, 1) if r < WORDS else slice(1, 2)
                types[which, :] += jnp.sum(back, axis=0, keepdims=True)


def attention_backward(
    spot, incoming, x, gain, normed, proj, logsum, mixed, total, layer, own, pieces, quarters, out_type=F32
):
    length, width = x.shape
    top = incoming.shape[0]
    n_t = proj.shape[0]
    last = quarters[-1] == n_t - 1
    count = len(quarters)
    inner = own[1].shape[1]
    if total is None:
        total = gain
    out = [jax.ShapeDtypeStruct((length, width), F32)]
    out_specs = [whole((length, width))]
    if last:
        out.append(jax.ShapeDtypeStruct((length, width), out_type))
        out += [jax.ShapeDtypeStruct(v, F32) for v in ((1, width), (1, width), (2, width))]
        out_specs += [whole(v.shape) for v in out[1:]]
    out += block_shapes(count, 1, width // GROUP, 4 * inner)
    out_specs += block_specs(1, width // GROUP, 4 * inner)
    return pl.pallas_call(
        functools.partial(attention_backward_kernel, quarters, last, layer, pieces.plan, len(pieces.arrays)),
        grid=(count,),
        out_shape=out,
        in_specs=[
            smem_spec(),
            whole((top, width)),
            whole((length, width)),
            whole((1, width)),
            whole((length, width)),
            per_quarter((length, 3 * inner), quarters[0]),
            whole((length, 128)),
            per_quarter((length, inner + inner % 128), quarters[0]),
            whole(total.shape),
        ]
        + [any_spec()] * (2 + len(pieces.arrays)),
        out_specs=out_specs,
        scratch_shapes=[
            pltpu.VMEM((count, width, 4 * inner), BF16),
            pltpu.VMEM((length, 3 * inner + (3 * inner) % 128), BF16),
            pltpu.SemaphoreType.DMA((count,)),
            pltpu.VMEM((width, top), BF16),
            pltpu.VMEM((width, length), BF16),
            pltpu.VMEM((3, width, inner), BF16),
            pltpu.VMEM((inner, width), BF16),
        ],
        compiler_params=params(),
        cost_estimate=KERNEL_COST,
        name="attention_backward",
    )(spot, incoming, x, gain, normed, proj, logsum, mixed, total, *own, *pieces.arrays)


def swap(values, bit, size):
    return lax.ppermute(values, "dp", [(i, i ^ bit) for i in range(size)])


def after(values, *others):
    return lax.optimization_barrier((values, others))[0]


def gate(outs, *others):
    return lax.optimization_barrier((outs, others))


def small_call(kernel, grid, in_specs, out_specs, out_shape, name):
    return pl.pallas_call(
        kernel,
        grid=grid,
        in_specs=in_specs,
        out_specs=out_specs,
        out_shape=out_shape,
        compiler_params=params(SMALL_VMEM),
        cost_estimate=SMALL_COST,
        name=name,
    )


def pack_kernel(groups, *refs):
    sources, targets = refs[: -len(groups)], refs[-len(groups) :]
    rows = targets[0].shape[2]
    for k, source in enumerate(sources):
        for target, (first, count) in zip(targets, groups):
            for m in range(count):
                target[m, k] = source[(first + m) * rows : (first + m + 1) * rows, :]


def pack(sources, *counts):
    total, width = sources[0].shape
    rows = total // sum(counts)
    groups = [(sum(counts[:i]), count) for i, count in enumerate(counts)]
    shapes = [(count, len(sources), rows, width) for count in counts]
    return small_call(
        functools.partial(pack_kernel, groups),
        (1,),
        [whole((total, width))] * len(sources),
        [whole(shape) for shape in shapes],
        [jax.ShapeDtypeStruct(shape, BF16) for shape in shapes],
        "pack",
    )(*sources)


def corner(x_piece, y_piece, n_dp, by_x):
    return swap(y_piece, 2, n_dp) if by_x else swap(x_piece, 4, n_dp)


def near_kernel(*refs):
    *operands, x_out, y_out = refs
    for out, four in ((x_out, operands[:4]), (y_out, operands[4:])):
        for i in range(2):
            out[i] = (four[2 * i][...].astype(F32) + four[2 * i + 1][0].astype(F32)).astype(BF16)


def far_kernel(*refs):
    *operands, x_out, y_out = refs
    for out, (kept, got, near) in ((x_out, operands[:3]), (y_out, operands[3:])):
        out[...] = (kept[...].astype(F32) + got[0].astype(F32) + near[0].astype(F32)).astype(BF16)


def own_kernel(*refs):
    operands, outs = refs[:8], refs[8:]
    half = len(outs) // 2
    for i, out in enumerate(outs):
        kept, got, near, far = operands[4 * (i // half) : 4 * (i // half) + 4]
        j = i % half
        total = kept[j].astype(F32) + got[0, j].astype(F32) + near[0, j].astype(F32) + far[j].astype(F32)
        out[0] = total.astype(out.dtype)


def rows_kernel(*refs):
    *sources, target = refs
    target[...] = jnp.zeros_like(target)
    at = 0
    for source in sources:
        count = source.shape[0]
        target[at : at + count, :] = source[...]
        at += count


def stack_rows(sources):
    width = sources[0].shape[1]
    count = -(-sum(v.shape[0] for v in sources) // 8) * 8
    return small_call(
        rows_kernel,
        (1,),
        [whole(v.shape) for v in sources],
        whole((count, width)),
        jax.ShapeDtypeStruct((count, width), F32),
        "stack_rows",
    )(*sources)


def relay_kernel(first, second, out):
    out[...] = (first[...].astype(F32) + second[...].astype(F32)).astype(BF16)


def last_kernel(*refs):
    *parts, out = refs
    total = parts[0][...].astype(F32)
    for part in parts[1:]:
        total = total + part[...].astype(F32)
    out[...] = total


class Reduction:
    def __init__(self, blocks, n_dp, n_t):
        self.keep, self.got = [], []
        self.n_dp, self.n_t = n_dp, n_t
        self.half = n_t // 2
        for keep, send in blocks:
            self.add(keep, send)
        self.shape = self.keep[0][0].shape[1:]
        self.zeros = (0,) * len(self.shape)

    def add(self, keep, send):
        self.keep.append(keep)
        self.got.append(swap(send, 1, self.n_dp))

    def pair(self, plane, half):
        n = len(self.keep)
        at = half // n
        specs = [
            pl.BlockSpec((self.half,) + self.shape, lambda _: (at,) + self.zeros),
            pl.BlockSpec((1, self.half) + self.shape, lambda _: (plane, at) + self.zeros),
        ]
        return list(zip([self.keep[half % n][plane], self.got[half % n]], specs))

    def call(self, kernel, operands, shapes, name):
        return small_call(
            kernel,
            (1,),
            [spec for _, spec in operands],
            [whole(v.shape) for v in shapes],
            shapes,
            name,
        )(*[v for v, _ in operands])

    def near(self):
        shape = jax.ShapeDtypeStruct((2, self.half) + self.shape, BF16)
        x, y = self.call(
            near_kernel,
            self.pair(1, 0) + self.pair(3, 0) + self.pair(2, 1) + self.pair(3, 1),
            [shape, shape],
            "near_sum",
        )
        self.from_near = [swap(x, 2, self.n_dp), swap(y, 4, self.n_dp)]
        return [x, y]

    def came(self, half, i):
        spec = pl.BlockSpec((1, self.half) + self.shape, lambda _: (i, 0) + self.zeros)
        return [(self.from_near[half], spec)]

    def far(self):
        shape = jax.ShapeDtypeStruct((self.half,) + self.shape, BF16)
        x, y = self.call(
            far_kernel,
            self.pair(2, 0) + self.came(0, 1) + self.pair(1, 1) + self.came(1, 1),
            [shape, shape],
            "far_sum",
        )
        self.from_far = [swap(x, 4, self.n_dp), swap(y, 2, self.n_dp)]
        return [x, y]

    def own(self, all_at_once=False):
        full = whole((self.half,) + self.shape)
        outs = self.call(
            own_kernel,
            [v for i in range(2) for v in self.pair(0, i) + self.came(i, 0) + [(self.from_far[i], full)]],
            [jax.ShapeDtypeStruct((1,) + self.shape, BF16 if k else F32) for k in range(self.n_t)],
            "own_sum",
        )
        if all_at_once:
            self.parts = [self.along(v, -k) if k else v for k, v in enumerate(outs)]
        else:
            self.waiting = outs[1]
            self.passed = self.along(outs[2], -1)
            self.parts = [outs[0], self.along(outs[3], 1)]
        return list(outs)

    def along(self, part, step):
        return lax.ppermute(part, "tensor", [(j, (j + step) % self.n_t) for j in range(self.n_t)])

    def pass_on(self):
        full = whole(self.waiting.shape)
        (out,) = self.call(
            relay_kernel,
            [(self.waiting, full), (self.passed, full)],
            [jax.ShapeDtypeStruct(self.waiting.shape, BF16)],
            "relay_sum",
        )
        self.parts.append(self.along(out, -1))
        return out


def finish(parts, n_dp):
    shape = parts[0].shape
    total = small_call(
        last_kernel, (1,), [whole(shape)] * len(parts), whole(shape), jax.ShapeDtypeStruct(shape, F32), "last_sum"
    )(*parts)
    return [spread_rows(total[0, m], n_dp) for m in range(shape[1])]


def spread_rows(total, n_dp):
    groups = n_dp // GROUP
    me = lax.axis_index("dp")
    rows = total.shape[0]
    bit = n_dp // 2
    while bit >= GROUP:
        rows //= 2
        second = (me // bit) % 2
        kept = lax.dynamic_slice_in_dim(total, second * rows, rows, 0)
        sent = lax.dynamic_slice_in_dim(total, (1 - second) * rows, rows, 0)
        total = kept + swap(sent, bit, n_dp)
        bit //= 2
    if groups > 1:
        total = lax.ppermute(
            total, "dp", [(h * GROUP + s, s * groups + h) for h in range(groups) for s in range(GROUP)]
        )
    return total


class SumAll:
    def __init__(self, values, n_dp, n_t):
        self.values, self.n_dp, self.n_t = values, n_dp, n_t
        self.bits = [("tensor", 1 << i) for i in range(n_t.bit_length() - 1)]
        self.bits += [("dp", 1 << i) for i in range(n_dp.bit_length() - 1)]
        self.got = None

    def step(self, token):
        if self.got is not None:
            self.values = self.values + after(self.got, token)
            self.got = None
        if self.bits:
            axis, bit = self.bits.pop(0)
            size = self.n_dp if axis == "dp" else self.n_t
            self.got = lax.ppermute(after(self.values, token), axis, [(i, i ^ bit) for i in range(size)])

    def result(self, token):
        while self.got is not None:
            self.step(token)
        return self.values


def shards(tokens, type_table, norm_gain, norm_bias, w_qkv, w_out, w_up, w_down, cotangent, positions, n_dp, n_t):
    total_rows, width = tokens.shape
    pair_count, slots = positions.shape
    assert pair_count == n_t
    length = total_rows // pair_count
    layers = w_qkv.shape[0]
    top = layers - 1
    inner = w_qkv.shape[3]
    me, quarter = lax.axis_index("dp"), lax.axis_index("tensor")
    rows = width // GROUP
    unit = width // n_dp
    spot = me % GROUP
    spots = jnp.reshape(spot, (1,)).astype(jnp.int32)

    def part_of(block):
        return lax.dynamic_slice_in_dim(block, spot * rows, rows, 0)

    mine = lax.dynamic_slice_in_dim(tokens, quarter * length, length, 0).astype(F32)
    row_ids = lax.broadcasted_iota(jnp.int32, (length, 1), 0)
    stream = mine + jnp.where(row_ids < WORDS, type_table[0], type_table[1])
    gains = [[norm_gain[l, i][None] for i in range(2)] for l in range(layers)]
    biases = [[norm_bias[l, i][None] for i in range(2)] for l in range(layers)]
    own_attn = (w_qkv.transpose(0, 2, 1, 3), w_out)
    own_mlp = (w_up, w_down)

    def attn_part(l):
        at = spot * rows
        left = lax.dynamic_slice(w_qkv, (l, at, 0, 0), (1, rows, 3, inner)).reshape(rows, 3 * inner)
        right = lax.dynamic_slice(w_out, (l, 0, at), (1, inner, rows))[0].T
        return jnp.concatenate([left, right], 1)

    def mlp_part(l, s=0):
        at = (spot ^ s) * rows
        return jnp.concatenate(
            [lax.dynamic_slice(w, (l, at, 0), (1, rows, w.shape[2]))[0] for w in (w_up, w_down)], 0
        )

    assert layers == 2
    near, far = 1, n_t - 1

    def hand_on(part, step):
        return lax.ppermute(part, "tensor", [(i, (i + step) % n_t) for i in range(n_t)])

    def to_neighbours(part):
        held = [None] * n_t
        held[near], held[far] = hand_on(part, 1), hand_on(part, -1)
        return held

    def passed_on(held):
        for k in range(2, far):
            held[k] = hand_on(held[k - 1], 1)
        return held[1:]

    def slices_of(matrices):
        return Pieces(
            [
                [
                    [(v[k], None, at) if isinstance(v, list) else (v, at + (k,), 0) for v, at in slices]
                    for k in range(n_t - 1)
                ]
                for slices in matrices
            ]
        )

    def core_swap(v):
        return swap(v, 1, n_dp)

    def one_matrix(own, x_piece, y_piece, way):
        own_c, x_c, y_c = core_swap(own), core_swap(x_piece), core_swap(y_piece)
        last = corner(x_piece, y_piece, n_dp, way)
        all_of = [own, own_c, x_piece, x_c, y_piece, y_c, last, core_swap(last)]
        return slices_of([[(v, (0,)) for v in all_of]])

    def two_matrices(own, x_piece, y_piece, token):
        own_c, x_c, y_c = core_swap(own), core_swap(x_piece), core_swap(y_piece)
        first, second = swap(after(x_piece, token)[0], 4, n_dp), swap(after(y_piece, token)[1], 2, n_dp)
        sides = [own, own_c, x_piece, x_c, y_piece, y_c]
        ends = [(first, core_swap(first)), (second, core_swap(second))]
        return slices_of(
            [[(v, (m,)) for v in sides] + [(v, ()) for v in ends[m]] for m in range(2)]
        )

    def two_with_corners(own, x_piece, y_piece, last):
        own_c, x_c, y_c = core_swap(own), core_swap(x_piece), core_swap(y_piece)
        last_c = [core_swap(v) for v in last]
        sides = [own, own_c, x_piece, x_c, y_piece, y_c]
        return slices_of(
            [[(v, (m,)) for v in sides] + [(last, m * rows), (last_c, m * rows)] for m in range(2)]
        )

    def sides_of(own):
        return swap(own, 2, n_dp), swap(own, 4, n_dp)

    def run_attention(l, x, pieces, work):
        return attention_forward(spots, x, gains[l][0], biases[l][0], l, own_attn, pieces, n_t, work)

    def run_feed_forward(l, x, pieces, keep, out_type):
        return mlp_forward(spots, x, gains[l][1], biases[l][1], l, own_mlp, pieces, n_t, keep, out_type)

    part_a, part_m = attn_part(0), mlp_part(0)
    part_l = jnp.concatenate([attn_part(1), mlp_part(1)], 0)
    held_a = to_neighbours(part_a)
    held_m = to_neighbours(after(part_m, (held_a[near], held_a[far])))
    hops_a = passed_on(held_a)
    hops_a[0] = after(hops_a[0], part_m, stream, own_attn)
    (own_a,) = pack(hops_a, 1)
    x_a, y_a = sides_of(own_a)
    held_m[near], held_m[far] = after((held_m[near], held_m[far]), (x_a, y_a))
    attn_pieces = [one_matrix(own_a, *after((x_a, y_a), held_m[near], held_m[far]), False)]
    held_l = to_neighbours(after(part_l, held_m[near], held_m[far]))
    hops_m = passed_on(held_m)
    hops_m[0] = after(hops_m[0], part_l)
    (own_m,) = pack(hops_m, 2)
    x_m, y_m = sides_of(own_m)
    first = run_attention(0, after(stream, own_m), attn_pieces[0], 40_000_000_000)
    first, ((held_l[near], held_l[far]),) = gate(first, (held_l[near], held_l[far]))
    x_m, y_m = after((x_m, y_m), first[0])
    mlp_pieces = [two_matrices(own_m, x_m, y_m, first[0])]
    hops_l = passed_on(held_l)
    own_a, own_m = pack(hops_l, 1, 2)
    held_c = to_neighbours(after(mlp_part(1, 6), hops_l))
    x_a, y_a = sides_of(own_a)
    x_m, y_m = sides_of(own_m)
    second = run_feed_forward(0, after(first[0], own_a), mlp_pieces[0], True, F32)
    second, ((x_a, y_a), held_c) = gate(second, (x_a, y_a), held_c)
    attn_pieces.append(one_matrix(own_a, x_a, y_a, True))
    hops_c = passed_on(held_c)
    third = run_attention(1, second[0], attn_pieces[1], 1_000_000)
    third, ((x_m, y_m), hops_c) = gate(third, (x_m, y_m), hops_c)
    mlp_pieces.append(two_with_corners(own_m, x_m, y_m, hops_c))
    saved = [(stream, *first[1:], first[0], *second[1:]), (second[0], *third[1:], third[0])]

    def put_pairs(held):
        out = jnp.zeros((total_rows, width), F32)
        for k, v in enumerate(held):
            out = lax.dynamic_update_slice(out, v.astype(F32), (((quarter - k) % n_t) * length, 0))
        return out

    place = lax.dynamic_slice_in_dim(positions, quarter, 1, 0)[0]
    cot = lax.dynamic_slice_in_dim(cotangent, quarter, 1, 0)[0]
    pick = (lax.broadcasted_iota(jnp.int32, (1, TOP_ROWS), 1) == place[:, None]).astype(BF16)
    pick = jnp.concatenate([pick, jnp.zeros((SLOT_ROWS - slots, TOP_ROWS), BF16)], 0)
    slot_cot = jnp.concatenate(
        [jnp.where(place[:, None] >= 0, cot, 0), jnp.zeros((SLOT_ROWS - slots, width), BF16)], 0
    )
    incoming = tn(pick, slot_cot)

    everything = tuple(range(n_t))
    halves = (everything[: n_t // 2], everything[n_t // 2 :])
    gain_grads = [[None, None] for _ in range(layers)]
    bias_grads = [[None, None] for _ in range(layers)]
    stream_l, normed, proj, logsum, mixed, middle = saved[top]
    grad_middle, gain_grads[top][1], bias_grads[top][1], slot_rows = top_backward(
        spots, incoming, middle, gains[top][1], biases[top][1], pick, slot_cot, top, own_mlp, mlp_pieces[top], n_t
    )
    all_rows = lax.all_gather(slot_rows, ("dp", "tensor"))
    total, incoming, gain_grads[top][0], bias_grads[top][0], _, *keep, send = attention_backward(
        spots, grad_middle, stream_l, gains[top][0], normed, proj, logsum, mixed, None,
        top, own_attn, attn_pieces[top], everything,
    )
    top_attn = Reduction([(keep, send)], n_dp, n_t)

    (last_stream,) = run_feed_forward(top, after(middle, total), mlp_pieces[top], False, BF16)
    last_stream, (top_attn.got,) = gate(last_stream, top_attn.got)
    hidden_held = [last_stream, hand_on(last_stream, 1)]
    ready = top_attn.near()

    stream_l, normed, proj, logsum, mixed, middle_l, normed_mlp, upward = saved[0]
    outs = mlp_backward(
        spots, after(incoming, ready), middle_l, gains[0][1], normed_mlp, upward, None,
        0, own_mlp, mlp_pieces[0], everything, True,
    )
    outs, (top_attn.from_near, hidden_held) = gate(outs, top_attn.from_near, hidden_held)
    grad_middle, gain_grads[0][1], bias_grads[0][1], *keep, send = outs[1:]
    low_mlp = Reduction([(keep, send)], n_dp, n_t)
    hidden_held.append(hand_on(hidden_held[-1], 1))
    ready = top_attn.far()

    outs = attention_backward(
        spots, after(grad_middle, ready), stream_l, gains[0][0], normed, proj, logsum, mixed, None,
        0, own_attn, attn_pieces[0], halves[0],
    )
    outs, (low_mlp.got, top_attn.from_far, hidden_held) = gate(
        outs, low_mlp.got, top_attn.from_far, hidden_held
    )
    hidden_held.append(hand_on(hidden_held[-1], 1))
    total, *keep, send = outs
    first_half = (keep, send)
    ready = low_mlp.near()
    top_attn.from_far = after(top_attn.from_far, ready)
    ready = top_attn.own(True)

    outs = attention_backward(
        spots, after(grad_middle, ready), stream_l, gains[0][0], normed, proj, logsum, mixed, total,
        0, own_attn, attn_pieces[0], halves[1], BF16,
    )
    outs, (low_mlp.from_near, top_attn.parts) = gate(outs, low_mlp.from_near, top_attn.parts)
    incoming, gain_grads[0][0], bias_grads[0][0], type_grad, *keep, send = outs[1:]
    low_attn = Reduction([after(first_half, send), (keep, send)], n_dp, n_t)
    grad_tokens = lax.all_gather(incoming, "tensor", tiled=True)
    ready = low_mlp.far()
    low_attn.got = after(low_attn.got, ready)
    ready = low_attn.near()

    rows_all = SumAll(
        stack_rows(
            [after(type_grad, ready)]
            + [g for pair in gain_grads for g in pair]
            + [g for pair in bias_grads for g in pair]
        ),
        n_dp,
        n_t,
    )

    def finished(reduction, token):
        return finish(after(reduction.parts, token), n_dp)

    sums = {}
    rows_all.step(ready)
    hidden_out = put_pairs(after(hidden_held, ready))
    rows_all.step(hidden_out)
    low_mlp.from_far = after(low_mlp.from_far, hidden_out)
    ready = low_mlp.own()
    rows_all.step(ready)
    low_attn.from_near = after(low_attn.from_near, rows_all.values)
    ready = low_attn.far()

    all_rows = after(all_rows, ready)
    all_cot = all_rows[:, :SLOT_ROWS].reshape(-1, width)
    all_normed = all_rows[:, SLOT_ROWS:].reshape(-1, width)
    slot_up = nn(all_normed, w_up[top])
    slot_grad = (nt(all_cot, w_down[top]) * gelu_slope(slot_up)).astype(BF16)
    grad_up_top = tn(lax.dynamic_slice_in_dim(all_normed, me * unit, unit, 1), slot_grad)
    grad_down_top = tn(
        gelu(slot_up).astype(BF16), lax.dynamic_slice_in_dim(all_cot, me * unit, unit, 1)
    )
    ready = (grad_up_top, grad_down_top)
    ready, (low_attn.from_far, low_mlp.passed) = gate(ready, low_attn.from_far, low_mlp.passed)
    ready = low_mlp.pass_on()
    low_attn.from_far = after(low_attn.from_far, ready)
    ready = low_attn.own()
    rows_all.step(ready)
    (sums["attn", top],) = finished(top_attn, ready)
    low_attn.passed = after(low_attn.passed, rows_all.got if rows_all.got is not None else ready)
    ready = low_attn.pass_on()
    rows_all.step(ready)
    rows_all = rows_all.result(ready)
    grad_tokens = after(grad_tokens, rows_all).astype(F32)
    sums["down", 0], sums["up", 0] = finished(low_mlp, grad_tokens)
    (sums["attn", 0],) = finished(low_attn, (sums["down", 0], sums["up", 0]))

    rows_mine = lax.dynamic_slice_in_dim(rows_all, me * unit, unit, 1)
    grad_gain = rows_mine[2 : 2 + 2 * layers].reshape(layers, 2, unit)
    grad_bias = rows_mine[2 + 2 * layers : 2 + 4 * layers].reshape(layers, 2, unit)
    grad_qkv = jnp.stack([sums["attn", l][:, : 3 * inner].reshape(unit, 3, inner) for l in range(layers)])
    grad_out = jnp.stack([sums["attn", l][:, 3 * inner :].T for l in range(layers)])
    grad_up = jnp.stack([grad_up_top if l == top else sums["up", l] for l in range(layers)])
    grad_down = jnp.stack([grad_down_top if l == top else sums["down", l].T for l in range(layers)])
    return hidden_out, grad_tokens, rows_mine[:2], grad_gain, grad_bias, grad_qkv, grad_out, grad_up, grad_down


def solution(mesh):
    n_dp, n_t = mesh.shape["dp"], mesh.shape["tensor"]
    placed = (
        P("dp", None),
        P(),
        P(),
        P(),
        P(None, None, None, "tensor"),
        P(None, "tensor", None),
        P(None, None, "tensor"),
        P(None, "tensor", None),
        P("dp", None, None),
        P("dp", None),
    )

    def run(*args):
        return shards(*args, n_dp, n_t)

    return jax.shard_map(
        run,
        mesh=mesh,
        in_specs=placed,
        out_specs=(
            P("dp", None),
            P("dp", None),
            P(None, "dp"),
            P(None, None, "dp"),
            P(None, None, "dp"),
            P(None, "dp", None, "tensor"),
            P(None, "tensor", "dp"),
            P(None, "dp", "tensor"),
            P(None, "tensor", "dp"),
        ),
        check_vma=False,
    )
```
